32 devices in a mesh: grp: 8 (over z, x), loc: 4 (over y, core).
Axes of the slice: x: 2, y: 2, z: 4, core: 2. Of those that a mesh axis runs over, the one named last changes fastest.
Arguments:
- tokens: bfloat16 [16384, 768], P(('grp', 'loc')), may hold values from -6 to 6
- cotangent: bfloat16 [16384, 768], P(('grp', 'loc')), may hold values from -6 to 6
- w_query: bfloat16 [768, 768], replicated, may hold values from -0.21875 to 0.21875
- w_key: bfloat16 [768, 768], replicated, may hold values from -0.21875 to 0.21875
- w_value: bfloat16 [768, 768], replicated, may hold values from -0.21875 to 0.21875
- w_output: bfloat16 [768, 768], replicated, may hold values from -1.75 to 1.75
- attn_gain: float32 [768], replicated, may hold values from 0.5 to 1.5
- bias_table: float32 [32, 12], replicated, may hold values from -4 to 4
- moe_gain: float32 [768], replicated, may hold values from 0.5 to 1.5
- router_weight: float32 [768, 32], replicated, may hold values from -0.25 to 0.25
- router_bias: float32 [32], replicated, may hold values from -0.75 to 0.75
- expert_in: bfloat16 [32, 768, 3072], P(('grp', 'loc')), may hold values from -0.21875 to 0.21875
- expert_out: bfloat16 [32, 3072, 768], P(('grp', 'loc')), may hold values from -6 to 6
- expert_ids: int32 [16384, 1], P(('grp', 'loc')), may hold values from 0 to 31; in each aligned block of 512 rows (0 to 511, 512 to 1023, ...) at most 32 rows name the same one
- bucket_ids: int32 [512, 512], replicated, may hold values from 0 to 31
Outputs:
- layer_out: bfloat16 [16384, 768], P(('grp', 'loc'))
- grad_tokens: bfloat16 [16384, 768], P(('grp', 'loc'))
- grad_query: float32 [768, 768], replicated
- grad_key: float32 [768, 768], replicated
- grad_value: float32 [768, 768], replicated
- grad_output: float32 [768, 768], replicated
- grad_attn_gain: float32 [768], replicated
- grad_table: float32 [32, 12], replicated
- grad_moe_gain: float32 [768], replicated
- grad_router: float32 [768, 32], replicated
- grad_router_bias: float32 [32], replicated
- grad_expert_in: float32 [32, 768, 3072], P(('grp', 'loc'))
- grad_expert_out: float32 [32, 3072, 768], P(('grp', 'loc'))
The draws below stay inside these ranges and needn't reach their ends.
Inputs may be any that keep to these rules, and one draw needn't show every extreme that they name: `expert_ids`: in the rows of one device no expert is named by more than 32 rows, a bound that some block reaches of them.
All inputs are finite; a program needn't handle non-finite values.
Results may differ from the reference program's by a relative error of at most 0.018.
Values may be sent and summed in bfloat16 or wider, within the bound.
No kernel may reach another device: no remote copies, remote signals or barrier semaphores. Data moves between devices by JAX's collectives and lax.ppermute only.
A program may use at most 192 MiB of HBM per device.

```python
import math
import jax
import jax.numpy as jnp
import numpy as np
from jax import lax

D = 768
HEADS = 12
HEAD = 64
FF = 3072
BUCKETS = 32
SEQ = 512
TOK_DEV = 512
TOKENS = 16384
EXPERTS = 32
MOST = 32
CAP = 640


def plant(drawn, rng, least, high):
    longest = drawn.shape.index(max(drawn.shape))
    spots = []
    for shift in (0, 1):
        where = [jax.random.randint(jax.random.fold_in(rng, axis), (), 0, length) for axis, length in enumerate(drawn.shape)]
        where[longest] = (where[longest] + shift) % drawn.shape[longest]
        spots.append(tuple(where))
    return drawn.at[spots[0]].set(least).at[spots[1]].set(high)


def level_of(own_key, dims, shards, smallest, largest):
    level = 1.0
    for position, shards_of in shards:
        steps = jax.random.uniform(jax.random.fold_in(jax.random.fold_in(own_key, 6), position), (shards_of,), jnp.float32, smallest / len(shards), largest / len(shards))
        level = level * jnp.repeat(jnp.exp(steps), dims[position] // shards_of).reshape((-1,) + (1,) * (len(dims) - 1 - position))
    return level


def deal_out(stream_key, own, number, rows, count, top, limit, lean):
    sequence = jax.random.permutation(stream_key, count)
    heavy_load, common = shares(count, rows * top, limit, lean, True), shares(count, rows * top, limit, lean, False)
    places = jnp.arange(count)

    def named(sizes, turn):
        used = int((sizes > 0).sum())
        fixed = max(1, used // 4)
        moved = fixed + (places - fixed + turn * (used - fixed)) % max(1, count - fixed)
        return jnp.zeros((count,), jnp.int32).at[sequence[jnp.where(places < fixed, places, moved)]].set(jnp.asarray(sizes, jnp.int32))

    sizes = jnp.where(number % 4 == 0, named(heavy_load, number // 4), named(common, number - number // 4 - 1))
    mixed = jax.random.permutation(jax.random.fold_in(own, 3), count)
    donor, sink = mixed[0:count // 2 * 2:2], mixed[1:count // 2 * 2:2]
    room = jnp.minimum(sizes[donor] - 1, limit - sizes[sink]) // 2
    room = jnp.where((donor == sequence[0]) | (sink == sequence[0]) | (sizes[sink] == 0), 0, jnp.maximum(room, 0))
    moved = jax.random.randint(jax.random.fold_in(own, 4), (count // 2,), 0, 1 << 20) % (room + 1)
    sizes = sizes.at[donor].add(-moved).at[sink].add(moved)
    labels = jnp.searchsorted(jnp.cumsum(sizes), jnp.arange(rows * top), side="right").astype(jnp.int32)
    grid = labels.reshape(top, rows).T
    grid = grid[jax.random.permutation(jax.random.fold_in(own, 1), rows)]
    turn = jax.random.randint(jax.random.fold_in(own, 2), (rows, 1), 0, top)
    return jnp.take_along_axis(grid, (jnp.arange(top)[None, :] + turn) % top, axis=1)


def shares(amount, total, most, slope, full):
    weights = [(1 << 20) // math.isqrt(rank ** slope) + 1 for rank in range(1, amount + 1)]
    largest = most if full else min(most, max(-(-total // amount), total * weights[0] // sum(weights)))
    least = 1 if total - largest >= amount - 1 else 0
    given, spare = [largest] + [least] * (amount - 1), total - largest - least * (amount - 1)
    while spare > 0:
        candidates = [i for i in range(1, amount) if given[i] < largest] or [i for i in range(1, amount) if given[i] < most]
        pool, left = sum([weights[i] for i in candidates]), spare
        for i in candidates:
            more = min(most - given[i], max(1, left * weights[i] // pool), spare)
            given[i] = given[i] + more
            spare = spare - more
    return np.array(given)


def gaussian(key, dims, width, most, cuts=(), kind=jnp.bfloat16):
    result = jax.random.normal(key, dims, jnp.float32) * width
    if len(cuts) > 0:
        result = level_of(key, dims, cuts, -0.22, 0.18) * result
    return jnp.clip(result, min=-most, max=most).astype(kind)


def setup_inputs(seed: int = 0) -> dict:
    key_list = jax.random.split(jax.random.key(seed), 16)
    tokens = gaussian(key_list[0], (TOKENS, D), 1.0, 6.0, ((0, 32),))
    cotangent = gaussian(key_list[1], (TOKENS, D), 1.0, 6.0, ((0, 32),))
    w_query = gaussian(key_list[2], (D, D), D ** -0.5, 0.21875)
    w_key = gaussian(key_list[3], (D, D), D ** -0.5, 0.21875)
    w_value = gaussian(key_list[4], (D, D), D ** -0.5, 0.21875)
    w_output = gaussian(key_list[5], (D, D), (D // 64) ** -0.5, 1.75)
    attn_gain = jnp.clip(1.0 + 0.1 * jax.random.normal(key_list[6], (D,), jnp.float32), 0.5, 1.5)
    bias_table = gaussian(key_list[7], (BUCKETS, HEADS), 1.0, 4.0, (), jnp.float32)
    moe_gain = jnp.clip(1.0 + 0.1 * jax.random.normal(key_list[8], (D,), jnp.float32), 0.5, 1.5)
    router_weight = gaussian(key_list[9], (D, EXPERTS), (0.5 / D ** 0.5), 0.25, (), jnp.float32)
    router_bias = gaussian(key_list[10], (EXPERTS,), 0.05, 0.75, (), jnp.float32)
    expert_in = gaussian(key_list[11], (EXPERTS, D, FF), D ** -0.5, 0.21875, ((0, 32),))
    expert_out = gaussian(key_list[12], (EXPERTS, FF, D), (1.7 * EXPERTS / FF ** 0.5), 6.0, ((0, 32),))
    expert_ids_keys = jax.random.split(jax.random.fold_in(key_list[13], 1), TOKENS // TOK_DEV)
    expert_ids_turns = jax.random.permutation(jax.random.fold_in(key_list[13], 3), TOKENS // TOK_DEV)
    expert_ids = jax.vmap(lambda own, number: deal_out(jax.random.fold_in(key_list[13], 2), own, number, TOK_DEV, EXPERTS, 1, MOST, 2))(expert_ids_keys, expert_ids_turns).reshape((TOKENS, 1))
    bucket_ids = plant(jax.random.randint(key_list[14], (SEQ, SEQ), 0, BUCKETS), jax.random.fold_in(key_list[14], 1), 0, BUCKETS - 1).astype(jnp.int32)
    return dict(tokens=tokens, cotangent=cotangent, w_query=w_query, w_key=w_key, w_value=w_value, w_output=w_output, attn_gain=attn_gain, bias_table=bias_table, moe_gain=moe_gain, router_weight=router_weight, router_bias=router_bias, expert_in=expert_in, expert_out=expert_out, expert_ids=expert_ids, bucket_ids=bucket_ids)


@jax.custom_vjp
def low(v):
    return lax.optimization_barrier(v.astype(jnp.bfloat16)).astype(jnp.float32)

@jax.custom_vjp
def low_back(v):
    return v

def low_keep(v):
    return (low(v), None)

def low_pass(kept, grad):
    return (grad,)

def back_keep(v):
    return (v, None)

def back_low(kept, grad):
    return (low(grad),)
low.defvjp(low_keep, low_pass)
low_back.defvjp(back_keep, back_low)

def norm_apply(values, gain_vec):
    return values * lax.rsqrt(lax.optimization_barrier(jnp.mean(values * values, axis=-1, keepdims=True)) + 1e-06) * gain_vec

def matmul_high(left_mat, right_mat):
    return jnp.dot(left_mat, right_mat, precision=lax.Precision.HIGHEST, preferred_element_type=jnp.float32)

def smooth_act(values):
    return jax.nn.gelu(values, approximate=True)

def layer(inputs, w_query, w_key, w_value, w_output, attn_gain, bias_table, moe_gain, router_weight, router_bias, expert_in, expert_out, expert_ids, bucket_ids):
    highest = lax.Precision.HIGHEST
    n_rows = inputs.shape[0]
    n_seqs = n_rows // SEQ
    group_seqs = math.gcd(n_seqs, max(1, 4096 // SEQ))
    normed_one = low(norm_apply(inputs, attn_gain))
    query = low_back(low(matmul_high(normed_one, w_query)))
    keys_all = low_back(low(matmul_high(normed_one, w_key)))
    values_all = low_back(low(matmul_high(normed_one, w_value)))
    bucket_hot = (bucket_ids[:, :, None] == jnp.arange(BUCKETS, dtype=jnp.int32)).astype(jnp.float32)
    rel_bias = jnp.einsum('qkb,bh->hqk', bucket_hot, bias_table, precision=highest)
    scaling = HEAD ** (-0.5)
    head_shape = (group_seqs, SEQ, HEADS, HEAD)

    def attend_block(pieces):
        q_block, k_block, v_block = pieces
        scores = jnp.einsum('sqhd,skhd->shqk', q_block.reshape(head_shape), k_block.reshape(head_shape), precision=highest) * scaling + rel_bias
        scores = low_back(scores)
        weights = jax.nn.softmax(scores, axis=-1)
        mixed = jnp.einsum('shqk,skhd->sqhd', low(weights), v_block.reshape(head_shape), precision=highest)
        return mixed.reshape(group_seqs, SEQ, D)
    block_shape = (n_seqs // group_seqs, group_seqs, SEQ, D)
    attended = lax.map(jax.checkpoint(attend_block), (query.reshape(block_shape), keys_all.reshape(block_shape), values_all.reshape(block_shape)))
    attended = low_back(low(attended.reshape(n_rows, D)))
    middle = inputs + low_back(matmul_high(attended, w_output))
    normed_two = low(norm_apply(middle, moe_gain))
    logits = matmul_high(normed_two, router_weight) + router_bias
    router_probs = jax.nn.softmax(logits, axis=-1)
    chosen = expert_ids[:, 0].astype(jnp.int32)
    one_hot = (chosen[:, None] == jnp.arange(EXPERTS, dtype=jnp.int32)).astype(jnp.int32)
    global_slot = lax.optimization_barrier(jnp.sum((jnp.cumsum(one_hot, axis=0) - 1) * one_hot, axis=1)).astype(jnp.int32)
    kept_mask = global_slot < CAP
    place_slot = jnp.where(kept_mask, global_slot, CAP).astype(jnp.int32)
    gate_value = lax.optimization_barrier(jnp.sum(router_probs * one_hot.astype(jnp.float32), axis=1))
    buffers = jnp.zeros((EXPERTS, CAP + 1, D), jnp.float32).at[chosen, place_slot].add(normed_two)
    buffers = low_back(buffers)
    hidden_pre = low_back(jnp.einsum('ecd,edf->ecf', buffers, expert_in, precision=highest))
    hidden_low = low(smooth_act(hidden_pre))
    results = low_back(low(jnp.einsum('ecf,efd->ecd', hidden_low, expert_out, precision=highest)))
    picked = results[chosen, place_slot]
    moe_term = jnp.where(kept_mask[:, None], gate_value[:, None] * picked, 0.0)
    return middle + moe_term

def reference(tokens, cotangent, w_query, w_key, w_value, w_output, attn_gain, bias_table, moe_gain, router_weight, router_bias, expert_in, expert_out, expert_ids, bucket_ids):
    floats = tuple((member.astype(jnp.float32) for member in (tokens, w_query, w_key, w_value, w_output, attn_gain, bias_table, moe_gain, router_weight, router_bias, expert_in, expert_out)))

    def forward(*members):
        return layer(*members, expert_ids, bucket_ids)
    layer_out, pull_back = jax.vjp(forward, *floats)
    gradients = pull_back(cotangent.astype(jnp.float32))
    return (layer_out.astype(jnp.bfloat16), gradients[0].astype(jnp.bfloat16), gradients[1], gradients[2], gradients[3], gradients[4], gradients[5], gradients[6], gradients[7], gradients[8], gradients[9], gradients[10], gradients[11])
```

```python
import functools

import jax
import jax.numpy as jnp
from jax import lax
from jax.experimental import pallas as pl
from jax.experimental.pallas import tpu as pltpu
from jax.sharding import PartitionSpec as P

AXES = ("grp", "loc")
LOW = jnp.bfloat16
F32 = jnp.float32
NN = (((1,), (0,)), ((), ()))
NT = (((1,), (1,)), ((), ()))
TN = (((0,), (0,)), ((), ()))
VMEM_BYTES = 56 * 1024 * 1024
EMPTY = 2.0**20
FAR = 1 << 20


def dot(left, right, dims=NN):
    return lax.dot_general(left, right, dims, preferred_element_type=F32)


def split(values):
    high = values.astype(LOW)
    rest = values - high.astype(F32)
    middle = rest.astype(LOW)
    return high, middle, (rest - middle.astype(F32)).astype(LOW)


def params():
    return pltpu.CompilerParams(vmem_limit_bytes=VMEM_BYTES)


def cost(flops, nbytes, trans=0):
    return pl.CostEstimate(flops=int(flops), bytes_accessed=int(nbytes), transcendentals=int(trans))


def shape(dims, dtype):
    return jax.ShapeDtypeStruct(dims, dtype)


def norm_scale(values):
    return lax.rsqrt(jnp.mean(values * values, axis=-1, keepdims=True) + 1e-06)


def dispatch_kernel(ids_ref, dy_ref, out_ref, row_ref, col_ref, *, most):
    n = ids_ref.shape[0]
    slots = out_ref.shape[0]
    ids_col = jnp.broadcast_to(ids_ref[...], (n, n))
    sub = lax.broadcasted_iota(jnp.int32, (n, n), 0)
    lane = lax.broadcasted_iota(jnp.int32, (n, n), 1)
    ids_row = jnp.sum(jnp.where(sub == lane, ids_col, 0), axis=0, keepdims=True)
    same = ids_col == ids_row
    rank_row = jnp.sum(jnp.where(same & (sub < lane), 1, 0), axis=0, keepdims=True)
    rank_col = jnp.sum(jnp.where(same & (lane < sub), 1, 0), axis=1, keepdims=True)
    slot_row = ids_row * most + rank_row
    row_ref[...] = jnp.broadcast_to(slot_row, row_ref.shape)
    col_ref[...] = jnp.broadcast_to(ids_ref[...] * most + rank_col, col_ref.shape)
    place = lax.broadcasted_iota(jnp.int32, (slots, n), 0) == slot_row
    hot = place.astype(F32)
    filled = jnp.sum(hot, axis=1, keepdims=True)
    rows = dot(hot.astype(LOW), dy_ref[...])
    out_ref[...] = jnp.where(filled > 0.0, rows, EMPTY).astype(LOW)


def dispatch(ids, dy, slots, most):
    n, width = dy.shape
    return pl.pallas_call(
        functools.partial(dispatch_kernel, most=most),
        out_shape=(
            shape((slots, width), LOW),
            shape((8, n), jnp.int32),
            shape((n, 128), jnp.int32),
        ),
        compiler_params=params(),
        cost_estimate=cost(2 * slots * n * width, 4 * slots * width),
        name="dispatch",
    )(ids, dy)


def attend_kernel(
    tok_ref,
    gain_ref,
    tab_ref,
    bucket_ref,
    wq_ref,
    wk_ref,
    wv_ref,
    wo_ref,
    moe_gain_ref,
    row_ref,
    q_ref,
    k_ref,
    v_ref,
    w_ref,
    att_ref,
    normed_ref,
    mid_ref,
    out_ref,
    att_s,
    *,
    scaling,
):
    step = pl.program_id(0)
    pairs = pl.num_programs(0)
    n = tok_ref.shape[0]

    @pl.when(step == 0)
    def _():
        inputs = tok_ref[...].astype(F32)
        normed_ref[...] = (inputs * norm_scale(inputs) * gain_ref[...]).astype(LOW)

    normed = normed_ref[...]
    query = dot(normed, wq_ref[...]).astype(LOW)
    keys = dot(normed, wk_ref[...]).astype(LOW)
    values = dot(normed, wv_ref[...]).astype(LOW)
    q_ref[...] = query
    k_ref[...] = keys
    v_ref[...] = values
    low_half = lax.broadcasted_iota(jnp.int32, query.shape, 1) < query.shape[1] // 2
    zero = jnp.zeros_like(query)
    total = jnp.zeros((n, query.shape[1]), F32)
    for h in range(2):
        mine = low_half if h == 0 else ~low_half
        scores = dot(jnp.where(mine, query, zero), keys, NT) * scaling
        table = jnp.broadcast_to(tab_ref[step, pl.ds(h, 1), :], (n, 128))
        bias = [
            jnp.take_along_axis(
                table, bucket_ref[:, c * 128 : (c + 1) * 128], axis=1, mode="promise_in_bounds"
            )
            for c in range(n // 128)
        ]
        scores = scores + jnp.concatenate(bias, axis=1)
        top = jnp.max(scores, axis=1, keepdims=True)
        grown = jnp.exp(scores - top)
        weights = (grown * (1.0 / jnp.sum(grown, axis=1, keepdims=True))).astype(LOW)
        w_ref[h] = weights
        total = total + dot(weights, jnp.where(mine, values, zero))
    att_s[step] = total.astype(LOW)

    @pl.when(step == pairs - 1)
    def _():
        attended = jnp.concatenate([att_s[i] for i in range(att_s.shape[0])], axis=1)
        att_ref[...] = attended
        middle = tok_ref[...].astype(F32) + dot(attended, wo_ref[...])
        mid_ref[...] = middle
        normed_two = (middle * norm_scale(middle) * moe_gain_ref[...]).astype(LOW)
        slots = out_ref.shape[0]
        place = lax.broadcasted_iota(jnp.int32, (slots, n), 0) == row_ref[0:1, :]
        out_ref[...] = dot(place.astype(F32).astype(LOW), normed_two).astype(LOW)


def attend(tokens, gain, table, buckets, wq, wk, wv, wo, moe_gain, row, slots, n_heads):
    n, width = tokens.shape
    pairs = n_heads // 2
    span = width // pairs
    whole = lambda *dims: pl.BlockSpec(dims, lambda p: (0,) * len(dims))
    cols = lambda rows: pl.BlockSpec((rows, span), lambda p: (0, p))
    return pl.pallas_call(
        functools.partial(attend_kernel, scaling=(width // n_heads) ** -0.5),
        grid=(pairs,),
        in_specs=[
            whole(n, width),
            whole(1, width),
            whole(*table.shape),
            whole(n, n),
            cols(width),
            cols(width),
            cols(width),
            whole(width, width),
            whole(1, width),
            whole(8, n),
        ],
        out_specs=[
            cols(n),
            cols(n),
            cols(n),
            pl.BlockSpec((2, n, n), lambda p: (p, 0, 0)),
            whole(n, width),
            whole(n, width),
            whole(n, width),
            whole(slots, width),
        ],
        out_shape=[
            shape((n, width), LOW),
            shape((n, width), LOW),
            shape((n, width), LOW),
            shape((n_heads, n, n), LOW),
            shape((n, width), LOW),
            shape((n, width), LOW),
            shape((n, width), F32),
            shape((slots, width), LOW),
        ],
        scratch_shapes=[pltpu.VMEM((pairs, n, span), LOW)],
        compiler_params=params(),
        cost_estimate=cost(
            8 * n * width * width + 4 * n_heads * n * n * span + 2 * slots * n * width,
            2 * n_heads * n * n + 24 * n * width,
            n_heads * n * n,
        ),
        name="attend",
    )(
        tokens,
        gain.reshape(1, width),
        table,
        buckets,
        wq,
        wk,
        wv,
        wo,
        moe_gain.reshape(1, width),
        row,
    )


def arrive_kernel(dy_ref, dyc_ref, row_ref, col_ref):
    slots = dy_ref.shape[0]
    keep = dyc_ref.shape[0]
    edge = dy_ref[:, 0:128]
    valid = jnp.where(edge.astype(F32) < EMPTY * 0.5, 1.0, 0.0).astype(LOW)
    sub = lax.broadcasted_iota(jnp.int32, (slots, slots), 0)
    lane = lax.broadcasted_iota(jnp.int32, (slots, slots), 1)
    before = jnp.where(lane < sub, 1.0, 0.0).astype(LOW)
    slot_col = dot(before, valid)
    slot_col = jnp.where(valid > 0.5, slot_col, float(FAR)).astype(jnp.int32)
    first = jnp.where(lax.broadcasted_iota(jnp.int32, (8, 128), 1) == 0, 1.0, 0.0).astype(LOW)
    valid_row = dot(first, valid, NT)
    slot_row = dot(valid_row.astype(LOW), before, NT)
    slot_row = jnp.where(valid_row > 0.5, slot_row, float(FAR)).astype(jnp.int32)
    row_ref[...] = slot_row
    col_ref[...] = slot_col
    place = lax.broadcasted_iota(jnp.int32, (keep, slots), 0) == slot_row[0:1, :]
    dyc_ref[...] = dot(place.astype(F32).astype(LOW), dy_ref[...]).astype(LOW)


def arrive(dy_rows, keep):
    slots, width = dy_rows.shape
    return pl.pallas_call(
        arrive_kernel,
        out_shape=(
            shape((keep, width), LOW),
            shape((8, slots), jnp.int32),
            shape((slots, 128), jnp.int32),
        ),
        compiler_params=params(),
        cost_estimate=cost(2 * keep * slots * width, 4 * slots * width),
        name="arrive",
    )(dy_rows)


def expert_kernel(
    me_ref,
    x_ref,
    dyc_ref,
    row_ref,
    col_ref,
    router_ref,
    rbias_ref,
    win_ref,
    wout_ref,
    dn_ref,
    res_ref,
    hid_ref,
    dpre_ref,
    xc_ref,
    dres_ref,
    dlog_ref,
    sum_s,
    drow_s,
    prob_s,
):
    step = pl.program_id(0)
    keep = xc_ref.shape[0]
    slots = x_ref.shape[0]
    n_exp = router_ref.shape[1]

    @pl.when(step == 0)
    def _():
        place = lax.broadcasted_iota(jnp.int32, (keep, slots), 0) == row_ref[0:1, :]
        rows = dot(place.astype(F32).astype(LOW), x_ref[...]).astype(LOW)
        xc_ref[...] = rows
        high, middle, low = split(router_ref[...])
        logits = dot(rows, high) + (dot(rows, middle) + dot(rows, low)) + rbias_ref[...]
        grown = jnp.exp(logits - jnp.max(logits, axis=1, keepdims=True))
        probs = grown / jnp.sum(grown, axis=1, keepdims=True)
        prob_s[...] = probs
        mine = lax.broadcasted_iota(jnp.int32, probs.shape, 1) == me_ref[0]
        gate = jnp.sum(jnp.where(mine, probs, 0.0), axis=1, keepdims=True)
        dres_ref[...] = (gate * dyc_ref[...].astype(F32)).astype(LOW)
        sum_s[...] = jnp.zeros_like(sum_s)
        drow_s[...] = jnp.zeros_like(drow_s)

    rows = xc_ref[...]
    win = win_ref[...]
    wout = wout_ref[...]
    pre = dot(rows, win)
    rate = 0.7978845608028654
    square = pre * pre
    tanh = jnp.tanh(rate * pre * (1.0 + 0.044715 * square))
    half = 0.5 * (1.0 + tanh)
    hidden = (pre * half).astype(LOW)
    slope = half + (0.5 * rate) * pre * (1.0 - tanh * tanh) * (1.0 + 3 * 0.044715 * square)
    dhid = dot(dres_ref[...], wout, NT)
    dpre = (dhid * slope).astype(LOW)
    hid_ref[...] = hidden
    dpre_ref[...] = dpre
    sum_s[...] += dot(hidden, wout)
    drow_s[...] += dot(dpre, win, NT)

    @pl.when(step == pl.num_programs(0) - 1)
    def _():
        result = sum_s[...].astype(LOW).astype(F32)
        dgate = jnp.sum(dyc_ref[...].astype(F32) * result, axis=1, keepdims=True)
        probs = prob_s[...]
        mine = lax.broadcasted_iota(jnp.int32, probs.shape, 1) == me_ref[0]
        gate = jnp.sum(jnp.where(mine, probs, 0.0), axis=1, keepdims=True)
        dlogits = probs * (jnp.where(mine, dgate, 0.0) - gate * dgate)
        dlog_ref[...] = dlogits
        high, middle, _ = split(router_ref[...])
        dhigh, dmiddle, _ = split(dlogits)
        side = dot(dhigh, high, NT) + (dot(dhigh, middle, NT) + dot(dmiddle, high, NT))
        grad = (drow_s[...] + side).astype(LOW)
        place = lax.broadcasted_iota(jnp.int32, (slots, keep), 1) == col_ref[:, 0:1]
        place = place.astype(F32).astype(LOW)
        dn_ref[...] = dot(place, grad).astype(LOW)
        res_ref[...] = dot(place, (gate * result).astype(LOW)).astype(LOW)


def expert(me, arrived, dyc, row, col, router, rbias, expert_in, expert_out):
    slots, width = arrived.shape
    keep = dyc.shape[0]
    n_exp = router.shape[1]
    ff = expert_in.shape[2]
    block = 768 if ff % 768 == 0 else ff
    whole = lambda *dims: pl.BlockSpec(dims, lambda f: (0,) * len(dims))
    return pl.pallas_call(
        expert_kernel,
        grid=(ff // block,),
        in_specs=[
            pl.BlockSpec(memory_space=pltpu.SMEM),
            whole(slots, width),
            whole(keep, width),
            whole(8, slots),
            whole(slots, 128),
            whole(width, n_exp),
            whole(1, n_exp),
            pl.BlockSpec((None, width, block), lambda f: (0, 0, f)),
            pl.BlockSpec((None, block, width), lambda f: (0, f, 0)),
        ],
        out_specs=[
            whole(slots, width),
            whole(slots, width),
            pl.BlockSpec((keep, block), lambda f: (0, f)),
            pl.BlockSpec((keep, block), lambda f: (0, f)),
            whole(keep, width),
            whole(keep, width),
            whole(keep, n_exp),
        ],
        out_shape=[
            shape((slots, width), LOW),
            shape((slots, width), LOW),
            shape((keep, ff), LOW),
            shape((keep, ff), LOW),
            shape((keep, width), LOW),
            shape((keep, width), LOW),
            shape((keep, n_exp), F32),
        ],
        scratch_shapes=[
            pltpu.VMEM((keep, width), F32),
            pltpu.VMEM((keep, width), F32),
            pltpu.VMEM((keep, n_exp), F32),
        ],
        compiler_params=params(),
        cost_estimate=cost(
            8 * keep * width * ff + 6 * keep * slots * width, 16 * width * ff, keep * ff
        ),
        name="expert",
    )(me, arrived, dyc, row, col, router, rbias.reshape(1, n_exp), expert_in, expert_out)


def middle_kernel(dn_ref, col_ref, mid_ref, dy_ref, gain_ref, wo_ref, dmid_ref, dbr_ref, datt_ref, gain_out):
    n = mid_ref.shape[0]
    slots = dn_ref.shape[0]
    place = lax.broadcasted_iota(jnp.int32, (n, slots), 1) == col_ref[:, 0:1]
    dnormed = dot(place.astype(F32).astype(LOW), dn_ref[...])
    middle = mid_ref[...]
    inv = norm_scale(middle)
    scaled = dnormed * gain_ref[...]
    inner = jnp.mean(scaled * middle, axis=1, keepdims=True)
    dmid = dy_ref[...].astype(F32) + inv * scaled - middle * (inv * inv * inv) * inner
    dmid_ref[...] = dmid
    branch = dmid.astype(LOW)
    dbr_ref[...] = branch
    datt_ref[...] = dot(branch, wo_ref[...], NT).astype(LOW)
    gain_out[...] = jnp.broadcast_to(
        jnp.sum(dnormed * middle * inv, axis=0, keepdims=True), gain_out.shape
    )


def middle_back(dn_rows, col, middle, dy, moe_gain, wo):
    n, width = middle.shape
    return pl.pallas_call(
        middle_kernel,
        out_shape=(
            shape((n, width), F32),
            shape((n, width), LOW),
            shape((n, width), LOW),
            shape((8, width), F32),
        ),
        compiler_params=params(),
        cost_estimate=cost(2 * n * width * (width + dn_rows.shape[0]), 14 * n * width),
        name="middle_back",
    )(dn_rows, col, middle, dy, moe_gain.reshape(1, width), wo)


def attend_back_kernel(q_ref, k_ref, v_ref, da_ref, w_ref, grads_ref, ds_ref, *, scaling):
    n, span = q_ref.shape
    half = span // 2
    query, keys, values, grad = q_ref[...], k_ref[...], v_ref[...], da_ref[...]
    query_t = query.astype(F32).T.astype(LOW)
    grad_t = grad.astype(F32).T.astype(LOW)
    low_half = lax.broadcasted_iota(jnp.int32, query.shape, 1) < half
    zero = jnp.zeros_like(query)
    dquery = jnp.zeros((n, span), F32)
    dkeys, dvalues = [], []
    for h in range(2):
        mine = low_half if h == 0 else ~low_half
        weights_low = w_ref[h]
        weights = weights_low.astype(F32)
        dweights = dot(jnp.where(mine, grad, zero), values, NT)
        both = weights * dweights
        dscores = (both - weights * jnp.sum(both, axis=1, keepdims=True)).astype(LOW)
        ds_ref[h] = dscores
        dquery = dquery + dot(dscores, jnp.where(mine, keys, zero))
        dkeys.append(dot(query_t[h * half : (h + 1) * half, :], dscores))
        dvalues.append(dot(grad_t[h * half : (h + 1) * half, :], weights_low))
    grads_ref[:, 0:span] = (dquery * scaling).astype(LOW)
    grads_ref[:, span : 2 * span] = (jnp.concatenate(dkeys, axis=0).T * scaling).astype(LOW)
    grads_ref[:, 2 * span :] = jnp.concatenate(dvalues, axis=0).T.astype(LOW)


def attend_back(query, keys, values, grad, weights):
    n_heads, n, _ = weights.shape
    width = query.shape[1]
    pairs = n_heads // 2
    span = width // pairs
    cols = pl.BlockSpec((n, span), lambda p: (0, p))
    square = pl.BlockSpec((2, n, n), lambda p: (p, 0, 0))
    return pl.pallas_call(
        functools.partial(attend_back_kernel, scaling=(width // n_heads) ** -0.5),
        grid=(pairs,),
        in_specs=[cols, cols, cols, cols, square],
        out_specs=[pl.BlockSpec((n, 3 * span), lambda p: (0, p)), square],
        out_shape=[shape((n, 3 * width), LOW), shape((n_heads, n, n), LOW)],
        compiler_params=params(),
        cost_estimate=cost(10 * n_heads * n * n * span // 2, 4 * n_heads * n * n + 14 * n * width),
        name="attend_back",
    )(query, keys, values, grad, weights)


def table_kernel(ds_ref, bucket_ref, out_ref, sum_s, *, n_buckets):
    step = pl.program_id(0)
    n_heads, rows, n = ds_ref.shape
    band = 16

    @pl.when(step == 0)
    def _():
        sum_s[...] = jnp.zeros_like(sum_s)

    total = sum_s[...]
    for r in range(rows // band):
        span = slice(r * band, (r + 1) * band)
        grads = ds_ref[:, span, :].reshape(n_heads * band, n)
        buckets = bucket_ref[span, :]
        hot = jnp.concatenate(
            [jnp.where(buckets == b, 1.0, 0.0).astype(LOW) for b in range(n_buckets)], axis=0
        )
        total = total + dot(grads, hot, NT)
    sum_s[...] = total

    @pl.when(step == pl.num_programs(0) - 1)
    def _():
        left = lax.broadcasted_iota(jnp.int32, total.shape, 0) % band
        right = lax.broadcasted_iota(jnp.int32, total.shape, 1) % band
        own = jnp.where(left == right, total, 0.0)
        own = jnp.sum(own.reshape(n_heads, band, n_buckets * band), axis=1)
        bucket = lax.broadcasted_iota(jnp.int32, (n_buckets * band, n_buckets), 1)
        column = lax.broadcasted_iota(jnp.int32, (n_buckets * band, n_buckets), 0)
        fold = jnp.where(column // band == bucket, 1.0, 0.0).astype(LOW)
        high, middle, low = split(own)
        out_ref[...] = dot(high, fold) + dot(middle, fold) + dot(low, fold)


def table_back(dscores, buckets, n_buckets):
    n_heads, n, _ = dscores.shape
    rows, band = 64, 16
    dims = (n_heads * band, n_buckets * band)
    return pl.pallas_call(
        functools.partial(table_kernel, n_buckets=n_buckets),
        grid=(n // rows,),
        in_specs=[
            pl.BlockSpec((n_heads, rows, n), lambda r: (0, r, 0)),
            pl.BlockSpec((rows, n), lambda r: (r, 0)),
        ],
        out_specs=pl.BlockSpec((n_heads, n_buckets), lambda r: (0, 0)),
        out_shape=shape((n_heads, n_buckets), F32),
        scratch_shapes=[pltpu.VMEM(dims, F32)],
        compiler_params=params(),
        cost_estimate=cost(2 * dims[0] * dims[1] * n * n // band, 2 * n_heads * n * n),
        name="table_back",
    )(dscores, buckets)


class Ring:
    def __init__(self, n_grp, n_loc):
        size = n_grp * n_loc
        bits = size.bit_length() - 1
        low = n_loc.bit_length() - 1
        self.size = size
        ys, xs = list(range(1, low)), list(range(low, bits - 2))
        first, second = (ys + xs, xs + ys) if len(ys) == len(xs) else (ys + xs, ys + xs)
        self.plane = list(zip(first, second))
        self.near, self.far = (bits - 2, bits - 2), (bits - 1, bits - 1)
        self.core = (0, 0)

    def swap(self, value, shifts):
        pairs = [(i, i ^ (1 << shifts[i & 1])) for i in range(self.size)]
        return lax.ppermute(value, AXES, pairs)

    def side(self, me, shifts):
        shift = jnp.where(me & 1 == 0, shifts[0], shifts[1])
        return (me >> shift) & 1

    def halve(self, value, me, shifts):
        rows = value.shape[0] // 2
        side = self.side(me, shifts)
        sent = lax.dynamic_slice_in_dim(value, (1 - side) * rows, rows, 0)
        kept = lax.dynamic_slice_in_dim(value, side * rows, rows, 0)
        got = self.swap(sent, shifts)
        return (kept.astype(F32) + got.astype(F32)).astype(LOW)

    def double(self, value, me, shifts):
        got = self.swap(value, shifts)
        side = self.side(me, shifts)
        low = jnp.where(side == 0, value, got)
        high = jnp.where(side == 0, got, value)
        return jnp.concatenate([low, high], axis=0)

    def total(self, kept, sent, me):
        value = (kept + self.swap(sent, self.core).astype(F32)).astype(LOW)
        order = self.plane + [self.near]
        for shifts in order:
            value = self.halve(value, me, shifts)
        got = self.swap(value, self.far)
        value = (value.astype(F32) + got.astype(F32)).astype(LOW)
        for shifts in reversed(order[1:]):
            value = self.double(value, me, shifts)
        near = self.swap(value, order[0])
        return value, near, self.swap(value, self.core), self.swap(near, self.core)

    def where(self, me):
        sides = [self.side(me, self.plane[0]), self.side(me ^ 1, self.plane[0])]
        return jnp.stack([me & 1] + sides)


def unpack_kernel(where_ref, own_ref, near_ref, core_ref, far_ref, *out_refs):
    rows = pl.program_id(0)
    mine = jnp.where(where_ref[1] == rows, own_ref[...], near_ref[...])
    other = jnp.where(where_ref[2] == rows, core_ref[...], far_ref[...])
    low = jnp.where(where_ref[0] == 0, mine, other).astype(F32)
    high = jnp.where(where_ref[0] == 0, other, mine).astype(F32)
    if len(out_refs) == 1:
        out_refs[0][...] = jnp.concatenate([low, high], axis=1)
        return
    span = 128
    half = low.shape[1] // 3
    for i, out_ref in enumerate(out_refs):
        for p in range(half // span):
            at = (3 * p + i) * span
            out_ref[:, p * span : (p + 1) * span] = low[:, at : at + span]
            out_ref[:, half + p * span : half + (p + 1) * span] = high[:, at : at + span]


def unpack(where, pieces, n_outs):
    rows, cols = pieces[0].shape
    block = 64 if rows % 64 == 0 else rows
    steps = rows // block
    width = 2 * cols // n_outs
    piece = pl.BlockSpec((block, cols), lambda h, r: (r, 0))
    return pl.pallas_call(
        unpack_kernel,
        grid=(2, steps),
        in_specs=[pl.BlockSpec(memory_space=pltpu.SMEM)] + [piece] * 4,
        out_specs=[pl.BlockSpec((block, width), lambda h, r: (h * steps + r, 0))] * n_outs,
        out_shape=[shape((2 * rows, width), F32)] * n_outs,
        compiler_params=params(),
        cost_estimate=cost(rows * cols, 32 * rows * cols),
        name="unpack",
    )(where, *pieces)


def tokens_kernel(grads_ref, wq_ref, wk_ref, wv_ref, tok_ref, gain_ref, dmid_ref, out_ref, gain_out, sum_s):
    step = pl.program_id(0)
    span = wq_ref.shape[1]
    grads = grads_ref[...]
    joined = jnp.concatenate([wq_ref[...], wk_ref[...], wv_ref[...]], axis=1)
    part = dot(grads, joined, NT)

    @pl.when(step == 0)
    def _():
        sum_s[...] = part

    @pl.when(step > 0)
    def _():
        sum_s[...] += part

    @pl.when(step == pl.num_programs(0) - 1)
    def _():
        dnormed = sum_s[...]
        inputs = tok_ref[...].astype(F32)
        inv = norm_scale(inputs)
        scaled = dnormed * gain_ref[...]
        inner = jnp.mean(scaled * inputs, axis=1, keepdims=True)
        out_ref[...] = (
            dmid_ref[...] + inv * scaled - inputs * (inv * inv * inv) * inner
        ).astype(LOW)
        gain_out[...] = jnp.broadcast_to(
            jnp.sum(dnormed * inputs * inv, axis=0, keepdims=True), gain_out.shape
        )


def tokens_back(grads, wq, wk, wv, tokens, gain, dmid, n_heads):
    n, width = tokens.shape
    pairs = n_heads // 2
    span = width // pairs
    whole = lambda *dims: pl.BlockSpec(dims, lambda p: (0,) * len(dims))
    cols = pl.BlockSpec((width, span), lambda p: (0, p))
    return pl.pallas_call(
        tokens_kernel,
        grid=(pairs,),
        in_specs=[
            pl.BlockSpec((n, 3 * span), lambda p: (0, p)),
            cols,
            cols,
            cols,
            whole(n, width),
            whole(1, width),
            whole(n, width),
        ],
        out_specs=[whole(n, width), whole(8, width)],
        out_shape=[shape((n, width), LOW), shape((8, width), F32)],
        scratch_shapes=[pltpu.VMEM((n, width), F32)],
        compiler_params=params(),
        cost_estimate=cost(6 * n * width * width, 6 * width * width + 14 * n * width),
        name="tokens_back",
    )(grads, wq, wk, wv, tokens, gain.reshape(1, width), dmid)


def leave_kernel(res_ref, col_ref, mid_ref, out_ref):
    n = mid_ref.shape[0]
    slots = res_ref.shape[0]
    place = lax.broadcasted_iota(jnp.int32, (n, slots), 1) == col_ref[:, 0:1]
    out_ref[...] = (mid_ref[...] + dot(place.astype(F32).astype(LOW), res_ref[...])).astype(LOW)


def leave(res_rows, col, middle):
    n, width = middle.shape
    return pl.pallas_call(
        leave_kernel,
        out_shape=shape((n, width), LOW),
        compiler_params=params(),
        cost_estimate=cost(2 * n * width * res_rows.shape[0], 10 * n * width),
        name="leave",
    )(res_rows, col, middle)


def exchange(rows):
    return lax.all_to_all(rows, AXES, split_axis=0, concat_axis=0, tiled=True)


def sum_small(parts, n_dev):
    flat = jnp.concatenate([part.reshape(-1) for part in parts])
    size = flat.shape[0]
    lines = -(-size // 1024) * 8
    block = jnp.pad(flat, (0, lines * 128 - size)).reshape(1, lines, 128)
    sent = jnp.broadcast_to(block, (n_dev, lines, 128))
    total = jnp.sum(exchange(sent), axis=0).reshape(-1)
    found, start = [], 0
    for part in parts:
        found.append(total[start : start + part.size].reshape(part.shape))
        start += part.size
    return found


def body(
    n_grp,
    n_loc,
    tokens,
    cotangent,
    w_query,
    w_key,
    w_value,
    w_output,
    attn_gain,
    bias_table,
    moe_gain,
    router_weight,
    router_bias,
    expert_in,
    expert_out,
    expert_ids,
    bucket_ids,
):
    n_rows, width = tokens.shape
    n_buckets, n_heads = bias_table.shape
    n_experts = router_weight.shape[1]
    most = max(2, 2 * n_rows // n_experts)
    slots = n_experts * most
    keep = 5 * n_rows // 4
    me = (lax.axis_index("grp") * lax.axis_size("loc") + lax.axis_index("loc")).reshape(1)

    dy_out, row, col = dispatch(expert_ids, cotangent, slots, most)
    dy_rows = exchange(dy_out)

    table = jnp.pad(bias_table.T, ((0, 0), (0, 128 - n_buckets))).reshape(n_heads // 2, 2, 128)
    query, keys, values, weights, attended, normed_one, middle, x_out = attend(
        tokens, attn_gain, table, bucket_ids, w_query, w_key, w_value, w_output, moe_gain, row,
        slots, n_heads,
    )
    x_rows = exchange(x_out)
    dyc, krow, kcol = arrive(dy_rows, keep)
    dn_sent, res_sent, hidden, dpre, xc, dres, dlogits = expert(
        me, x_rows, dyc, krow, kcol, router_weight, router_bias, expert_in, expert_out
    )
    dn_rows = exchange(dn_sent)
    grad_expert_out = dot(hidden, dres, TN)
    grad_expert_in = dot(xc, dpre, TN)
    grad_router = lax.dot_general(
        dlogits, xc.astype(F32), TN, precision=lax.Precision.HIGHEST, preferred_element_type=F32
    )
    grad_router_bias = jnp.sum(dlogits, axis=0)

    dn_rows, res_sent, grad_expert_in, grad_expert_out = lax.optimization_barrier(
        (dn_rows, res_sent, grad_expert_in, grad_expert_out)
    )
    res_rows = exchange(res_sent)
    dmid, dbranch, datt, moe_gain_rows = middle_back(
        dn_rows, col, middle, cotangent, moe_gain, w_output
    )

    ring = Ring(n_grp, n_loc)
    core = me[0] & 1
    part = width // 2

    def share(value, which, size):
        return lax.dynamic_slice_in_dim(value, which * size, size, 1)

    where = ring.where(me[0])
    extra = -(-n_experts // 128) * 128
    grad_router = jnp.pad(grad_router, ((0, extra - n_experts), (0, 0)))
    out_sent = dot(attended, share(dbranch, 1 - core, part), TN)
    out_kept = dot(attended, share(dbranch, core, part), TN)
    out_sent = jnp.concatenate([out_sent, share(grad_router, 1 - core, part)]).astype(LOW)
    out_kept = jnp.concatenate([out_kept, share(grad_router, core, part)])
    out_pieces = ring.total(out_kept, out_sent, me[0])

    grads, dscores = attend_back(query, keys, values, datt, weights)
    in_sent = dot(normed_one, share(grads, 1 - core, 3 * part), TN).astype(LOW)
    in_kept = dot(normed_one, share(grads, core, 3 * part), TN)
    in_pieces = ring.total(in_kept, in_sent, me[0])

    layer_out = leave(res_rows, col, middle)
    grad_table = table_back(dscores, bucket_ids, n_buckets)
    grad_tokens, attn_gain_rows = tokens_back(
        grads, w_query, w_key, w_value, tokens, attn_gain, dmid, n_heads
    )
    grad_attn_gain, grad_table, grad_moe_gain, grad_router_bias = sum_small(
        (attn_gain_rows[0], grad_table, moe_gain_rows[0], grad_router_bias), n_grp * n_loc
    )
    (grad_output,) = unpack(where, out_pieces, 1)
    grad_query, grad_key, grad_value = unpack(where, in_pieces, 3)
    return (
        layer_out,
        grad_tokens,
        grad_query,
        grad_key,
        grad_value,
        grad_output[:width],
        grad_attn_gain,
        grad_table.T,
        grad_moe_gain,
        grad_output[width : width + n_experts].T,
        grad_router_bias,
        grad_expert_in[None],
        grad_expert_out[None],
    )


def solution(mesh):
    rows, flat = P(AXES, None), P(AXES, None, None)
    return jax.shard_map(
        functools.partial(body, mesh.shape["grp"], mesh.shape["loc"]),
        mesh=mesh,
        in_specs=(
            rows, rows, P(), P(), P(), P(), P(), P(), P(), P(), P(), flat, flat, rows, P(),
        ),
        out_specs=(
            rows, rows, P(), P(), P(), P(), P(), P(), P(), P(), P(), flat, flat,
        ),
        check_vma=False,
    )
```

```python
import functools

import jax
import jax.numpy as jnp
from jax import lax
from jax.experimental import pallas as pl
from jax.experimental.pallas import tpu as pltpu
from jax.sharding import PartitionSpec as P

AXES = ("grp", "loc")
LOW = jnp.bfloat16
F32 = jnp.float32
NN = (((1,), (0,)), ((), ()))
NT = (((1,), (1,)), ((), ()))
TN = (((0,), (0,)), ((), ()))
VMEM_BYTES = 56 * 1024 * 1024
EMPTY = 2.0**20


def dot(left, right, dims=NN):
    return lax.dot_general(left, right, dims, preferred_element_type=F32)


def split(values):
    high = values.astype(LOW)
    rest = values - high.astype(F32)
    middle = rest.astype(LOW)
    return high, middle, (rest - middle.astype(F32)).astype(LOW)


def params():
    return pltpu.CompilerParams(vmem_limit_bytes=VMEM_BYTES)


def cost(flops, nbytes, trans=0):
    return pl.CostEstimate(flops=int(flops), bytes_accessed=int(nbytes), transcendentals=int(trans))


def shape(dims, dtype):
    return jax.ShapeDtypeStruct(dims, dtype)


def norm_scale(values):
    return lax.rsqrt(jnp.mean(values * values, axis=-1, keepdims=True) + 1e-06)


def dispatch_kernel(ids_ref, dy_ref, out_ref, row_ref, col_ref, *, most):
    n = ids_ref.shape[1]
    slots = out_ref.shape[0]
    sub = lax.broadcasted_iota(jnp.int32, (n, n), 0)
    lane = lax.broadcasted_iota(jnp.int32, (n, n), 1)
    ids_row = ids_ref[...]
    ids_col = jnp.sum(jnp.where(sub == lane, ids_row, 0), axis=1, keepdims=True)
    same = ids_col == ids_row
    rank_row = jnp.sum(jnp.where(same & (sub < lane), 1, 0), axis=0, keepdims=True)
    rank_col = jnp.sum(jnp.where(same & (lane < sub), 1, 0), axis=1, keepdims=True)
    half = most // 2

    def halves(ids, rank):
        low = jnp.where(rank < half, ids * half + rank, -1)
        return low, jnp.where(rank < half, -1, ids * half + rank - half)

    low, high = halves(ids_row, rank_row)
    upper = lax.broadcasted_iota(jnp.int32, row_ref.shape, 0) < 4
    row_ref[...] = jnp.where(upper, low, high)
    low, high = halves(ids_col, rank_col)
    spot = lax.broadcasted_iota(jnp.int32, col_ref.shape, 1)
    full = ids_col * most + rank_col
    col_ref[...] = jnp.where(spot < 32, low, jnp.where(spot < 64, high, full))
    place = lax.broadcasted_iota(jnp.int32, (slots, n), 0) == ids_row * most + rank_row
    hot = place.astype(F32)
    filled = jnp.sum(hot, axis=1, keepdims=True)
    rows = dot(hot.astype(LOW), dy_ref[...])
    out_ref[...] = jnp.where(filled > 0.0, rows, EMPTY).astype(LOW)


def dispatch(ids, dy, slots, most):
    n, width = dy.shape
    return pl.pallas_call(
        functools.partial(dispatch_kernel, most=most),
        out_shape=(
            shape((slots, width), LOW),
            shape((8, n), jnp.int32),
            shape((n, 128), jnp.int32),
        ),
        compiler_params=params(),
        cost_estimate=cost(2 * slots * n * width, 4 * slots * width),
        name="dispatch",
    )(ids.reshape(1, n), dy)


def attend_kernel(
    tok_ref,
    gain_ref,
    tab_ref,
    bucket_ref,
    wq_ref,
    wk_ref,
    wv_ref,
    wo_ref,
    moe_gain_ref,
    row_ref,
    q_ref,
    k_ref,
    v_ref,
    w_ref,
    att_t_ref,
    normed_t_ref,
    mid_ref,
    low_ref,
    high_ref,
    wt_ref,
    att_s,
    normed_s,
    *,
    scaling,
):
    step = pl.program_id(0)
    pairs = pl.num_programs(0)
    n = tok_ref.shape[0]

    @pl.when(step == 0)
    def _():
        inputs = tok_ref[...].astype(F32)
        normed_one = (inputs * norm_scale(inputs) * gain_ref[...]).astype(LOW)
        normed_s[...] = normed_one
        normed_t_ref[...] = normed_one.T

    normed = normed_s[...]
    query = dot(normed, wq_ref[...]).astype(LOW)
    keys = dot(normed, wk_ref[...]).astype(LOW)
    values = dot(normed, wv_ref[...]).astype(LOW)
    q_ref[...] = query
    k_ref[...] = keys
    v_ref[...] = values
    span = query.shape[1]
    for i, ref in enumerate((wq_ref, wk_ref, wv_ref)):
        wt_ref[i * span : (i + 1) * span, :] = ref[...].T
    low_half = lax.broadcasted_iota(jnp.int32, query.shape, 1) < query.shape[1] // 2
    zero = jnp.zeros_like(query)
    total = jnp.zeros((n, query.shape[1]), F32)
    for h in range(2):
        mine = low_half if h == 0 else ~low_half
        scores = dot(jnp.where(mine, query, zero), keys, NT) * scaling
        table = jnp.broadcast_to(tab_ref[step, pl.ds(h, 1), :], (n, 128))
        bias = [
            jnp.take_along_axis(
                table, bucket_ref[:, c * 128 : (c + 1) * 128], axis=1, mode="promise_in_bounds"
            )
            for c in range(n // 128)
        ]
        scores = scores + jnp.concatenate(bias, axis=1)
        top = jnp.max(scores, axis=1, keepdims=True)
        grown = jnp.exp(scores - top)
        weights = (grown * (1.0 / jnp.sum(grown, axis=1, keepdims=True))).astype(LOW)
        w_ref[h] = weights
        total = total + dot(weights, jnp.where(mine, values, zero))
    att_s[step] = total.astype(LOW)

    @pl.when(step == pairs - 1)
    def _():
        attended = jnp.concatenate([att_s[i] for i in range(att_s.shape[0])], axis=1)
        att_t_ref[...] = attended.T
        middle = tok_ref[...].astype(F32) + dot(attended, wo_ref[...])
        mid_ref[...] = middle
        normed_two = (middle * norm_scale(middle) * moe_gain_ref[...]).astype(LOW)
        for ref, row in ((low_ref, 0), (high_ref, 4)):
            slot = lax.broadcasted_iota(jnp.int32, (ref.shape[0], n), 0)
            place = slot == row_ref[row : row + 1, :]
            ref[...] = dot(place.astype(F32).astype(LOW), normed_two).astype(LOW)


def attend(tokens, gain, table, buckets, wq, wk, wv, wo, moe_gain, row, slots, n_heads):
    n, width = tokens.shape
    pairs = n_heads // 2
    span = width // pairs
    whole = lambda *dims: pl.BlockSpec(dims, lambda p: (0,) * len(dims))
    cols = lambda rows: pl.BlockSpec((rows, span), lambda p: (0, p))
    return pl.pallas_call(
        functools.partial(attend_kernel, scaling=(width // n_heads) ** -0.5),
        grid=(pairs,),
        in_specs=[
            whole(n, width),
            whole(1, width),
            whole(*table.shape),
            whole(n, n),
            cols(width),
            cols(width),
            cols(width),
            whole(width, width),
            whole(1, width),
            whole(8, n),
        ],
        out_specs=[
            cols(n),
            cols(n),
            cols(n),
            pl.BlockSpec((2, n, n), lambda p: (p, 0, 0)),
            whole(width, n),
            whole(width, n),
            whole(n, width),
            whole(slots // 2, width),
            whole(slots // 2, width),
            pl.BlockSpec((3 * span, width), lambda p: (p, 0)),
        ],
        out_shape=[
            shape((n, width), LOW),
            shape((n, width), LOW),
            shape((n, width), LOW),
            shape((n_heads, n, n), LOW),
            shape((width, n), LOW),
            shape((width, n), LOW),
            shape((n, width), F32),
            shape((slots // 2, width), LOW),
            shape((slots // 2, width), LOW),
            shape((3 * width, width), LOW),
        ],
        scratch_shapes=[pltpu.VMEM((pairs, n, span), LOW), pltpu.VMEM((n, width), LOW)],
        compiler_params=params(),
        cost_estimate=cost(
            8 * n * width * width + 4 * n_heads * n * n * span + 2 * slots * n * width,
            2 * n_heads * n * n + 24 * n * width,
            n_heads * n * n,
        ),
        name="attend",
    )(
        tokens,
        gain.reshape(1, width),
        table,
        buckets,
        wq,
        wk,
        wv,
        wo,
        moe_gain.reshape(1, width),
        row,
    )


def arrive_kernel(dy_ref, low_ref, high_ref, low_kept, high_kept, *, most, keep):
    slots = dy_ref.shape[0]
    half = most // 2
    edge = dy_ref[:, 0:128]
    valid = jnp.where(edge.astype(F32) < EMPTY * 0.5, 1.0, 0.0).astype(LOW)
    sub = lax.broadcasted_iota(jnp.int32, (slots, slots), 0)
    lane = lax.broadcasted_iota(jnp.int32, (slots, slots), 1)
    before = jnp.where(lane < sub, 1.0, 0.0).astype(LOW)
    first = jnp.where(lax.broadcasted_iota(jnp.int32, (8, 128), 1) == 0, 1.0, 0.0).astype(LOW)
    valid_row = dot(first, valid, NT)
    slot_row = dot(valid_row.astype(LOW), before, NT)
    kept = ((valid_row > 0.5) & (slot_row < keep - 0.5))[0:1, :]
    sub = lax.broadcasted_iota(jnp.int32, (slots // 2, slots), 0)
    lane = lax.broadcasted_iota(jnp.int32, (slots // 2, slots), 1)
    here = sub // half * most + sub % half
    for at, ref, kept_ref in ((0, low_ref, low_kept), (half, high_ref, high_kept)):
        place = jnp.where((lane == here + at) & kept, 1.0, 0.0)
        kept_ref[...] = jnp.broadcast_to(jnp.sum(place, axis=1, keepdims=True), kept_ref.shape)
        ref[...] = dot(place.astype(LOW), dy_ref[...]).astype(LOW)


def arrive(dy_rows, most, keep):
    slots, width = dy_rows.shape
    return pl.pallas_call(
        functools.partial(arrive_kernel, most=most, keep=keep),
        out_shape=(
            shape((slots // 2, width), LOW),
            shape((slots // 2, width), LOW),
            shape((slots // 2, 128), F32),
            shape((slots // 2, 128), F32),
        ),
        compiler_params=params(),
        cost_estimate=cost(2 * slots * slots * width, 4 * slots * width),
        name="arrive",
    )(dy_rows)


def expert_kernel(
    me_ref, x_ref, dyc_ref, kept_ref, router_ref, rbias_ref, win_ref, wout_ref, *refs, n_in
):
    dn_ref, res_ref, hid_ref, dpre_ref, dres_ref, dlog_ref, sum_s, drow_s, prob_s = refs[n_in:]
    step = pl.program_id(0)

    def gate_of(probs):
        mine = lax.broadcasted_iota(jnp.int32, probs.shape, 1) == me_ref[0]
        return mine, jnp.sum(jnp.where(mine, probs, 0.0), axis=1, keepdims=True)

    @pl.when(step == 0)
    def _():
        rows = x_ref[...]
        high, middle, low = split(router_ref[...])
        logits = dot(rows, high) + (dot(rows, middle) + dot(rows, low)) + rbias_ref[...]
        grown = jnp.exp(logits - jnp.max(logits, axis=1, keepdims=True))
        probs = grown / jnp.sum(grown, axis=1, keepdims=True)
        prob_s[...] = probs
        dres_ref[...] = (gate_of(probs)[1] * dyc_ref[...].astype(F32)).astype(LOW)
        sum_s[...] = jnp.zeros_like(sum_s)
        drow_s[...] = jnp.zeros_like(drow_s)

    rows = x_ref[...]
    win = win_ref[...]
    wout = wout_ref[...]
    pre = dot(rows, win)
    rate = 0.7978845608028654
    square = pre * pre
    tanh = jnp.tanh(rate * pre * (1.0 + 0.044715 * square))
    half = 0.5 * (1.0 + tanh)
    hidden = (pre * half).astype(LOW)
    slope = half + (0.5 * rate) * pre * (1.0 - tanh * tanh) * (1.0 + 3 * 0.044715 * square)
    dhid = dot(dres_ref[...], wout, NT)
    dpre = (dhid * slope).astype(LOW)
    hid_ref[...] = hidden
    dpre_ref[...] = dpre
    sum_s[...] += dot(hidden, wout)
    drow_s[...] += dot(dpre, win, NT)

    @pl.when(step == pl.num_programs(0) - 1)
    def _():
        result = sum_s[...].astype(LOW).astype(F32)
        dgate = jnp.sum(dyc_ref[...].astype(F32) * result, axis=1, keepdims=True)
        probs = prob_s[...]
        mine, gate = gate_of(probs)
        dlogits = probs * (jnp.where(mine, dgate, 0.0) - gate * dgate)
        dlog_ref[...] = dlogits
        high, middle, _ = split(router_ref[...])
        dhigh, dmiddle, _ = split(dlogits)
        side = dot(dhigh, high, NT) + (dot(dhigh, middle, NT) + dot(dmiddle, high, NT))
        dn_ref[...] = (drow_s[...] + side).astype(LOW)
        res_ref[...] = (kept_ref[:, 0:1] * gate * result).astype(LOW)


def expert(me, rows, dyc, kept, router, rbias, expert_in, expert_out, earlier=()):
    n, width = rows.shape
    n_exp = router.shape[1]
    ff = expert_in.shape[2]
    block = 768 if ff % 768 == 0 else ff
    at = 1 if earlier else 0
    whole = lambda *dims: pl.BlockSpec(dims, lambda f: (0,) * len(dims))
    return pl.pallas_call(
        functools.partial(expert_kernel, n_in=len(earlier)),
        grid=(ff // block,),
        in_specs=[
            pl.BlockSpec(memory_space=pltpu.SMEM),
            whole(n, width),
            whole(n, width),
            whole(n, 128),
            whole(width, n_exp),
            whole(1, n_exp),
            pl.BlockSpec((None, width, block), lambda f: (0, 0, f)),
            pl.BlockSpec((None, block, width), lambda f: (0, f, 0)),
        ]
        + [pl.BlockSpec(memory_space=pl.ANY)] * len(earlier),
        out_specs=[
            whole(n, width),
            whole(n, width),
            pl.BlockSpec((n, block), lambda f: (at, f)),
            pl.BlockSpec((n, block), lambda f: (at, f)),
            pl.BlockSpec((n, width), lambda f: (at, 0)),
            pl.BlockSpec((n, n_exp), lambda f: (at, 0)),
        ],
        out_shape=[
            shape((n, width), LOW),
            shape((n, width), LOW),
            shape((2 * n, ff), LOW),
            shape((2 * n, ff), LOW),
            shape((2 * n, width), LOW),
            shape((2 * n, n_exp), F32),
        ],
        scratch_shapes=[
            pltpu.VMEM((n, width), F32),
            pltpu.VMEM((n, width), F32),
            pltpu.VMEM((n, n_exp), F32),
        ],
        input_output_aliases={8 + i: 2 + i for i in range(len(earlier))},
        compiler_params=params(),
        cost_estimate=cost(8 * n * width * ff, 16 * width * ff, n * ff),
        name="expert",
    )(me, rows, dyc, kept, router, rbias.reshape(1, n_exp), expert_in, expert_out, *earlier)


def back_kernel(
    core_ref,
    low_ref,
    high_ref,
    col_ref,
    mid_ref,
    dy_ref,
    gain_ref,
    wo_ref,
    attended_ref,
    routed_ref,
    q_ref,
    k_ref,
    v_ref,
    w_ref,
    normed_ref,
    dmid_ref,
    gain_out,
    grads_ref,
    ds_ref,
    sent_a,
    kept_a,
    sent_b,
    kept_b,
    datt_s,
    *,
    scaling,
):
    step = pl.program_id(0)
    n, span = q_ref.shape
    width = mid_ref.shape[1]
    part = width // 2
    half = span // 2
    tail = routed_ref.shape[1]
    lead = sent_a.shape[1] - tail - width
    lead_pairs = lead // (3 * span)
    sides = [
        pl.ds(pl.multiple_of(core * part, 128), part) for core in (1 - core_ref[0], core_ref[0])
    ]

    @pl.when(step == 0)
    def _():
        dnormed = jnp.zeros((n, width), F32)
        for ref, at in ((low_ref, 0), (high_ref, 32)):
            place = lax.broadcasted_iota(jnp.int32, (n, ref.shape[0]), 1) == col_ref[:, at : at + 1]
            dnormed = dnormed + dot(place.astype(F32).astype(LOW), ref[...])
        middle = mid_ref[...]
        inv = norm_scale(middle)
        scaled = dnormed * gain_ref[...]
        inner = jnp.mean(scaled * middle, axis=1, keepdims=True)
        dmid = dy_ref[...].astype(F32) + inv * scaled - middle * (inv * inv * inv) * inner
        dmid_ref[...] = dmid
        branch = dmid.astype(LOW)
        datt = dot(branch, wo_ref[...], NT).astype(LOW)
        for p in range(datt_s.shape[0]):
            datt_s[p] = datt[:, p * span : (p + 1) * span]
        gain_out[...] = jnp.broadcast_to(
            jnp.sum(dnormed * middle * inv, axis=0, keepdims=True), gain_out.shape
        )
        for ref, rows in zip((sent_a, kept_a), sides):
            ref[:, :width] = dot(attended_ref[rows, :], branch).astype(LOW)
            ref[:, width + lead :] = routed_ref[rows, :].astype(LOW)

    @pl.when(step > 0)
    def _():
        pair = step - 1
        query, keys, values, grad = q_ref[...], k_ref[...], v_ref[...], datt_s[pair]
        query_t = query.astype(F32).T.astype(LOW)
        grad_t = grad.astype(F32).T.astype(LOW)
        low_half = lax.broadcasted_iota(jnp.int32, query.shape, 1) < half
        zero = jnp.zeros_like(query)
        dquery = jnp.zeros((n, span), F32)
        dkeys, dvalues = [], []
        for h in range(2):
            mine = low_half if h == 0 else ~low_half
            weights_low = w_ref[h]
            weights = weights_low.astype(F32)
            dweights = dot(jnp.where(mine, grad, zero), values, NT)
            both = weights * dweights
            dscores = (both - weights * jnp.sum(both, axis=1, keepdims=True)).astype(LOW)
            ds_ref[h] = dscores
            dquery = dquery + dot(dscores, jnp.where(mine, keys, zero))
            dkeys.append(dot(query_t[h * half : (h + 1) * half, :], dscores))
            dvalues.append(dot(grad_t[h * half : (h + 1) * half, :], weights_low))
        grads = jnp.concatenate(
            [
                dquery * scaling,
                jnp.concatenate(dkeys, axis=0).T * scaling,
                jnp.concatenate(dvalues, axis=0).T,
            ],
            axis=1,
        ).astype(LOW)
        grads_ref[...] = grads
        products = [dot(normed_ref[rows, :], grads).astype(LOW) for rows in sides]

        @pl.when(pair < lead_pairs)
        def _():
            at = pl.multiple_of(width + pair * (3 * span), 128)
            for ref, product in zip((sent_a, kept_a), products):
                ref[:, pl.ds(at, 3 * span)] = product

        @pl.when(pair >= lead_pairs)
        def _():
            at = pl.multiple_of((pair - lead_pairs) * (3 * span), 128)
            for ref, product in zip((sent_b, kept_b), products):
                ref[:, pl.ds(at, 3 * span)] = product


def back(
    core, low, high, col, middle, dy, moe_gain, wo, attended_t, routed, query, keys, values, weights,
    normed_t, lead_pairs,
):
    n_heads, n, _ = weights.shape
    slots, width = low.shape
    pairs = n_heads // 2
    span = width // pairs
    columns_a = width + 3 * span * lead_pairs + routed.shape[1]
    columns_b = 3 * span * (pairs - lead_pairs)
    whole = lambda *dims: pl.BlockSpec(dims, lambda p: (0,) * len(dims))
    pair = lambda p: jnp.maximum(p - 1, 0)
    cols = lambda size: pl.BlockSpec((n, size), lambda p: (0, pair(p)))
    square = pl.BlockSpec((2, n, n), lambda p: (pair(p), 0, 0))
    return pl.pallas_call(
        functools.partial(back_kernel, scaling=(width // n_heads) ** -0.5),
        grid=(1 + pairs,),
        in_specs=[
            pl.BlockSpec(memory_space=pltpu.SMEM),
            whole(slots, width),
            whole(slots, width),
            whole(n, 128),
            whole(n, width),
            whole(n, width),
            whole(1, width),
            whole(width, width),
            whole(width, n),
            whole(*routed.shape),
            cols(span),
            cols(span),
            cols(span),
            square,
            whole(width, n),
        ],
        out_specs=[
            whole(n, width),
            whole(8, width),
            cols(3 * span),
            square,
            whole(width // 2, columns_a),
            whole(width // 2, columns_a),
            whole(width // 2, columns_b),
            whole(width // 2, columns_b),
        ],
        out_shape=[
            shape((n, width), F32),
            shape((8, width), F32),
            shape((n, 3 * width), LOW),
            shape((n_heads, n, n), LOW),
            shape((width // 2, columns_a), LOW),
            shape((width // 2, columns_a), LOW),
            shape((width // 2, columns_b), LOW),
            shape((width // 2, columns_b), LOW),
        ],
        scratch_shapes=[pltpu.VMEM((pairs, n, span), LOW)],
        compiler_params=params(),
        cost_estimate=cost(1000, 1000),
        name="back",
    )(
        core, low, high, col, middle, dy, moe_gain.reshape(1, width), wo, attended_t, routed, query,
        keys, values, weights, normed_t,
    )


def table_kernel(ds_ref, bucket_ref, out_ref, sum_s, *, n_buckets):
    step = pl.program_id(0)
    n_heads, rows, n = ds_ref.shape
    band = 16

    @pl.when(step == 0)
    def _():
        sum_s[...] = jnp.zeros_like(sum_s)

    total = sum_s[...]
    for r in range(rows // band):
        span = slice(r * band, (r + 1) * band)
        grads = ds_ref[:, span, :].reshape(n_heads * band, n)
        buckets = bucket_ref[span, :]
        hot = jnp.concatenate(
            [jnp.where(buckets == b, 1.0, 0.0).astype(LOW) for b in range(n_buckets)], axis=0
        )
        total = total + dot(grads, hot, NT)
    sum_s[...] = total

    @pl.when(step == pl.num_programs(0) - 1)
    def _():
        left = lax.broadcasted_iota(jnp.int32, total.shape, 0) % band
        right = lax.broadcasted_iota(jnp.int32, total.shape, 1) % band
        own = jnp.where(left == right, total, 0.0)
        own = jnp.sum(own.reshape(n_heads, band, n_buckets * band), axis=1)
        bucket = lax.broadcasted_iota(jnp.int32, (n_buckets * band, n_buckets), 1)
        column = lax.broadcasted_iota(jnp.int32, (n_buckets * band, n_buckets), 0)
        fold = jnp.where(column // band == bucket, 1.0, 0.0).astype(LOW)
        high, middle, low = split(own)
        out_ref[...] = dot(high, fold) + dot(middle, fold) + dot(low, fold)


def table_back(dscores, buckets, n_buckets):
    n_heads, n, _ = dscores.shape
    rows, band = 64, 16
    dims = (n_heads * band, n_buckets * band)
    return pl.pallas_call(
        functools.partial(table_kernel, n_buckets=n_buckets),
        grid=(n // rows,),
        in_specs=[
            pl.BlockSpec((n_heads, rows, n), lambda r: (0, r, 0)),
            pl.BlockSpec((rows, n), lambda r: (r, 0)),
        ],
        out_specs=pl.BlockSpec((n_heads, n_buckets), lambda r: (0, 0)),
        out_shape=shape((n_heads, n_buckets), F32),
        scratch_shapes=[pltpu.VMEM(dims, F32)],
        compiler_params=params(),
        cost_estimate=cost(2 * dims[0] * dims[1] * n * n // band, 2 * n_heads * n * n),
        name="table_back",
    )(dscores, buckets)


def add(left, right):
    return (left.astype(F32) + right.astype(F32)).astype(LOW)


def tie(*values):
    return lax.optimization_barrier(values)


class Ring:
    def __init__(self, n_grp, n_loc):
        size = n_grp * n_loc
        bits = size.bit_length() - 1
        low = n_loc.bit_length() - 1
        self.size = size
        ys, xs = list(range(1, low)), list(range(low, bits - 2))
        first, second = (ys + xs, xs + ys) if len(ys) == len(xs) else (ys + xs, ys + xs)
        self.plane = list(zip(first, second))
        self.near, self.far = (bits - 2, bits - 2), (bits - 1, bits - 1)
        self.core = (0, 0)

    def swap(self, value, shifts):
        pairs = [(i, i ^ (1 << shifts[i & 1])) for i in range(self.size)]
        return lax.ppermute(value, AXES, pairs)

    def side(self, me, shifts):
        shift = jnp.where(me & 1 == 0, shifts[0], shifts[1])
        return (me >> shift) & 1

    def cut(self, value, me, shifts):
        halves = value.reshape(2, value.shape[0] // 2, value.shape[1])
        side = self.side(me, shifts)
        return [lax.dynamic_index_in_dim(halves, at, 0, keepdims=False) for at in (1 - side, side)]

    def join(self, value, got, me, shifts):
        side = self.side(me, shifts)
        low = jnp.where(side == 0, value, got)
        high = jnp.where(side == 0, got, value)
        return jnp.concatenate([low, high], axis=0)

    def where(self, me):
        sides = [self.side(me, self.plane[0]), self.side(me ^ 1, self.plane[0])]
        return jnp.stack([me & 1] + sides)


def unpack_kernel(where_ref, own_a, core_a, own_b, core_b, *refs):
    mine = pl.program_id(0) == where_ref[0]
    rows_a = jnp.where(mine, own_a[...], core_a[...]).astype(F32)
    rows_b = jnp.where(mine, own_b[...], core_b[...]).astype(F32)
    outs = refs[-5:]
    width = outs[3].shape[1]
    outs[3][...] = rows_a[:, :width]
    span = 128
    half = rows_b.shape[1] // 3
    rest = width + 3 * half
    outs[4][...] = rows_a[:, rest : rest + outs[4].shape[1]]
    for i in range(3):
        for p in range(half // span):
            at = (3 * p + i) * span
            here = slice(p * span, (p + 1) * span)
            outs[i][:, here] = rows_a[:, width + at : width + at + span]
            there = slice(half + p * span, half + (p + 1) * span)
            outs[i][:, there] = rows_b[:, at : at + span]


def unpack(where, own_a, core_a, own_b, core_b, late, earlier, width, n_experts):
    rows = own_a.shape[0]
    parts = 1
    size = rows // parts
    earlier = tuple(earlier)

    def place(c, r, where_ref):
        side = jnp.where(c == where_ref[0], where_ref[1], where_ref[2])
        return (2 * c + (1 - side if late else side)) * parts + r, 0

    piece = lambda value: pl.BlockSpec((size, value.shape[1]), lambda c, r, where_ref: (r, 0))
    return pl.pallas_call(
        unpack_kernel,
        grid_spec=pltpu.PrefetchScalarGridSpec(
            num_scalar_prefetch=1,
            grid=(2, parts),
            in_specs=[piece(value) for value in (own_a, core_a, own_b, core_b)]
            + [pl.BlockSpec(memory_space=pl.ANY)] * len(earlier),
            out_specs=[pl.BlockSpec((size, width), place)] * 4
            + [pl.BlockSpec((size, n_experts), place)],
        ),
        out_shape=[shape((width, width), F32)] * 4 + [shape((width, n_experts), F32)],
        input_output_aliases={5 + i: i for i in range(len(earlier))},
        compiler_params=params(),
        cost_estimate=cost(rows * width, 24 * rows * width),
        name="unpack",
    )(where, own_a, core_a, own_b, core_b, *earlier)


def tokens_kernel(grads_ref, wt_ref, tok_ref, gain_ref, dmid_ref, out_ref, gain_out, sum_s):
    step = pl.program_id(0)
    part = dot(grads_ref[...], wt_ref[...])

    @pl.when(step == 0)
    def _():
        sum_s[...] = part

    @pl.when(step > 0)
    def _():
        sum_s[...] += part

    @pl.when(step == pl.num_programs(0) - 1)
    def _():
        dnormed = sum_s[...]
        inputs = tok_ref[...].astype(F32)
        inv = norm_scale(inputs)
        scaled = dnormed * gain_ref[...]
        inner = jnp.mean(scaled * inputs, axis=1, keepdims=True)
        out_ref[...] = (
            dmid_ref[...] + inv * scaled - inputs * (inv * inv * inv) * inner
        ).astype(LOW)
        gain_out[...] = jnp.broadcast_to(
            jnp.sum(dnormed * inputs * inv, axis=0, keepdims=True), gain_out.shape
        )


def tokens_back(grads, weights_t, tokens, gain, dmid):
    n, width = tokens.shape
    steps = 3
    block = grads.shape[1] // steps
    whole = lambda *dims: pl.BlockSpec(dims, lambda p: (0,) * len(dims))
    return pl.pallas_call(
        tokens_kernel,
        grid=(steps,),
        in_specs=[
            pl.BlockSpec((n, block), lambda p: (0, p)),
            pl.BlockSpec((block, width), lambda p: (p, 0)),
            whole(n, width),
            whole(1, width),
            whole(n, width),
        ],
        out_specs=[whole(n, width), whole(8, width)],
        out_shape=[shape((n, width), LOW), shape((8, width), F32)],
        scratch_shapes=[pltpu.VMEM((n, width), F32)],
        compiler_params=params(),
        cost_estimate=cost(6 * n * width * width, 6 * width * width + 14 * n * width),
        name="tokens_back",
    )(grads, weights_t, tokens, gain.reshape(1, width), dmid)


def leave_kernel(res_ref, col_ref, mid_ref, out_ref):
    n = mid_ref.shape[0]
    slots = res_ref.shape[0]
    place = lax.broadcasted_iota(jnp.int32, (n, slots), 1) == col_ref[:, 64:65]
    out_ref[...] = (mid_ref[...] + dot(place.astype(F32).astype(LOW), res_ref[...])).astype(LOW)


def leave(res_rows, col, middle):
    n, width = middle.shape
    return pl.pallas_call(
        leave_kernel,
        out_shape=shape((n, width), LOW),
        compiler_params=params(),
        cost_estimate=cost(2 * n * width * res_rows.shape[0], 10 * n * width),
        name="leave",
    )(res_rows, col, middle)


def exchange(rows):
    return lax.all_to_all(rows, AXES, split_axis=0, concat_axis=0, tiled=True)


def sum_small(parts, n_dev):
    flat = jnp.concatenate([part.reshape(-1) for part in parts])
    size = flat.shape[0]
    lines = -(-size // 1024) * 8
    block = jnp.pad(flat, (0, lines * 128 - size)).reshape(1, lines, 128)
    sent = jnp.broadcast_to(block, (n_dev, lines, 128))
    total = jnp.sum(exchange(sent), axis=0).reshape(-1)
    found, start = [], 0
    for part in parts:
        found.append(total[start : start + part.size].reshape(part.shape))
        start += part.size
    return found


def body(
    n_grp,
    n_loc,
    tokens,
    cotangent,
    w_query,
    w_key,
    w_value,
    w_output,
    attn_gain,
    bias_table,
    moe_gain,
    router_weight,
    router_bias,
    expert_in,
    expert_out,
    expert_ids,
    bucket_ids,
):
    n_rows, width = tokens.shape
    n_buckets, n_heads = bias_table.shape
    n_experts = router_weight.shape[1]
    most = max(2, 2 * n_rows // n_experts)
    slots = n_experts * most
    keep = 5 * n_rows // 4
    me = (lax.axis_index("grp") * lax.axis_size("loc") + lax.axis_index("loc")).reshape(1)

    dy_out, row, col = dispatch(expert_ids, cotangent, slots, most)
    dy_out, attn_gain, moe_gain, bias_table = tie(dy_out, attn_gain, moe_gain, bias_table)
    dy_rows = exchange(dy_out)

    table = jnp.pad(bias_table.T, ((0, 0), (0, 128 - n_buckets))).reshape(n_heads // 2, 2, 128)
    query, keys, values, weights, attended_t, normed_t, middle, x_low, x_high, weights_t = attend(
        tokens, attn_gain, table, bucket_ids, w_query, w_key, w_value, w_output, moe_gain, row,
        slots, n_heads,
    )
    dy_rows, x_low = tie(dy_rows, x_low)
    x_low = exchange(x_low)
    arrived = arrive(dy_rows, most, keep)
    x_low, x_high, *arrived = tie(x_low, x_high, *arrived)
    dy_low, dy_high, kept_low, kept_high = arrived
    x_high = exchange(x_high)
    model = (router_weight, router_bias, expert_in, expert_out)
    dn_low, res_low, *earlier = expert(me, x_low, dy_low, kept_low, *model)
    dn_low, x_high = tie(dn_low, x_high)
    dn_low = exchange(dn_low)
    from_high = expert(me, x_high, dy_high, kept_high, *model, earlier)
    dn_low, *from_high = tie(dn_low, *from_high)
    dn_high, res_high, hidden, dpre, dres, dlogits = from_high
    dn_high = exchange(dn_high)
    x_rows = jnp.concatenate([x_low, x_high])
    res_sent = jnp.concatenate(
        [value.reshape(n_experts, most // 2, width) for value in (res_low, res_high)], axis=1
    ).reshape(slots, width)
    grad_expert_out = dot(hidden, dres, TN)
    grad_expert_out, dlogits, x_rows = tie(grad_expert_out, dlogits, x_rows)
    grad_expert_in = dot(x_rows, dpre, TN)
    grad_router = lax.dot_general(
        x_rows.astype(F32), dlogits, TN, precision=lax.Precision.HIGHEST, preferred_element_type=F32
    )
    grad_router_bias = jnp.sum(dlogits, axis=0)

    extra = -(-n_experts // 128) * 128 - n_experts
    routed = jnp.pad(grad_router, ((0, 0), (0, extra)))
    ring = Ring(n_grp, n_loc)
    rank = me[0]
    where = ring.where(rank)
    dn_high, res_sent, grad_expert_in, grad_expert_out, routed, grad_router_bias, where = tie(
        dn_high, res_sent, grad_expert_in, grad_expert_out, routed, grad_router_bias, where
    )
    res_rows = exchange(res_sent)
    dmid, moe_gain_rows, grads, dscores, sent_a, kept_a, sent_b, kept_b = back(
        me & 1, dn_low, dn_high, col, middle, cotangent, moe_gain, w_output, attended_t, routed, query,
        keys, values, weights, normed_t, n_heads // 4,
    )

    def step(kept, got, shifts):
        kept, got = ring.cut(kept, rank, shifts), ring.cut(got, rank, shifts)
        return [add(left, right) for left, right in zip(kept, got)]

    got_a = ring.swap(sent_a, ring.core)
    sent_a, kept_a = step(kept_a, got_a, ring.plane[0])
    got_b = ring.swap(sent_b, ring.core)
    got_b, sent_a = tie(got_b, sent_a)
    got_a = ring.swap(sent_a, ring.plane[0])
    sent_b, kept_b = step(kept_b, got_b, ring.plane[0])
    sent_b, grads = tie(sent_b, grads)
    got_b = ring.swap(sent_b, ring.plane[0])
    grad_tokens, attn_gain_rows = tokens_back(grads, weights_t, tokens, attn_gain, dmid)
    got_a, got_b, grad_tokens, attn_gain_rows, res_rows = tie(
        got_a, got_b, grad_tokens, attn_gain_rows, res_rows
    )
    for shifts in ring.plane[1:] + [ring.near]:
        sent_a, kept_a = step(kept_a, got_a, shifts)
        sent_b, kept_b = step(kept_b, got_b, shifts)
        got_a, got_b = ring.swap(sent_a, shifts), ring.swap(sent_b, shifts)
    value_a, value_b = add(kept_a, got_a), add(kept_b, got_b)
    value_a, value_b, dscores = tie(value_a, value_b, dscores)
    got_a, got_b = ring.swap(value_a, ring.far), ring.swap(value_b, ring.far)
    grad_table = table_back(dscores, bucket_ids, n_buckets)
    got_a, got_b, grad_table = tie(got_a, got_b, grad_table)
    value_a, value_b = add(value_a, got_a), add(value_b, got_b)
    for place, shifts in enumerate(reversed(ring.plane[1:] + [ring.near])):
        if place == 0:
            value_a, value_b, res_rows = tie(value_a, value_b, res_rows)
        if place == 1:
            value_a, value_b, grad_table = tie(value_a, value_b, grad_table)
        got_a, got_b = ring.swap(value_a, shifts), ring.swap(value_b, shifts)
        if place == 0:
            layer_out = leave(res_rows, col, middle)
            got_a, got_b, layer_out = tie(got_a, got_b, layer_out)
        if place == 1:
            smalls = sum_small(
                (attn_gain_rows[0], grad_table, moe_gain_rows[0], grad_router_bias), n_grp * n_loc
            )
        value_a = ring.join(value_a, got_a, rank, shifts)
        value_b = ring.join(value_b, got_b, rank, shifts)
    near_a, near_b = ring.swap(value_a, ring.plane[0]), ring.swap(value_b, ring.plane[0])
    core_a, core_b = ring.swap(value_a, ring.core), ring.swap(value_b, ring.core)
    outs = unpack(where, value_a, core_a, value_b, core_b, False, (), width, n_experts)
    near_a, near_b, *rest = tie(near_a, near_b, *outs, *smalls)
    outs, smalls = rest[:5], rest[5:]
    far_a, far_b = ring.swap(near_a, ring.core), ring.swap(near_b, ring.core)
    outs = unpack(where, near_a, far_a, near_b, far_b, True, outs, width, n_experts)
    grad_query, grad_key, grad_value, grad_output, grad_router = outs
    grad_attn_gain, grad_table, grad_moe_gain, grad_router_bias = smalls
    return (
        layer_out,
        grad_tokens,
        grad_query,
        grad_key,
        grad_value,
        grad_output,
        grad_attn_gain,
        grad_table.T,
        grad_moe_gain,
        grad_router,
        grad_router_bias,
        grad_expert_in[None],
        grad_expert_out[None],
    )


def solution(mesh):
    rows, flat = P(AXES, None), P(AXES, None, None)
    return jax.shard_map(
        functools.partial(body, mesh.shape["grp"], mesh.shape["loc"]),
        mesh=mesh,
        in_specs=(
            rows, rows, P(), P(), P(), P(), P(), P(), P(), P(), P(), flat, flat, rows, P(),
        ),
        out_specs=(
            rows, rows, P(), P(), P(), P(), P(), P(), P(), P(), P(), flat, flat,
        ),
        check_vma=False,
    )
```

```python
import functools

import jax
import jax.numpy as jnp
from jax import lax
from jax.experimental import pallas as pl
from jax.experimental.pallas import tpu as pltpu
from jax.sharding import PartitionSpec as P

AXES = ("grp", "loc")
LOW = jnp.bfloat16
F32 = jnp.float32
NN = (((1,), (0,)), ((), ()))
NT = (((1,), (1,)), ((), ()))
TN = (((0,), (0,)), ((), ()))
VMEM_BYTES = 56 * 1024 * 1024
EMPTY = 2.0**20


def dot(left, right, dims=NN):
    return lax.dot_general(left, right, dims, preferred_element_type=F32)


def split(values):
    high = values.astype(LOW)
    rest = values - high.astype(F32)
    middle = rest.astype(LOW)
    return high, middle, (rest - middle.astype(F32)).astype(LOW)


def params():
    return pltpu.CompilerParams(vmem_limit_bytes=VMEM_BYTES)


def cost(flops, nbytes, trans=0):
    return pl.CostEstimate(flops=int(flops), bytes_accessed=int(nbytes), transcendentals=int(trans))


def shape(dims, dtype):
    return jax.ShapeDtypeStruct(dims, dtype)


def norm_scale(values):
    return lax.rsqrt(jnp.mean(values * values, axis=-1, keepdims=True) + 1e-06)


def dispatch_kernel(ids_ref, dy_ref, out_ref, row_ref, col_ref, *, most):
    n = ids_ref.shape[1]
    slots = out_ref.shape[0]
    sub = lax.broadcasted_iota(jnp.int32, (n, n), 0)
    lane = lax.broadcasted_iota(jnp.int32, (n, n), 1)
    ids_row = ids_ref[...]
    ids_col = jnp.sum(jnp.where(sub == lane, ids_row, 0), axis=1, keepdims=True)
    same = ids_col == ids_row
    rank_row = jnp.sum(jnp.where(same & (sub < lane), 1, 0), axis=0, keepdims=True)
    rank_col = jnp.sum(jnp.where(same & (lane < sub), 1, 0), axis=1, keepdims=True)
    half = most // 2

    def halves(ids, rank):
        low = jnp.where(rank < half, ids * half + rank, -1)
        return low, jnp.where(rank < half, -1, ids * half + rank - half)

    low, high = halves(ids_row, rank_row)
    upper = lax.broadcasted_iota(jnp.int32, row_ref.shape, 0) < 4
    row_ref[...] = jnp.where(upper, low, high)
    low, high = halves(ids_col, rank_col)
    spot = lax.broadcasted_iota(jnp.int32, col_ref.shape, 1)
    full = ids_col * most + rank_col
    col_ref[...] = jnp.where(spot < 32, low, jnp.where(spot < 64, high, full))
    place = lax.broadcasted_iota(jnp.int32, (slots, n), 0) == ids_row * most + rank_row
    hot = place.astype(F32)
    filled = jnp.sum(hot, axis=1, keepdims=True)
    rows = dot(hot.astype(LOW), dy_ref[...])
    out_ref[...] = jnp.where(filled > 0.0, rows, EMPTY).astype(LOW)


def dispatch(ids, dy, slots, most):
    n, width = dy.shape
    return pl.pallas_call(
        functools.partial(dispatch_kernel, most=most),
        out_shape=(
            shape((slots, width), LOW),
            shape((8, n), jnp.int32),
            shape((n, 128), jnp.int32),
        ),
        compiler_params=params(),
        cost_estimate=cost(2 * slots * n * width, 4 * slots * width),
        name="dispatch",
    )(ids.reshape(1, n), dy)


def attend_kernel(
    tok_ref,
    gain_ref,
    tab_ref,
    bucket_ref,
    wq_ref,
    wk_ref,
    wv_ref,
    wo_ref,
    moe_gain_ref,
    row_ref,
    q_ref,
    k_ref,
    v_ref,
    w_ref,
    att_t_ref,
    normed_t_ref,
    mid_ref,
    low_ref,
    high_ref,
    wt_ref,
    att_s,
    normed_s,
    *,
    scaling,
):
    step = pl.program_id(0)
    pairs = pl.num_programs(0)
    n = tok_ref.shape[0]

    @pl.when(step == 0)
    def _():
        inputs = tok_ref[...].astype(F32)
        normed_one = (inputs * norm_scale(inputs) * gain_ref[...]).astype(LOW)
        normed_s[...] = normed_one
        normed_t_ref[...] = normed_one.T

    normed = normed_s[...]
    query = dot(normed, wq_ref[...]).astype(LOW)
    keys = dot(normed, wk_ref[...]).astype(LOW)
    values = dot(normed, wv_ref[...]).astype(LOW)
    q_ref[...] = query
    k_ref[...] = keys
    v_ref[...] = values
    span = query.shape[1]
    for i, ref in enumerate((wq_ref, wk_ref, wv_ref)):
        wt_ref[i * span : (i + 1) * span, :] = ref[...].T
    low_half = lax.broadcasted_iota(jnp.int32, query.shape, 1) < query.shape[1] // 2
    zero = jnp.zeros_like(query)
    total = jnp.zeros((n, query.shape[1]), F32)
    for h in range(2):
        mine = low_half if h == 0 else ~low_half
        scores = dot(jnp.where(mine, query, zero), keys, NT) * scaling
        table = jnp.broadcast_to(tab_ref[step, pl.ds(h, 1), :], (n, 128))
        bias = [
            jnp.take_along_axis(
                table, bucket_ref[:, c * 128 : (c + 1) * 128], axis=1, mode="promise_in_bounds"
            )
            for c in range(n // 128)
        ]
        scores = scores + jnp.concatenate(bias, axis=1)
        top = jnp.max(scores, axis=1, keepdims=True)
        grown = jnp.exp(scores - top)
        weights = (grown * (1.0 / jnp.sum(grown, axis=1, keepdims=True))).astype(LOW)
        w_ref[h] = weights
        total = total + dot(weights, jnp.where(mine, values, zero))
    att_s[step] = total.astype(LOW)

    @pl.when(step == pairs - 1)
    def _():
        attended = jnp.concatenate([att_s[i] for i in range(att_s.shape[0])], axis=1)
        att_t_ref[...] = attended.T
        middle = tok_ref[...].astype(F32) + dot(attended, wo_ref[...])
        mid_ref[...] = middle
        normed_two = (middle * norm_scale(middle) * moe_gain_ref[...]).astype(LOW)
        for ref, row in ((low_ref, 0), (high_ref, 4)):
            slot = lax.broadcasted_iota(jnp.int32, (ref.shape[0], n), 0)
            place = slot == row_ref[row : row + 1, :]
            ref[...] = dot(place.astype(F32).astype(LOW), normed_two).astype(LOW)


def attend(tokens, gain, table, buckets, wq, wk, wv, wo, moe_gain, row, slots, n_heads):
    n, width = tokens.shape
    pairs = n_heads // 2
    span = width // pairs
    whole = lambda *dims: pl.BlockSpec(dims, lambda p: (0,) * len(dims))
    cols = lambda rows: pl.BlockSpec((rows, span), lambda p: (0, p))
    return pl.pallas_call(
        functools.partial(attend_kernel, scaling=(width // n_heads) ** -0.5),
        grid=(pairs,),
        in_specs=[
            whole(n, width),
            whole(1, width),
            whole(*table.shape),
            whole(n, n),
            cols(width),
            cols(width),
            cols(width),
            whole(width, width),
            whole(1, width),
            whole(8, n),
        ],
        out_specs=[
            cols(n),
            cols(n),
            cols(n),
            pl.BlockSpec((2, n, n), lambda p: (p, 0, 0)),
            whole(width, n),
            whole(width, n),
            whole(n, width),
            whole(slots // 2, width),
            whole(slots // 2, width),
            pl.BlockSpec((3 * span, width), lambda p: (p, 0)),
        ],
        out_shape=[
            shape((n, width), LOW),
            shape((n, width), LOW),
            shape((n, width), LOW),
            shape((n_heads, n, n), LOW),
            shape((width, n), LOW),
            shape((width, n), LOW),
            shape((n, width), F32),
            shape((slots // 2, width), LOW),
            shape((slots // 2, width), LOW),
            shape((3 * width, width), LOW),
        ],
        scratch_shapes=[pltpu.VMEM((pairs, n, span), LOW), pltpu.VMEM((n, width), LOW)],
        compiler_params=params(),
        cost_estimate=cost(
            8 * n * width * width + 4 * n_heads * n * n * span + 2 * slots * n * width,
            2 * n_heads * n * n + 24 * n * width,
            n_heads * n * n,
        ),
        name="attend",
    )(
        tokens,
        gain.reshape(1, width),
        table,
        buckets,
        wq,
        wk,
        wv,
        wo,
        moe_gain.reshape(1, width),
        row,
    )


def arrive_kernel(dy_ref, low_ref, high_ref, low_kept, high_kept, *, most, keep):
    slots = dy_ref.shape[0]
    half = most // 2
    edge = dy_ref[:, 0:128]
    valid = jnp.where(edge.astype(F32) < EMPTY * 0.5, 1.0, 0.0).astype(LOW)
    sub = lax.broadcasted_iota(jnp.int32, (slots, slots), 0)
    lane = lax.broadcasted_iota(jnp.int32, (slots, slots), 1)
    before = jnp.where(lane < sub, 1.0, 0.0).astype(LOW)
    first = jnp.where(lax.broadcasted_iota(jnp.int32, (8, 128), 1) == 0, 1.0, 0.0).astype(LOW)
    valid_row = dot(first, valid, NT)
    slot_row = dot(valid_row.astype(LOW), before, NT)
    kept = ((valid_row > 0.5) & (slot_row < keep - 0.5))[0:1, :]
    sub = lax.broadcasted_iota(jnp.int32, (slots // 2, slots), 0)
    lane = lax.broadcasted_iota(jnp.int32, (slots // 2, slots), 1)
    here = sub // half * most + sub % half
    for at, ref, kept_ref in ((0, low_ref, low_kept), (half, high_ref, high_kept)):
        place = jnp.where((lane == here + at) & kept, 1.0, 0.0)
        kept_ref[...] = jnp.broadcast_to(jnp.sum(place, axis=1, keepdims=True), kept_ref.shape)
        ref[...] = dot(place.astype(LOW), dy_ref[...]).astype(LOW)


def arrive(dy_rows, most, keep):
    slots, width = dy_rows.shape
    return pl.pallas_call(
        functools.partial(arrive_kernel, most=most, keep=keep),
        out_shape=(
            shape((slots // 2, width), LOW),
            shape((slots // 2, width), LOW),
            shape((slots // 2, 128), F32),
            shape((slots // 2, 128), F32),
        ),
        compiler_params=params(),
        cost_estimate=cost(2 * slots * slots * width, 4 * slots * width),
        name="arrive",
    )(dy_rows)


def expert_kernel(
    me_ref, x_ref, dyc_ref, kept_ref, router_ref, rbias_ref, win_ref, wout_ref, *refs, n_in
):
    dn_ref, res_ref, hid_ref, dpre_ref, dres_ref, dlog_ref, sum_s, drow_s, prob_s = refs[n_in:]
    step = pl.program_id(0)

    def gate_of(probs):
        mine = lax.broadcasted_iota(jnp.int32, probs.shape, 1) == me_ref[0]
        return mine, jnp.sum(jnp.where(mine, probs, 0.0), axis=1, keepdims=True)

    @pl.when(step == 0)
    def _():
        rows = x_ref[...]
        high, middle, low = split(router_ref[...])
        logits = dot(rows, high) + (dot(rows, middle) + dot(rows, low)) + rbias_ref[...]
        grown = jnp.exp(logits - jnp.max(logits, axis=1, keepdims=True))
        probs = grown / jnp.sum(grown, axis=1, keepdims=True)
        prob_s[...] = probs
        dres_ref[...] = (gate_of(probs)[1] * dyc_ref[...].astype(F32)).astype(LOW)
        sum_s[...] = jnp.zeros_like(sum_s)
        drow_s[...] = jnp.zeros_like(drow_s)

    rows = x_ref[...]
    win = win_ref[...]
    wout = wout_ref[...]
    pre = dot(rows, win)
    rate = 0.7978845608028654
    square = pre * pre
    tanh = jnp.tanh(rate * pre * (1.0 + 0.044715 * square))
    half = 0.5 * (1.0 + tanh)
    hidden = (pre * half).astype(LOW)
    slope = half + (0.5 * rate) * pre * (1.0 - tanh * tanh) * (1.0 + 3 * 0.044715 * square)
    dhid = dot(dres_ref[...], wout, NT)
    dpre = (dhid * slope).astype(LOW)
    hid_ref[...] = hidden
    dpre_ref[...] = dpre
    sum_s[...] += dot(hidden, wout)
    drow_s[...] += dot(dpre, win, NT)

    @pl.when(step == pl.num_programs(0) - 1)
    def _():
        result = sum_s[...].astype(LOW).astype(F32)
        dgate = jnp.sum(dyc_ref[...].astype(F32) * result, axis=1, keepdims=True)
        probs = prob_s[...]
        mine, gate = gate_of(probs)
        dlogits = probs * (jnp.where(mine, dgate, 0.0) - gate * dgate)
        dlog_ref[...] = dlogits
        high, middle, _ = split(router_ref[...])
        dhigh, dmiddle, _ = split(dlogits)
        side = dot(dhigh, high, NT) + (dot(dhigh, middle, NT) + dot(dmiddle, high, NT))
        dn_ref[...] = (drow_s[...] + side).astype(LOW)
        res_ref[...] = (kept_ref[:, 0:1] * gate * result).astype(LOW)


def expert(me, rows, dyc, kept, router, rbias, expert_in, expert_out, earlier=()):
    n, width = rows.shape
    n_exp = router.shape[1]
    ff = expert_in.shape[2]
    block = 768 if ff % 768 == 0 else ff
    at = 1 if earlier else 0
    whole = lambda *dims: pl.BlockSpec(dims, lambda f: (0,) * len(dims))
    return pl.pallas_call(
        functools.partial(expert_kernel, n_in=len(earlier)),
        grid=(ff // block,),
        in_specs=[
            pl.BlockSpec(memory_space=pltpu.SMEM),
            whole(n, width),
            whole(n, width),
            whole(n, 128),
            whole(width, n_exp),
            whole(1, n_exp),
            pl.BlockSpec((None, width, block), lambda f: (0, 0, f)),
            pl.BlockSpec((None, block, width), lambda f: (0, f, 0)),
        ]
        + [pl.BlockSpec(memory_space=pl.ANY)] * len(earlier),
        out_specs=[
            whole(n, width),
            whole(n, width),
            pl.BlockSpec((n, block), lambda f: (at, f)),
            pl.BlockSpec((n, block), lambda f: (at, f)),
            pl.BlockSpec((n, width), lambda f: (at, 0)),
            pl.BlockSpec((n, n_exp), lambda f: (at, 0)),
        ],
        out_shape=[
            shape((n, width), LOW),
            shape((n, width), LOW),
            shape((2 * n, ff), LOW),
            shape((2 * n, ff), LOW),
            shape((2 * n, width), LOW),
            shape((2 * n, n_exp), F32),
        ],
        scratch_shapes=[
            pltpu.VMEM((n, width), F32),
            pltpu.VMEM((n, width), F32),
            pltpu.VMEM((n, n_exp), F32),
        ],
        input_output_aliases={8 + i: 2 + i for i in range(len(earlier))},
        compiler_params=params(),
        cost_estimate=cost(8 * n * width * ff, 16 * width * ff, n * ff),
        name="expert",
    )(me, rows, dyc, kept, router, rbias.reshape(1, n_exp), expert_in, expert_out, *earlier)


def weights_kernel(
    low_ref, high_ref, hid_ref, dpre_ref, dres_ref, dlog_ref, in_ref, out_ref, routed_ref, bias_ref,
    x_s,
):
    @pl.when(pl.program_id(0) == 0)
    def _():
        n = low_ref.shape[0]
        x_s[:, :n] = low_ref[...].T
        x_s[:, n:] = high_ref[...].T
        dlogits = dlog_ref[...]
        rows = x_s[...]
        high, middle, low = split(dlogits)
        routed = dot(rows, high) + (dot(rows, middle) + dot(rows, low))
        routed_ref[...] = jnp.zeros_like(routed_ref)
        routed_ref[:, : routed.shape[1]] = routed
        bias_ref[...] = jnp.broadcast_to(jnp.sum(dlogits, axis=0, keepdims=True), bias_ref.shape)

    in_ref[...] = dot(x_s[...], dpre_ref[...])
    out_ref[...] = dot(hid_ref[...].T, dres_ref[...])


def weights_back(x_low, x_high, hidden, dpre, dres, dlogits):
    n, width = x_low.shape
    ff = hidden.shape[1]
    n_exp = dlogits.shape[1]
    tail = -(-n_exp // 128) * 128
    block = 512 if ff % 512 == 0 else ff
    whole = lambda *dims: pl.BlockSpec(dims, lambda f: (0,) * len(dims))
    cols = lambda rows: pl.BlockSpec((rows, block), lambda f: (0, f))
    return pl.pallas_call(
        weights_kernel,
        grid=(ff // block,),
        in_specs=[
            whole(n, width),
            whole(n, width),
            cols(2 * n),
            cols(2 * n),
            whole(2 * n, width),
            whole(2 * n, n_exp),
        ],
        out_specs=[
            cols(width),
            pl.BlockSpec((block, width), lambda f: (f, 0)),
            whole(width, tail),
            whole(8, n_exp),
        ],
        out_shape=[
            shape((width, ff), F32),
            shape((ff, width), F32),
            shape((width, tail), F32),
            shape((8, n_exp), F32),
        ],
        scratch_shapes=[pltpu.VMEM((width, 2 * n), LOW)],
        compiler_params=params(),
        cost_estimate=cost(8 * n * width * ff, 8 * width * ff),
        name="weights_back",
    )(x_low, x_high, hidden, dpre, dres, dlogits)


def back_kernel(
    core_ref,
    low_hbm,
    high_hbm,
    col_hbm,
    mid_hbm,
    dy_hbm,
    wo_hbm,
    attended_hbm,
    routed_hbm,
    normed_hbm,
    gain_ref,
    q_ref,
    k_ref,
    v_ref,
    w_ref,
    dmid_hbm,
    sent_hbm,
    kept_hbm,
    gain_out,
    grads_ref,
    ds_ref,
    sent_b,
    kept_b,
    datt_s,
    low_ref,
    high_ref,
    col_ref,
    mid_ref,
    dy_ref,
    wo_ref,
    attended_ref,
    routed_ref,
    normed_ref,
    dmid_ref,
    sent_a,
    kept_a,
    sems,
    *,
    scaling,
):
    step = pl.program_id(0)
    n, span = q_ref.shape
    width = mid_ref.shape[1]
    part = width // 2
    half = span // 2
    tail = routed_ref.shape[1]
    lead = sent_a.shape[1] - tail - width
    lead_pairs = lead // (3 * span)
    sides = [
        pl.ds(pl.multiple_of(core * part, 128), part) for core in (1 - core_ref[0], core_ref[0])
    ]
    ins = [
        (low_hbm, low_ref),
        (high_hbm, high_ref),
        (col_hbm, col_ref),
        (mid_hbm, mid_ref),
        (dy_hbm, dy_ref),
        (wo_hbm, wo_ref),
        (attended_hbm, attended_ref),
        (routed_hbm, routed_ref),
        (normed_hbm, normed_ref),
    ]
    outs = [(dmid_ref, dmid_hbm), (sent_a, sent_hbm), (kept_a, kept_hbm)]
    copies = [
        pltpu.make_async_copy(source, target, sems.at[at])
        for at, (source, target) in enumerate(ins + outs)
    ]
    from_low, from_high, from_col, from_mid, from_dy, from_wo, from_att, from_routed = copies[:8]
    from_normed, to_dmid, to_sent, to_kept = copies[8:]

    @pl.when(step == 0)
    def _():
        for copy in copies[:9]:
            copy.start()
        dnormed = jnp.zeros((n, width), F32)
        from_col.wait()
        for copy, ref, at in ((from_low, low_ref, 0), (from_high, high_ref, 32)):
            place = lax.broadcasted_iota(jnp.int32, (n, ref.shape[0]), 1) == col_ref[:, at : at + 1]
            copy.wait()
            dnormed = dnormed + dot(place.astype(F32).astype(LOW), ref[...])
        from_mid.wait()
        from_dy.wait()
        middle = mid_ref[...]
        inv = norm_scale(middle)
        scaled = dnormed * gain_ref[...]
        inner = jnp.mean(scaled * middle, axis=1, keepdims=True)
        dmid = dy_ref[...].astype(F32) + inv * scaled - middle * (inv * inv * inv) * inner
        dmid_ref[...] = dmid
        to_dmid.start()
        branch = dmid.astype(LOW)
        from_wo.wait()
        datt = dot(branch, wo_ref[...], NT).astype(LOW)
        for p in range(datt_s.shape[0]):
            datt_s[p] = datt[:, p * span : (p + 1) * span]
        gain_out[...] = jnp.broadcast_to(
            jnp.sum(dnormed * middle * inv, axis=0, keepdims=True), gain_out.shape
        )
        from_att.wait()
        from_routed.wait()
        for ref, rows in zip((sent_a, kept_a), sides):
            ref[:, :width] = dot(attended_ref[rows, :], branch).astype(LOW)
            ref[:, width + lead :] = routed_ref[rows, :].astype(LOW)
        from_normed.wait()

    @pl.when(step > 0)
    def _():
        pair = step - 1
        query, keys, values, grad = q_ref[...], k_ref[...], v_ref[...], datt_s[pair]
        low_half = lax.broadcasted_iota(jnp.int32, query.shape, 1) < half
        low_rows = lax.broadcasted_iota(jnp.int32, (span, n), 0) < half

        def stack(value):
            zero = jnp.zeros_like(value)
            return jnp.concatenate(
                [jnp.where(low_half, value, zero), jnp.where(low_half, zero, value)], axis=0
            )

        def spread(value):
            value = value.astype(F32).T.astype(LOW)
            zero = jnp.zeros_like(value)
            return jnp.concatenate(
                [jnp.where(low_rows, value, zero), jnp.where(low_rows, zero, value)], axis=1
            )

        weights_low = jnp.concatenate([w_ref[0], w_ref[1]], axis=0)
        weights = weights_low.astype(F32)
        both = weights * dot(stack(grad), values, NT)
        dscores = (both - weights * jnp.sum(both, axis=1, keepdims=True)).astype(LOW)
        ds_ref[0] = dscores[:n]
        ds_ref[1] = dscores[n:]
        dquery = dot(jnp.concatenate([dscores[:n], dscores[n:]], axis=1), stack(keys))
        dvalues = dot(spread(grad), weights_low)
        dkeys = dot(spread(query), dscores)
        grads = jnp.concatenate([dquery * scaling, dkeys.T * scaling, dvalues.T], axis=1)
        grads = grads.astype(LOW)
        grads_ref[...] = grads
        products = [dot(normed_ref[rows, :], grads).astype(LOW) for rows in sides]

        @pl.when(pair < lead_pairs)
        def _():
            at = pl.multiple_of(width + pair * (3 * span), 128)
            for ref, product in zip((sent_a, kept_a), products):
                ref[:, pl.ds(at, 3 * span)] = product

        @pl.when(pair >= lead_pairs)
        def _():
            for ref, product in zip((sent_b, kept_b), products):
                ref[...] = product

    @pl.when(step == lead_pairs)
    def _():
        to_sent.start()
        to_kept.start()

    @pl.when(step == pl.num_programs(0) - 1)
    def _():
        to_dmid.wait()
        to_sent.wait()
        to_kept.wait()


def back(
    core, low, high, col, middle, dy, moe_gain, wo, attended_t, routed, query, keys, values, weights,
    normed_t, lead_pairs,
):
    n_heads, n, _ = weights.shape
    width = low.shape[1]
    pairs = n_heads // 2
    span = width // pairs
    part = width // 2
    columns_a = width + 3 * span * lead_pairs + routed.shape[1]
    columns_b = 3 * span * (pairs - lead_pairs)
    pair = lambda p: jnp.maximum(p - 1, 0)
    late = lambda p: jnp.maximum(p - 1 - lead_pairs, 0)
    cols = lambda size: pl.BlockSpec((n, size), lambda p: (0, pair(p)))
    square = pl.BlockSpec((2, n, n), lambda p: (pair(p), 0, 0))
    piece = pl.BlockSpec((part, 3 * span), lambda p: (0, late(p)))
    anywhere = pl.BlockSpec(memory_space=pl.ANY)
    loaded = (low, high, col, middle, dy, wo, attended_t, routed, normed_t)
    return pl.pallas_call(
        functools.partial(back_kernel, scaling=(width // n_heads) ** -0.5),
        grid=(1 + pairs,),
        in_specs=[pl.BlockSpec(memory_space=pltpu.SMEM)]
        + [anywhere] * len(loaded)
        + [pl.BlockSpec((1, width), lambda p: (0, 0)), cols(span), cols(span), cols(span), square],
        out_specs=[anywhere] * 3
        + [pl.BlockSpec((8, width), lambda p: (0, 0)), cols(3 * span), square, piece, piece],
        out_shape=[
            shape((n, width), F32),
            shape((part, columns_a), LOW),
            shape((part, columns_a), LOW),
            shape((8, width), F32),
            shape((n, 3 * width), LOW),
            shape((n_heads, n, n), LOW),
            shape((part, columns_b), LOW),
            shape((part, columns_b), LOW),
        ],
        scratch_shapes=[pltpu.VMEM((pairs, n, span), LOW)]
        + [pltpu.VMEM(value.shape, value.dtype) for value in loaded]
        + [
            pltpu.VMEM((n, width), F32),
            pltpu.VMEM((part, columns_a), LOW),
            pltpu.VMEM((part, columns_a), LOW),
            pltpu.SemaphoreType.DMA((len(loaded) + 3,)),
        ],
        compiler_params=params(),
        cost_estimate=cost(1000, 1000),
        name="back",
    )(core, *loaded, moe_gain.reshape(1, width), query, keys, values, weights)


def table_kernel(ds_ref, bucket_ref, out_ref, sum_s, *, n_buckets):
    step = pl.program_id(0)
    n_heads, rows, n = ds_ref.shape
    band = 16

    @pl.when(step == 0)
    def _():
        sum_s[...] = jnp.zeros_like(sum_s)

    total = sum_s[...]
    for r in range(rows // band):
        span = slice(r * band, (r + 1) * band)
        grads = ds_ref[:, span, :].reshape(n_heads * band, n)
        buckets = bucket_ref[span, :]
        hot = jnp.concatenate(
            [jnp.where(buckets == b, 1.0, 0.0).astype(LOW) for b in range(n_buckets)], axis=0
        )
        total = total + dot(grads, hot, NT)
    sum_s[...] = total

    @pl.when(step == pl.num_programs(0) - 1)
    def _():
        left = lax.broadcasted_iota(jnp.int32, total.shape, 0) % band
        right = lax.broadcasted_iota(jnp.int32, total.shape, 1) % band
        own = jnp.where(left == right, total, 0.0)
        own = jnp.sum(own.reshape(n_heads, band, n_buckets * band), axis=1)
        bucket = lax.broadcasted_iota(jnp.int32, (n_buckets * band, n_buckets), 1)
        column = lax.broadcasted_iota(jnp.int32, (n_buckets * band, n_buckets), 0)
        fold = jnp.where(column // band == bucket, 1.0, 0.0).astype(LOW)
        high, middle, low = split(own)
        out_ref[...] = dot(high, fold) + dot(middle, fold) + dot(low, fold)


def table_back(dscores, buckets, n_buckets):
    n_heads, n, _ = dscores.shape
    rows, band = 64, 16
    dims = (n_heads * band, n_buckets * band)
    return pl.pallas_call(
        functools.partial(table_kernel, n_buckets=n_buckets),
        grid=(n // rows,),
        in_specs=[
            pl.BlockSpec((n_heads, rows, n), lambda r: (0, r, 0)),
            pl.BlockSpec((rows, n), lambda r: (r, 0)),
        ],
        out_specs=pl.BlockSpec((n_heads, n_buckets), lambda r: (0, 0)),
        out_shape=shape((n_heads, n_buckets), F32),
        scratch_shapes=[pltpu.VMEM(dims, F32)],
        compiler_params=params(),
        cost_estimate=cost(2 * dims[0] * dims[1] * n * n // band, 2 * n_heads * n * n),
        name="table_back",
    )(dscores, buckets)


def add(left, right):
    return (left.astype(F32) + right.astype(F32)).astype(LOW)


def tie(*values):
    return lax.optimization_barrier(values)


class Ring:
    def __init__(self, n_grp, n_loc):
        size = n_grp * n_loc
        bits = size.bit_length() - 1
        low = n_loc.bit_length() - 1
        self.size = size
        ys, xs = list(range(1, low)), list(range(low, bits - 2))
        first, second = (ys + xs, xs + ys) if len(ys) == len(xs) else (ys + xs, ys + xs)
        self.plane = list(zip(first, second))
        self.near, self.far = (bits - 2, bits - 2), (bits - 1, bits - 1)
        self.core = (0, 0)

    def swap(self, value, shifts):
        pairs = [(i, i ^ (1 << shifts[i & 1])) for i in range(self.size)]
        return lax.ppermute(value, AXES, pairs)

    def side(self, me, shifts):
        shift = jnp.where(me & 1 == 0, shifts[0], shifts[1])
        return (me >> shift) & 1

    def cut(self, value, me, shifts):
        halves = value.reshape(2, value.shape[0] // 2, value.shape[1])
        side = self.side(me, shifts)
        return [lax.dynamic_index_in_dim(halves, at, 0, keepdims=False) for at in (1 - side, side)]

    def join(self, value, got, me, shifts):
        side = self.side(me, shifts)
        low = jnp.where(side == 0, value, got)
        high = jnp.where(side == 0, got, value)
        return jnp.concatenate([low, high], axis=0)

    def where(self, me):
        sides = [self.side(me, self.plane[0]), self.side(me ^ 1, self.plane[0])]
        return jnp.stack([me & 1] + sides)


def unpack_kernel(where_ref, own_a, core_a, own_b, core_b, *refs):
    mine = pl.program_id(0) == where_ref[0]
    rows_a = jnp.where(mine, own_a[...], core_a[...]).astype(F32)
    rows_b = jnp.where(mine, own_b[...], core_b[...]).astype(F32)
    outs = refs[-5:]
    width = outs[3].shape[1]
    outs[3][...] = rows_a[:, :width]
    span = 128
    half = rows_b.shape[1] // 3
    rest = width + 3 * half
    outs[4][...] = rows_a[:, rest : rest + outs[4].shape[1]]
    for i in range(3):
        for p in range(half // span):
            at = (3 * p + i) * span
            here = slice(p * span, (p + 1) * span)
            outs[i][:, here] = rows_a[:, width + at : width + at + span]
            there = slice(half + p * span, half + (p + 1) * span)
            outs[i][:, there] = rows_b[:, at : at + span]


def unpack(where, own_a, core_a, own_b, core_b, late, earlier, width, n_experts):
    rows = own_a.shape[0]
    parts = 1
    size = rows // parts
    earlier = tuple(earlier)

    def place(c, r, where_ref):
        side = jnp.where(c == where_ref[0], where_ref[1], where_ref[2])
        return (2 * c + (1 - side if late else side)) * parts + r, 0

    piece = lambda value: pl.BlockSpec((size, value.shape[1]), lambda c, r, where_ref: (r, 0))
    return pl.pallas_call(
        unpack_kernel,
        grid_spec=pltpu.PrefetchScalarGridSpec(
            num_scalar_prefetch=1,
            grid=(2, parts),
            in_specs=[piece(value) for value in (own_a, core_a, own_b, core_b)]
            + [pl.BlockSpec(memory_space=pl.ANY)] * len(earlier),
            out_specs=[pl.BlockSpec((size, width), place)] * 4
            + [pl.BlockSpec((size, n_experts), place)],
        ),
        out_shape=[shape((width, width), F32)] * 4 + [shape((width, n_experts), F32)],
        input_output_aliases={5 + i: i for i in range(len(earlier))},
        compiler_params=params(),
        cost_estimate=cost(rows * width, 24 * rows * width),
        name="unpack",
    )(where, own_a, core_a, own_b, core_b, *earlier)


def tokens_kernel(grads_ref, wt_ref, tok_ref, gain_ref, dmid_ref, out_ref, gain_out, sum_s):
    step = pl.program_id(0)
    part = dot(grads_ref[...], wt_ref[...])

    @pl.when(step == 0)
    def _():
        sum_s[...] = part

    @pl.when(step > 0)
    def _():
        sum_s[...] += part

    @pl.when(step == pl.num_programs(0) - 1)
    def _():
        dnormed = sum_s[...]
        inputs = tok_ref[...].astype(F32)
        inv = norm_scale(inputs)
        scaled = dnormed * gain_ref[...]
        inner = jnp.mean(scaled * inputs, axis=1, keepdims=True)
        out_ref[...] = (
            dmid_ref[...] + inv * scaled - inputs * (inv * inv * inv) * inner
        ).astype(LOW)
        gain_out[...] = jnp.broadcast_to(
            jnp.sum(dnormed * inputs * inv, axis=0, keepdims=True), gain_out.shape
        )


def tokens_back(grads, weights_t, tokens, gain, dmid):
    n, width = tokens.shape
    steps = 3
    block = grads.shape[1] // steps
    whole = lambda *dims: pl.BlockSpec(dims, lambda p: (0,) * len(dims))
    return pl.pallas_call(
        tokens_kernel,
        grid=(steps,),
        in_specs=[
            pl.BlockSpec((n, block), lambda p: (0, p)),
            pl.BlockSpec((block, width), lambda p: (p, 0)),
            whole(n, width),
            whole(1, width),
            whole(n, width),
        ],
        out_specs=[whole(n, width), whole(8, width)],
        out_shape=[shape((n, width), LOW), shape((8, width), F32)],
        scratch_shapes=[pltpu.VMEM((n, width), F32)],
        compiler_params=params(),
        cost_estimate=cost(6 * n * width * width, 6 * width * width + 14 * n * width),
        name="tokens_back",
    )(grads, weights_t, tokens, gain.reshape(1, width), dmid)


def leave_kernel(res_ref, col_ref, mid_ref, out_ref):
    n = mid_ref.shape[0]
    slots = res_ref.shape[0]
    place = lax.broadcasted_iota(jnp.int32, (n, slots), 1) == col_ref[:, 64:65]
    out_ref[...] = (mid_ref[...] + dot(place.astype(F32).astype(LOW), res_ref[...])).astype(LOW)


def leave(res_rows, col, middle):
    n, width = middle.shape
    return pl.pallas_call(
        leave_kernel,
        out_shape=shape((n, width), LOW),
        compiler_params=params(),
        cost_estimate=cost(2 * n * width * res_rows.shape[0], 10 * n * width),
        name="leave",
    )(res_rows, col, middle)


def exchange(rows):
    return lax.all_to_all(rows, AXES, split_axis=0, concat_axis=0, tiled=True)


def sum_small(parts, n_dev):
    flat = jnp.concatenate([part.reshape(-1) for part in parts])
    size = flat.shape[0]
    lines = -(-size // 1024) * 8
    block = jnp.pad(flat, (0, lines * 128 - size)).reshape(1, lines, 128)
    sent = jnp.broadcast_to(block, (n_dev, lines, 128))
    total = jnp.sum(exchange(sent), axis=0).reshape(-1)
    found, start = [], 0
    for part in parts:
        found.append(total[start : start + part.size].reshape(part.shape))
        start += part.size
    return found


def body(
    n_grp,
    n_loc,
    tokens,
    cotangent,
    w_query,
    w_key,
    w_value,
    w_output,
    attn_gain,
    bias_table,
    moe_gain,
    router_weight,
    router_bias,
    expert_in,
    expert_out,
    expert_ids,
    bucket_ids,
):
    n_rows, width = tokens.shape
    n_buckets, n_heads = bias_table.shape
    n_experts = router_weight.shape[1]
    most = max(2, 2 * n_rows // n_experts)
    slots = n_experts * most
    keep = 5 * n_rows // 4
    me = (lax.axis_index("grp") * lax.axis_size("loc") + lax.axis_index("loc")).reshape(1)

    dy_out, row, col = dispatch(expert_ids, cotangent, slots, most)
    dy_out, attn_gain, moe_gain, bias_table = tie(dy_out, attn_gain, moe_gain, bias_table)
    dy_rows = exchange(dy_out)

    table = jnp.pad(bias_table.T, ((0, 0), (0, 128 - n_buckets))).reshape(n_heads // 2, 2, 128)
    query, keys, values, weights, attended_t, normed_t, middle, x_low, x_high, weights_t = attend(
        tokens, attn_gain, table, bucket_ids, w_query, w_key, w_value, w_output, moe_gain, row,
        slots, n_heads,
    )
    dy_rows, x_low = tie(dy_rows, x_low)
    x_low = exchange(x_low)
    arrived = arrive(dy_rows, most, keep)
    x_low, x_high, *arrived = tie(x_low, x_high, *arrived)
    dy_low, dy_high, kept_low, kept_high = arrived
    x_high = exchange(x_high)
    model = (router_weight, router_bias, expert_in, expert_out)
    dn_low, res_low, *earlier = expert(me, x_low, dy_low, kept_low, *model)
    dn_low, x_high = tie(dn_low, x_high)
    dn_low = exchange(dn_low)
    from_high = expert(me, x_high, dy_high, kept_high, *model, earlier)
    dn_low, *from_high = tie(dn_low, *from_high)
    dn_high, res_high, hidden, dpre, dres, dlogits = from_high
    dn_high = exchange(dn_high)
    res_sent = jnp.concatenate(
        [value.reshape(n_experts, most // 2, width) for value in (res_low, res_high)], axis=1
    ).reshape(slots, width)
    grad_expert_in, grad_expert_out, routed, bias_rows = weights_back(
        x_low, x_high, hidden, dpre, dres, dlogits
    )
    grad_router_bias = bias_rows[0]
    ring = Ring(n_grp, n_loc)
    rank = me[0]
    where = ring.where(rank)
    dn_high, res_sent, grad_expert_in, grad_expert_out, routed, grad_router_bias, where = tie(
        dn_high, res_sent, grad_expert_in, grad_expert_out, routed, grad_router_bias, where
    )
    res_rows = exchange(res_sent)
    dmid, sent_a, kept_a, moe_gain_rows, grads, dscores, sent_b, kept_b = back(
        me & 1, dn_low, dn_high, col, middle, cotangent, moe_gain, w_output, attended_t, routed, query,
        keys, values, weights, normed_t, n_heads // 4,
    )

    def step(kept, got, shifts):
        kept, got = ring.cut(kept, rank, shifts), ring.cut(got, rank, shifts)
        return [add(left, right) for left, right in zip(kept, got)]

    got_a = ring.swap(sent_a, ring.core)
    sent_a, kept_a = step(kept_a, got_a, ring.plane[0])
    got_b = ring.swap(sent_b, ring.core)
    got_b, sent_a = tie(got_b, sent_a)
    got_a = ring.swap(sent_a, ring.plane[0])
    sent_b, kept_b = step(kept_b, got_b, ring.plane[0])
    sent_b, grads = tie(sent_b, grads)
    got_b = ring.swap(sent_b, ring.plane[0])
    grad_tokens, attn_gain_rows = tokens_back(grads, weights_t, tokens, attn_gain, dmid)
    got_a, got_b, grad_tokens, attn_gain_rows, res_rows = tie(
        got_a, got_b, grad_tokens, attn_gain_rows, res_rows
    )
    for shifts in ring.plane[1:] + [ring.near]:
        sent_a, kept_a = step(kept_a, got_a, shifts)
        sent_b, kept_b = step(kept_b, got_b, shifts)
        got_a, got_b = ring.swap(sent_a, shifts), ring.swap(sent_b, shifts)
    value_a, value_b = add(kept_a, got_a), add(kept_b, got_b)
    value_a, value_b, dscores = tie(value_a, value_b, dscores)
    got_a, got_b = ring.swap(value_a, ring.far), ring.swap(value_b, ring.far)
    grad_table = table_back(dscores, bucket_ids, n_buckets)
    got_a, got_b, grad_table = tie(got_a, got_b, grad_table)
    value_a, value_b = add(value_a, got_a), add(value_b, got_b)
    for place, shifts in enumerate(reversed(ring.plane[1:] + [ring.near])):
        if place == 0:
            value_a, value_b, res_rows = tie(value_a, value_b, res_rows)
        if place == 1:
            value_a, value_b, grad_table = tie(value_a, value_b, grad_table)
        got_a, got_b = ring.swap(value_a, shifts), ring.swap(value_b, shifts)
        if place == 0:
            layer_out = leave(res_rows, col, middle)
            got_a, got_b, layer_out = tie(got_a, got_b, layer_out)
        if place == 1:
            smalls = sum_small(
                (attn_gain_rows[0], grad_table, moe_gain_rows[0], grad_router_bias), n_grp * n_loc
            )
        value_a = ring.join(value_a, got_a, rank, shifts)
        value_b = ring.join(value_b, got_b, rank, shifts)
    near_a, near_b = ring.swap(value_a, ring.plane[0]), ring.swap(value_b, ring.plane[0])
    core_a, core_b = ring.swap(value_a, ring.core), ring.swap(value_b, ring.core)
    outs = unpack(where, value_a, core_a, value_b, core_b, False, (), width, n_experts)
    near_a, near_b, *rest = tie(near_a, near_b, *outs, *smalls)
    outs, smalls = rest[:5], rest[5:]
    far_a, far_b = ring.swap(near_a, ring.core), ring.swap(near_b, ring.core)
    outs = unpack(where, near_a, far_a, near_b, far_b, True, outs, width, n_experts)
    grad_query, grad_key, grad_value, grad_output, grad_router = outs
    grad_attn_gain, grad_table, grad_moe_gain, grad_router_bias = smalls
    return (
        layer_out,
        grad_tokens,
        grad_query,
        grad_key,
        grad_value,
        grad_output,
        grad_attn_gain,
        grad_table.T,
        grad_moe_gain,
        grad_router,
        grad_router_bias,
        grad_expert_in[None],
        grad_expert_out[None],
    )


def solution(mesh):
    rows, flat = P(AXES, None), P(AXES, None, None)
    return jax.shard_map(
        functools.partial(body, mesh.shape["grp"], mesh.shape["loc"]),
        mesh=mesh,
        in_specs=(
            rows, rows, P(), P(), P(), P(), P(), P(), P(), P(), P(), flat, flat, rows, P(),
        ),
        out_specs=(
            rows, rows, P(), P(), P(), P(), P(), P(), P(), P(), P(), flat, flat,
        ),
        check_vma=False,
    )
```

```python
import functools

import jax
import jax.numpy as jnp
from jax import lax
from jax.experimental import pallas as pl
from jax.experimental.pallas import tpu as pltpu
from jax.sharding import PartitionSpec as P

AXES = ("grp", "loc")
LOW = jnp.bfloat16
F32 = jnp.float32
NN = (((1,), (0,)), ((), ()))
NT = (((1,), (1,)), ((), ()))
TN = (((0,), (0,)), ((), ()))
VMEM_BYTES = 56 * 1024 * 1024
EMPTY = 2.0**20


def dot(left, right, dims=NN):
    return lax.dot_general(left, right, dims, preferred_element_type=F32)


def split(values):
    high = values.astype(LOW)
    rest = values - high.astype(F32)
    middle = rest.astype(LOW)
    return high, middle, (rest - middle.astype(F32)).astype(LOW)


def params():
    return pltpu.CompilerParams(vmem_limit_bytes=VMEM_BYTES)


def cost(flops, nbytes, trans=0):
    return pl.CostEstimate(flops=int(flops), bytes_accessed=int(nbytes), transcendentals=int(trans))


def shape(dims, dtype):
    return jax.ShapeDtypeStruct(dims, dtype)


def norm_scale(values):
    return lax.rsqrt(jnp.mean(values * values, axis=-1, keepdims=True) + 1e-06)


def dispatch_kernel(ids_ref, dy_ref, out_ref, row_ref, col_ref, *, most):
    n = ids_ref.shape[1]
    slots = out_ref.shape[0]
    sub = lax.broadcasted_iota(jnp.int32, (n, n), 0)
    lane = lax.broadcasted_iota(jnp.int32, (n, n), 1)
    ids_row = ids_ref[...]
    ids_col = jnp.sum(jnp.where(sub == lane, ids_row, 0), axis=1, keepdims=True)
    same = ids_col == ids_row
    rank_row = jnp.sum(jnp.where(same & (sub < lane), 1, 0), axis=0, keepdims=True)
    rank_col = jnp.sum(jnp.where(same & (lane < sub), 1, 0), axis=1, keepdims=True)
    half = most // 2

    def halves(ids, rank):
        low = jnp.where(rank < half, ids * half + rank, -1)
        return low, jnp.where(rank < half, -1, ids * half + rank - half)

    low, high = halves(ids_row, rank_row)
    upper = lax.broadcasted_iota(jnp.int32, row_ref.shape, 0) < 4
    row_ref[...] = jnp.where(upper, low, high)
    low, high = halves(ids_col, rank_col)
    spot = lax.broadcasted_iota(jnp.int32, col_ref.shape, 1)
    full = ids_col * most + rank_col
    col_ref[...] = jnp.where(spot < 32, low, jnp.where(spot < 64, high, full))
    place = lax.broadcasted_iota(jnp.int32, (slots, n), 0) == ids_row * most + rank_row
    hot = place.astype(F32)
    filled = jnp.sum(hot, axis=1, keepdims=True)
    rows = dot(hot.astype(LOW), dy_ref[...])
    out_ref[...] = jnp.where(filled > 0.0, rows, EMPTY).astype(LOW)


def dispatch(ids, dy, slots, most):
    n, width = dy.shape
    return pl.pallas_call(
        functools.partial(dispatch_kernel, most=most),
        out_shape=(
            shape((slots, width), LOW),
            shape((8, n), jnp.int32),
            shape((n, 128), jnp.int32),
        ),
        compiler_params=params(),
        cost_estimate=cost(2 * slots * n * width, 4 * slots * width),
        name="dispatch",
    )(ids.reshape(1, n), dy)


def attend_kernel(
    tok_ref,
    gain_ref,
    tab_ref,
    bucket_ref,
    wq_ref,
    wk_ref,
    wv_ref,
    wo_ref,
    moe_gain_ref,
    row_ref,
    q_ref,
    k_ref,
    v_ref,
    w_ref,
    att_t_ref,
    normed_t_ref,
    mid_ref,
    low_ref,
    high_ref,
    wt_ref,
    att_s,
    normed_s,
    *,
    scaling,
):
    step = pl.program_id(0)
    pairs = pl.num_programs(0)
    n = tok_ref.shape[0]

    @pl.when(step == 0)
    def _():
        inputs = tok_ref[...].astype(F32)
        normed_one = (inputs * norm_scale(inputs) * gain_ref[...]).astype(LOW)
        normed_s[...] = normed_one
        normed_t_ref[...] = normed_one.T

    normed = normed_s[...]
    query = dot(normed, wq_ref[...]).astype(LOW)
    keys = dot(normed, wk_ref[...]).astype(LOW)
    values = dot(normed, wv_ref[...]).astype(LOW)
    q_ref[...] = query
    k_ref[...] = keys
    v_ref[...] = values
    span = query.shape[1]
    for i, ref in enumerate((wq_ref, wk_ref, wv_ref)):
        wt_ref[i * span : (i + 1) * span, :] = ref[...].T
    low_half = lax.broadcasted_iota(jnp.int32, query.shape, 1) < query.shape[1] // 2
    zero = jnp.zeros_like(query)
    total = jnp.zeros((n, query.shape[1]), F32)
    for h in range(2):
        mine = low_half if h == 0 else ~low_half
        scores = dot(jnp.where(mine, query, zero), keys, NT) * scaling
        table = jnp.broadcast_to(tab_ref[step, pl.ds(h, 1), :], (n, 128))
        bias = [
            jnp.take_along_axis(
                table, bucket_ref[:, c * 128 : (c + 1) * 128], axis=1, mode="promise_in_bounds"
            )
            for c in range(n // 128)
        ]
        scores = scores + jnp.concatenate(bias, axis=1)
        top = jnp.max(scores, axis=1, keepdims=True)
        grown = jnp.exp(scores - top)
        weights = (grown * (1.0 / jnp.sum(grown, axis=1, keepdims=True))).astype(LOW)
        w_ref[h] = weights
        total = total + dot(weights, jnp.where(mine, values, zero))
    att_s[step] = total.astype(LOW)

    @pl.when(step == pairs - 1)
    def _():
        attended = jnp.concatenate([att_s[i] for i in range(att_s.shape[0])], axis=1)
        att_t_ref[...] = attended.T
        middle = tok_ref[...].astype(F32) + dot(attended, wo_ref[...])
        mid_ref[...] = middle
        normed_two = (middle * norm_scale(middle) * moe_gain_ref[...]).astype(LOW)
        for ref, row in ((low_ref, 0), (high_ref, 4)):
            slot = lax.broadcasted_iota(jnp.int32, (ref.shape[0], n), 0)
            place = slot == row_ref[row : row + 1, :]
            ref[...] = dot(place.astype(F32).astype(LOW), normed_two).astype(LOW)


def attend(tokens, gain, table, buckets, wq, wk, wv, wo, moe_gain, row, slots, n_heads):
    n, width = tokens.shape
    pairs = n_heads // 2
    span = width // pairs
    whole = lambda *dims: pl.BlockSpec(dims, lambda p: (0,) * len(dims))
    cols = lambda rows: pl.BlockSpec((rows, span), lambda p: (0, p))
    return pl.pallas_call(
        functools.partial(attend_kernel, scaling=(width // n_heads) ** -0.5),
        grid=(pairs,),
        in_specs=[
            whole(n, width),
            whole(1, width),
            whole(*table.shape),
            whole(n, n),
            cols(width),
            cols(width),
            cols(width),
            whole(width, width),
            whole(1, width),
            whole(8, n),
        ],
        out_specs=[
            cols(n),
            cols(n),
            cols(n),
            pl.BlockSpec((2, n, n), lambda p: (p, 0, 0)),
            whole(width, n),
            whole(width, n),
            whole(n, width),
            whole(slots // 2, width),
            whole(slots // 2, width),
            pl.BlockSpec((3 * span, width), lambda p: (p, 0)),
        ],
        out_shape=[
            shape((n, width), LOW),
            shape((n, width), LOW),
            shape((n, width), LOW),
            shape((n_heads, n, n), LOW),
            shape((width, n), LOW),
            shape((width, n), LOW),
            shape((n, width), F32),
            shape((slots // 2, width), LOW),
            shape((slots // 2, width), LOW),
            shape((3 * width, width), LOW),
        ],
        scratch_shapes=[pltpu.VMEM((pairs, n, span), LOW), pltpu.VMEM((n, width), LOW)],
        compiler_params=params(),
        cost_estimate=cost(
            8 * n * width * width + 4 * n_heads * n * n * span + 2 * slots * n * width,
            2 * n_heads * n * n + 24 * n * width,
            n_heads * n * n,
        ),
        name="attend",
    )(
        tokens,
        gain.reshape(1, width),
        table,
        buckets,
        wq,
        wk,
        wv,
        wo,
        moe_gain.reshape(1, width),
        row,
    )


def arrive_kernel(dy_ref, low_ref, high_ref, low_kept, high_kept, *, most, keep):
    slots = dy_ref.shape[0]
    half = most // 2
    edge = dy_ref[:, 0:128]
    valid = jnp.where(edge.astype(F32) < EMPTY * 0.5, 1.0, 0.0).astype(LOW)
    sub = lax.broadcasted_iota(jnp.int32, (slots, slots), 0)
    lane = lax.broadcasted_iota(jnp.int32, (slots, slots), 1)
    before = jnp.where(lane < sub, 1.0, 0.0).astype(LOW)
    first = jnp.where(lax.broadcasted_iota(jnp.int32, (8, 128), 1) == 0, 1.0, 0.0).astype(LOW)
    valid_row = dot(first, valid, NT)
    slot_row = dot(valid_row.astype(LOW), before, NT)
    kept = ((valid_row > 0.5) & (slot_row < keep - 0.5))[0:1, :]
    sub = lax.broadcasted_iota(jnp.int32, (slots // 2, slots), 0)
    lane = lax.broadcasted_iota(jnp.int32, (slots // 2, slots), 1)
    here = sub // half * most + sub % half
    for at, ref, kept_ref in ((0, low_ref, low_kept), (half, high_ref, high_kept)):
        place = jnp.where((lane == here + at) & kept, 1.0, 0.0)
        kept_ref[...] = jnp.broadcast_to(jnp.sum(place, axis=1, keepdims=True), kept_ref.shape)
        ref[...] = dot(place.astype(LOW), dy_ref[...]).astype(LOW)


def arrive(dy_rows, most, keep):
    slots, width = dy_rows.shape
    return pl.pallas_call(
        functools.partial(arrive_kernel, most=most, keep=keep),
        out_shape=(
            shape((slots // 2, width), LOW),
            shape((slots // 2, width), LOW),
            shape((slots // 2, 128), F32),
            shape((slots // 2, 128), F32),
        ),
        compiler_params=params(),
        cost_estimate=cost(2 * slots * slots * width, 4 * slots * width),
        name="arrive",
    )(dy_rows)


def expert_kernel(
    me_ref, x_ref, dyc_ref, kept_ref, router_ref, rbias_ref, win_ref, wout_ref, *refs, n_in
):
    dn_ref, res_ref, hid_ref, dpre_ref, dres_ref, dlog_ref, sum_s, drow_s, prob_s = refs[n_in:]
    step = pl.program_id(0)

    def gate_of(probs):
        mine = lax.broadcasted_iota(jnp.int32, probs.shape, 1) == me_ref[0]
        return mine, jnp.sum(jnp.where(mine, probs, 0.0), axis=1, keepdims=True)

    @pl.when(step == 0)
    def _():
        rows = x_ref[...]
        high, middle, low = split(router_ref[...])
        logits = dot(rows, high) + (dot(rows, middle) + dot(rows, low)) + rbias_ref[...]
        grown = jnp.exp(logits - jnp.max(logits, axis=1, keepdims=True))
        probs = grown / jnp.sum(grown, axis=1, keepdims=True)
        prob_s[...] = probs
        dres_ref[...] = (gate_of(probs)[1] * dyc_ref[...].astype(F32)).astype(LOW)
        sum_s[...] = jnp.zeros_like(sum_s)
        drow_s[...] = jnp.zeros_like(drow_s)

    rows = x_ref[...]
    win = win_ref[...]
    wout = wout_ref[...]
    pre = dot(rows, win)
    rate = 0.7978845608028654
    square = pre * pre
    tanh = jnp.tanh(rate * pre * (1.0 + 0.044715 * square))
    half = 0.5 * (1.0 + tanh)
    hidden = (pre * half).astype(LOW)
    slope = half + (0.5 * rate) * pre * (1.0 - tanh * tanh) * (1.0 + 3 * 0.044715 * square)
    dhid = dot(dres_ref[...], wout, NT)
    dpre = (dhid * slope).astype(LOW)
    hid_ref[...] = hidden
    dpre_ref[...] = dpre
    sum_s[...] += dot(hidden, wout)
    drow_s[...] += dot(dpre, win, NT)

    @pl.when(step == pl.num_programs(0) - 1)
    def _():
        result = sum_s[...].astype(LOW).astype(F32)
        dgate = jnp.sum(dyc_ref[...].astype(F32) * result, axis=1, keepdims=True)
        probs = prob_s[...]
        mine, gate = gate_of(probs)
        dlogits = probs * (jnp.where(mine, dgate, 0.0) - gate * dgate)
        dlog_ref[...] = dlogits
        high, middle, _ = split(router_ref[...])
        dhigh, dmiddle, _ = split(dlogits)
        side = dot(dhigh, high, NT) + (dot(dhigh, middle, NT) + dot(dmiddle, high, NT))
        dn_ref[...] = (drow_s[...] + side).astype(LOW)
        res_ref[...] = (kept_ref[:, 0:1] * gate * result).astype(LOW)


def expert(me, rows, dyc, kept, router, rbias, expert_in, expert_out, earlier=()):
    n, width = rows.shape
    n_exp = router.shape[1]
    ff = expert_in.shape[2]
    block = 768 if ff % 768 == 0 else ff
    at = 1 if earlier else 0
    whole = lambda *dims: pl.BlockSpec(dims, lambda f: (0,) * len(dims))
    return pl.pallas_call(
        functools.partial(expert_kernel, n_in=len(earlier)),
        grid=(ff // block,),
        in_specs=[
            pl.BlockSpec(memory_space=pltpu.SMEM),
            whole(n, width),
            whole(n, width),
            whole(n, 128),
            whole(width, n_exp),
            whole(1, n_exp),
            pl.BlockSpec((None, width, block), lambda f: (0, 0, f)),
            pl.BlockSpec((None, block, width), lambda f: (0, f, 0)),
        ]
        + [pl.BlockSpec(memory_space=pl.ANY)] * len(earlier),
        out_specs=[
            whole(n, width),
            whole(n, width),
            pl.BlockSpec((n, block), lambda f: (at, f)),
            pl.BlockSpec((n, block), lambda f: (at, f)),
            pl.BlockSpec((n, width), lambda f: (at, 0)),
            pl.BlockSpec((n, n_exp), lambda f: (at, 0)),
        ],
        out_shape=[
            shape((n, width), LOW),
            shape((n, width), LOW),
            shape((2 * n, ff), LOW),
            shape((2 * n, ff), LOW),
            shape((2 * n, width), LOW),
            shape((2 * n, n_exp), F32),
        ],
        scratch_shapes=[
            pltpu.VMEM((n, width), F32),
            pltpu.VMEM((n, width), F32),
            pltpu.VMEM((n, n_exp), F32),
        ],
        input_output_aliases={8 + i: 2 + i for i in range(len(earlier))},
        compiler_params=params(),
        cost_estimate=cost(8 * n * width * ff, 16 * width * ff, n * ff),
        name="expert",
    )(me, rows, dyc, kept, router, rbias.reshape(1, n_exp), expert_in, expert_out, *earlier)


def weights_kernel(
    low_ref, high_ref, hid_ref, dpre_ref, dres_ref, dlog_ref, in_ref, out_ref, routed_ref, bias_ref,
    x_s,
):
    @pl.when(pl.program_id(0) == 0)
    def _():
        n = low_ref.shape[0]
        x_s[:, :n] = low_ref[...].T
        x_s[:, n:] = high_ref[...].T
        dlogits = dlog_ref[...]
        rows = x_s[...]
        high, middle, low = split(dlogits)
        routed = dot(rows, high) + (dot(rows, middle) + dot(rows, low))
        routed_ref[...] = jnp.zeros_like(routed_ref)
        routed_ref[:, : routed.shape[1]] = routed
        bias_ref[...] = jnp.broadcast_to(jnp.sum(dlogits, axis=0, keepdims=True), bias_ref.shape)

    in_ref[...] = dot(x_s[...], dpre_ref[...])
    out_ref[...] = dot(hid_ref[...].T, dres_ref[...])


def weights_back(x_low, x_high, hidden, dpre, dres, dlogits):
    n, width = x_low.shape
    ff = hidden.shape[1]
    n_exp = dlogits.shape[1]
    tail = -(-n_exp // 128) * 128
    block = 512 if ff % 512 == 0 else ff
    whole = lambda *dims: pl.BlockSpec(dims, lambda f: (0,) * len(dims))
    cols = lambda rows: pl.BlockSpec((rows, block), lambda f: (0, f))
    return pl.pallas_call(
        weights_kernel,
        grid=(ff // block,),
        in_specs=[
            whole(n, width),
            whole(n, width),
            cols(2 * n),
            cols(2 * n),
            whole(2 * n, width),
            whole(2 * n, n_exp),
        ],
        out_specs=[
            cols(width),
            pl.BlockSpec((block, width), lambda f: (f, 0)),
            whole(width, tail),
            whole(8, n_exp),
        ],
        out_shape=[
            shape((width, ff), F32),
            shape((ff, width), F32),
            shape((width, tail), F32),
            shape((8, n_exp), F32),
        ],
        scratch_shapes=[pltpu.VMEM((width, 2 * n), LOW)],
        compiler_params=params(),
        cost_estimate=cost(8 * n * width * ff, 8 * width * ff),
        name="weights_back",
    )(x_low, x_high, hidden, dpre, dres, dlogits)


def back_kernel(
    core_ref,
    low_hbm,
    high_hbm,
    col_hbm,
    mid_hbm,
    dy_hbm,
    wo_hbm,
    attended_hbm,
    routed_hbm,
    normed_hbm,
    gain_ref,
    q_ref,
    k_ref,
    v_ref,
    w_ref,
    dmid_hbm,
    sent_hbm,
    kept_hbm,
    gain_out,
    grads_ref,
    ds_ref,
    sent_b,
    kept_b,
    datt_s,
    low_ref,
    high_ref,
    col_ref,
    mid_ref,
    dy_ref,
    wo_ref,
    attended_ref,
    routed_ref,
    normed_ref,
    dmid_ref,
    sent_a,
    kept_a,
    sems,
    *,
    scaling,
):
    step = pl.program_id(0)
    n, span = q_ref.shape
    width = mid_ref.shape[1]
    part = width // 2
    half = span // 2
    tail = routed_ref.shape[1]
    lead = sent_a.shape[1] - tail - width
    lead_pairs = lead // (3 * span)
    sides = [
        pl.ds(pl.multiple_of(core * part, 128), part) for core in (1 - core_ref[0], core_ref[0])
    ]
    ins = [
        (low_hbm, low_ref),
        (high_hbm, high_ref),
        (col_hbm, col_ref),
        (mid_hbm, mid_ref),
        (dy_hbm, dy_ref),
        (wo_hbm, wo_ref),
        (attended_hbm, attended_ref),
        (routed_hbm, routed_ref),
        (normed_hbm, normed_ref),
    ]
    outs = [(dmid_ref, dmid_hbm), (sent_a, sent_hbm), (kept_a, kept_hbm)]
    copies = [
        pltpu.make_async_copy(source, target, sems.at[at])
        for at, (source, target) in enumerate(ins + outs)
    ]
    from_low, from_high, from_col, from_mid, from_dy, from_wo, from_att, from_routed = copies[:8]
    from_normed, to_dmid, to_sent, to_kept = copies[8:]

    @pl.when(step == 0)
    def _():
        for copy in copies[:9]:
            copy.start()
        dnormed = jnp.zeros((n, width), F32)
        from_col.wait()
        for copy, ref, at in ((from_low, low_ref, 0), (from_high, high_ref, 32)):
            place = lax.broadcasted_iota(jnp.int32, (n, ref.shape[0]), 1) == col_ref[:, at : at + 1]
            copy.wait()
            dnormed = dnormed + dot(place.astype(F32).astype(LOW), ref[...])
        from_mid.wait()
        from_dy.wait()
        middle = mid_ref[...]
        inv = norm_scale(middle)
        scaled = dnormed * gain_ref[...]
        inner = jnp.mean(scaled * middle, axis=1, keepdims=True)
        dmid = dy_ref[...].astype(F32) + inv * scaled - middle * (inv * inv * inv) * inner
        dmid_ref[...] = dmid
        to_dmid.start()
        branch = dmid.astype(LOW)
        from_wo.wait()
        datt = dot(branch, wo_ref[...], NT).astype(LOW)
        for p in range(datt_s.shape[0]):
            datt_s[p] = datt[:, p * span : (p + 1) * span]
        gain_out[...] = jnp.broadcast_to(
            jnp.sum(dnormed * middle * inv, axis=0, keepdims=True), gain_out.shape
        )
        from_att.wait()
        from_routed.wait()
        for ref, rows in zip((sent_a, kept_a), sides):
            ref[:, :width] = dot(attended_ref[rows, :], branch).astype(LOW)
            ref[:, width + lead :] = routed_ref[rows, :].astype(LOW)
        from_normed.wait()

    @pl.when(step > 0)
    def _():
        pair = step - 1
        query, keys, values, grad = q_ref[...], k_ref[...], v_ref[...], datt_s[pair]
        low_half = lax.broadcasted_iota(jnp.int32, query.shape, 1) < half
        low_rows = lax.broadcasted_iota(jnp.int32, (span, n), 0) < half

        def stack(value):
            zero = jnp.zeros_like(value)
            return jnp.concatenate(
                [jnp.where(low_half, value, zero), jnp.where(low_half, zero, value)], axis=0
            )

        def spread(value):
            value = value.astype(F32).T.astype(LOW)
            zero = jnp.zeros_like(value)
            return jnp.concatenate(
                [jnp.where(low_rows, value, zero), jnp.where(low_rows, zero, value)], axis=1
            )

        weights_low = jnp.concatenate([w_ref[0], w_ref[1]], axis=0)
        weights = weights_low.astype(F32)
        both = weights * dot(stack(grad), values, NT)
        dscores = (both - weights * jnp.sum(both, axis=1, keepdims=True)).astype(LOW)
        ds_ref[0] = dscores[:n]
        ds_ref[1] = dscores[n:]
        dquery = dot(jnp.concatenate([dscores[:n], dscores[n:]], axis=1), stack(keys))
        dvalues = dot(spread(grad), weights_low)
        dkeys = dot(spread(query), dscores)
        grads = jnp.concatenate([dquery * scaling, dkeys.T * scaling, dvalues.T], axis=1)
        grads = grads.astype(LOW)
        grads_ref[...] = grads
        products = [dot(normed_ref[rows, :], grads).astype(LOW) for rows in sides]

        @pl.when(pair < lead_pairs)
        def _():
            at = pl.multiple_of(width + pair * (3 * span), 128)
            for ref, product in zip((sent_a, kept_a), products):
                ref[:, pl.ds(at, 3 * span)] = product

        @pl.when(pair >= lead_pairs)
        def _():
            for ref, product in zip((sent_b, kept_b), products):
                ref[...] = product

    @pl.when(step == lead_pairs)
    def _():
        to_sent.start()
        to_kept.start()

    @pl.when(step == pl.num_programs(0) - 1)
    def _():
        to_dmid.wait()
        to_sent.wait()
        to_kept.wait()


def back(
    core, low, high, col, middle, dy, moe_gain, wo, attended_t, routed, query, keys, values, weights,
    normed_t, lead_pairs,
):
    n_heads, n, _ = weights.shape
    width = low.shape[1]
    pairs = n_heads // 2
    span = width // pairs
    part = width // 2
    columns_a = width + 3 * span * lead_pairs + routed.shape[1]
    columns_b = 3 * span * (pairs - lead_pairs)
    pair = lambda p: jnp.maximum(p - 1, 0)
    late = lambda p: jnp.maximum(p - 1 - lead_pairs, 0)
    cols = lambda size: pl.BlockSpec((n, size), lambda p: (0, pair(p)))
    square = pl.BlockSpec((2, n, n), lambda p: (pair(p), 0, 0))
    piece = pl.BlockSpec((part, 3 * span), lambda p: (0, late(p)))
    anywhere = pl.BlockSpec(memory_space=pl.ANY)
    loaded = (low, high, col, middle, dy, wo, attended_t, routed, normed_t)
    return pl.pallas_call(
        functools.partial(back_kernel, scaling=(width // n_heads) ** -0.5),
        grid=(1 + pairs,),
        in_specs=[pl.BlockSpec(memory_space=pltpu.SMEM)]
        + [anywhere] * len(loaded)
        + [pl.BlockSpec((1, width), lambda p: (0, 0)), cols(span), cols(span), cols(span), square],
        out_specs=[anywhere] * 3
        + [pl.BlockSpec((8, width), lambda p: (0, 0)), cols(3 * span), square, piece, piece],
        out_shape=[
            shape((n, width), F32),
            shape((part, columns_a), LOW),
            shape((part, columns_a), LOW),
            shape((8, width), F32),
            shape((n, 3 * width), LOW),
            shape((n_heads, n, n), LOW),
            shape((part, columns_b), LOW),
            shape((part, columns_b), LOW),
        ],
        scratch_shapes=[pltpu.VMEM((pairs, n, span), LOW)]
        + [pltpu.VMEM(value.shape, value.dtype) for value in loaded]
        + [
            pltpu.VMEM((n, width), F32),
            pltpu.VMEM((part, columns_a), LOW),
            pltpu.VMEM((part, columns_a), LOW),
            pltpu.SemaphoreType.DMA((len(loaded) + 3,)),
        ],
        compiler_params=params(),
        cost_estimate=cost(1000, 1000),
        name="back",
    )(core, *loaded, moe_gain.reshape(1, width), query, keys, values, weights)


def table_kernel(ds_ref, bucket_ref, out_ref, sum_s, *, n_buckets):
    step = pl.program_id(0)
    n_heads, rows, n = ds_ref.shape
    band = 16

    @pl.when(step == 0)
    def _():
        sum_s[...] = jnp.zeros_like(sum_s)

    total = sum_s[...]
    for r in range(rows // band):
        span = slice(r * band, (r + 1) * band)
        grads = ds_ref[:, span, :].reshape(n_heads * band, n)
        buckets = bucket_ref[span, :]
        hot = jnp.concatenate(
            [jnp.where(buckets == b, 1.0, 0.0).astype(LOW) for b in range(n_buckets)], axis=0
        )
        total = total + dot(hot, grads, NT)
    sum_s[...] = total

    @pl.when(step == pl.num_programs(0) - 1)
    def _():
        left = lax.broadcasted_iota(jnp.int32, total.shape, 0) % band
        right = lax.broadcasted_iota(jnp.int32, total.shape, 1) % band
        own = jnp.where(left == right, total, 0.0).T
        own = jnp.sum(own.reshape(n_heads, band, n_buckets * band), axis=1)
        bucket = lax.broadcasted_iota(jnp.int32, (n_buckets * band, n_buckets), 1)
        column = lax.broadcasted_iota(jnp.int32, (n_buckets * band, n_buckets), 0)
        fold = jnp.where(column // band == bucket, 1.0, 0.0).astype(LOW)
        high, middle, low = split(own)
        out_ref[...] = dot(high, fold) + dot(middle, fold) + dot(low, fold)


def table_back(dscores, buckets, n_buckets):
    n_heads, n, _ = dscores.shape
    rows, band = 64, 16
    dims = (n_buckets * band, n_heads * band)
    return pl.pallas_call(
        functools.partial(table_kernel, n_buckets=n_buckets),
        grid=(n // rows,),
        in_specs=[
            pl.BlockSpec((n_heads, rows, n), lambda r: (0, r, 0)),
            pl.BlockSpec((rows, n), lambda r: (r, 0)),
        ],
        out_specs=pl.BlockSpec((n_heads, n_buckets), lambda r: (0, 0)),
        out_shape=shape((n_heads, n_buckets), F32),
        scratch_shapes=[pltpu.VMEM(dims, F32)],
        compiler_params=params(),
        cost_estimate=cost(2 * dims[0] * dims[1] * n * n // band, 2 * n_heads * n * n),
        name="table_back",
    )(dscores, buckets)


def add(left, right):
    return (left.astype(F32) + right.astype(F32)).astype(LOW)


def tie(*values):
    return lax.optimization_barrier(values)


class Ring:
    def __init__(self, n_grp, n_loc):
        size = n_grp * n_loc
        bits = size.bit_length() - 1
        low = n_loc.bit_length() - 1
        self.size = size
        ys, xs = list(range(1, low)), list(range(low, bits - 2))
        first, second = (ys + xs, xs + ys) if len(ys) == len(xs) else (ys + xs, ys + xs)
        plane = list(zip(first, second))
        layers = [(bits - 2, bits - 2), (bits - 1, bits - 1)]
        self.core = (0, 0)
        self.order_a = plane + layers
        self.order_b = layers + plane

    def swap(self, value, shifts):
        pairs = [(i, i ^ (1 << shifts[i & 1])) for i in range(self.size)]
        return lax.ppermute(value, AXES, pairs)

    def side(self, me, shifts):
        shift = jnp.where(me & 1 == 0, shifts[0], shifts[1])
        return (me >> shift) & 1

    def cut(self, value, me, shifts):
        halves = value.reshape(2, value.shape[0] // 2, value.shape[1])
        side = self.side(me, shifts)
        return [lax.dynamic_index_in_dim(halves, at, 0, keepdims=False) for at in (1 - side, side)]

    def join(self, value, got, me, shifts):
        side = self.side(me, shifts)
        low = jnp.where(side == 0, value, got)
        high = jnp.where(side == 0, got, value)
        return jnp.concatenate([low, high], axis=0)

    def where(self, me):
        sides = [self.side(it, order[0]) for order in (self.order_a, self.order_b) for it in (me, me ^ 1)]
        return jnp.stack([me & 1] + sides)


def unpack_kernel(where_ref, own_a, core_a, own_b, core_b, *refs, late):
    *outs, routed_ref, rows_s, sems = refs[-7:]
    rows, width = rows_s.shape[2:]
    span = 128
    ahead = (own_a.shape[1] - width) // (3 * span)
    copies = []
    for core in range(2):
        mine = where_ref[0] == core
        rows_a = jnp.where(mine, own_a[...], core_a[...]).astype(F32)
        rows_b = jnp.where(mine, own_b[...], core_b[...]).astype(F32)
        side_a = jnp.where(mine, where_ref[1], where_ref[2])
        side_b = jnp.where(mine, where_ref[3], where_ref[4])
        at_a, at_b = (2 * core + (1 - side if late else side) for side in (side_a, side_b))
        rows_s[core, 3] = rows_a[:, :width]
        for i in range(3):
            for p in range(width // span):
                value, lead = (rows_a, width) if p < ahead else (rows_b, -3 * ahead * span)
                at = lead + (3 * p + i) * span
                rows_s[core, i, :, p * span : (p + 1) * span] = value[:, at : at + span]
        edge = ahead * span
        moves = [(i, at_a, 0, edge) for i in range(3)] + [(i, at_b, edge, width) for i in range(3)]
        for i, at, start, end in moves + [(3, at_a, 0, width)]:
            here = pl.ds(pl.multiple_of(at * rows, 8), rows)
            copy = pltpu.make_async_copy(
                rows_s.at[core, i, :, start:end],
                outs[i].at[here, start:end],
                sems.at[len(copies)],
            )
            copy.start()
            copies.append(copy)
        routed = rows_a[:, width + 3 * edge :].T[: routed_ref.shape[0], :]
        if core == 0:
            routed_ref[...] = refs[0][...] if late else jnp.zeros_like(routed_ref)
        for at in range(4):

            @pl.when(at_a == at)
            def _():
                routed_ref[:, at * rows : (at + 1) * rows] = routed

    for copy in copies:
        copy.wait()


def unpack(where, own_a, core_a, own_b, core_b, late, earlier, width, n_experts):
    rows = own_a.shape[0]
    inputs = (own_a, core_a, own_b, core_b) + tuple(earlier[4:])
    kept = tuple(earlier[:4])
    anywhere = pl.BlockSpec(memory_space=pl.ANY)
    vmem = pl.BlockSpec(memory_space=pltpu.VMEM)
    return pl.pallas_call(
        functools.partial(unpack_kernel, late=late),
        in_specs=[pl.BlockSpec(memory_space=pltpu.SMEM)]
        + [vmem] * len(inputs)
        + [anywhere] * len(kept),
        out_specs=[anywhere] * 4 + [vmem],
        out_shape=[shape((width, width), F32)] * 4 + [shape((n_experts, width), F32)],
        scratch_shapes=[
            pltpu.VMEM((2, 4, rows, width), F32),
            pltpu.SemaphoreType.DMA((14,)),
        ],
        input_output_aliases={6 + i: i for i in range(len(kept))},
        compiler_params=pltpu.CompilerParams(vmem_limit_bytes=24 * 1024 * 1024),
        cost_estimate=cost(rows * width, 24 * rows * width),
        name="unpack",
    )(where, *inputs, *kept)


def tokens_kernel(grads_ref, wt_ref, tok_ref, gain_ref, dmid_ref, out_ref, gain_out, sum_s):
    step = pl.program_id(0)
    part = dot(grads_ref[...], wt_ref[...])

    @pl.when(step == 0)
    def _():
        sum_s[...] = part

    @pl.when(step > 0)
    def _():
        sum_s[...] += part

    @pl.when(step == pl.num_programs(0) - 1)
    def _():
        dnormed = sum_s[...]
        inputs = tok_ref[...].astype(F32)
        inv = norm_scale(inputs)
        scaled = dnormed * gain_ref[...]
        inner = jnp.mean(scaled * inputs, axis=1, keepdims=True)
        out_ref[...] = (
            dmid_ref[...] + inv * scaled - inputs * (inv * inv * inv) * inner
        ).astype(LOW)
        gain_out[...] = jnp.broadcast_to(
            jnp.sum(dnormed * inputs * inv, axis=0, keepdims=True), gain_out.shape
        )


def tokens_back(grads, weights_t, tokens, gain, dmid):
    n, width = tokens.shape
    steps = 3
    block = grads.shape[1] // steps
    whole = lambda *dims: pl.BlockSpec(dims, lambda p: (0,) * len(dims))
    return pl.pallas_call(
        tokens_kernel,
        grid=(steps,),
        in_specs=[
            pl.BlockSpec((n, block), lambda p: (0, p)),
            pl.BlockSpec((block, width), lambda p: (p, 0)),
            whole(n, width),
            whole(1, width),
            whole(n, width),
        ],
        out_specs=[whole(n, width), whole(8, width)],
        out_shape=[shape((n, width), LOW), shape((8, width), F32)],
        scratch_shapes=[pltpu.VMEM((n, width), F32)],
        compiler_params=params(),
        cost_estimate=cost(6 * n * width * width, 6 * width * width + 14 * n * width),
        name="tokens_back",
    )(grads, weights_t, tokens, gain.reshape(1, width), dmid)


def leave_kernel(res_ref, col_ref, mid_ref, out_ref):
    n = mid_ref.shape[0]
    slots = res_ref.shape[0]
    place = lax.broadcasted_iota(jnp.int32, (n, slots), 1) == col_ref[:, 64:65]
    out_ref[...] = (mid_ref[...] + dot(place.astype(F32).astype(LOW), res_ref[...])).astype(LOW)


def leave(res_rows, col, middle):
    n, width = middle.shape
    return pl.pallas_call(
        leave_kernel,
        out_shape=shape((n, width), LOW),
        compiler_params=params(),
        cost_estimate=cost(2 * n * width * res_rows.shape[0], 10 * n * width),
        name="leave",
    )(res_rows, col, middle)


def exchange(rows):
    return lax.all_to_all(rows, AXES, split_axis=0, concat_axis=0, tiled=True)


def pack_small(parts):
    flat = jnp.concatenate([part.reshape(-1) for part in parts])
    lines = -(-flat.shape[0] // 1024) * 8
    return jnp.pad(flat, (0, lines * 128 - flat.shape[0])).reshape(lines, 128)


def unpack_small(packed, parts):
    flat, found, start = packed.reshape(-1), [], 0
    for part in parts:
        found.append(flat[start : start + part.size].reshape(part.shape))
        start += part.size
    return found


def body(
    n_grp,
    n_loc,
    tokens,
    cotangent,
    w_query,
    w_key,
    w_value,
    w_output,
    attn_gain,
    bias_table,
    moe_gain,
    router_weight,
    router_bias,
    expert_in,
    expert_out,
    expert_ids,
    bucket_ids,
):
    n_rows, width = tokens.shape
    n_buckets, n_heads = bias_table.shape
    n_experts = router_weight.shape[1]
    most = max(2, 2 * n_rows // n_experts)
    slots = n_experts * most
    keep = 5 * n_rows // 4
    me = (lax.axis_index("grp") * lax.axis_size("loc") + lax.axis_index("loc")).reshape(1)

    dy_out, row, col = dispatch(expert_ids, cotangent, slots, most)
    dy_out, attn_gain, moe_gain, bias_table = tie(dy_out, attn_gain, moe_gain, bias_table)
    dy_rows = exchange(dy_out)

    table = jnp.pad(bias_table.T, ((0, 0), (0, 128 - n_buckets))).reshape(n_heads // 2, 2, 128)
    query, keys, values, weights, attended_t, normed_t, middle, x_low, x_high, weights_t = attend(
        tokens, attn_gain, table, bucket_ids, w_query, w_key, w_value, w_output, moe_gain, row,
        slots, n_heads,
    )
    dy_rows, x_low = tie(dy_rows, x_low)
    x_low = exchange(x_low)
    arrived = arrive(dy_rows, most, keep)
    x_low, x_high, *arrived = tie(x_low, x_high, *arrived)
    dy_low, dy_high, kept_low, kept_high = arrived
    x_high = exchange(x_high)
    model = (router_weight, router_bias, expert_in, expert_out)
    dn_low, res_low, *earlier = expert(me, x_low, dy_low, kept_low, *model)
    dn_low, x_high = tie(dn_low, x_high)
    dn_low = exchange(dn_low)
    from_high = expert(me, x_high, dy_high, kept_high, *model, earlier)
    dn_low, *from_high = tie(dn_low, *from_high)
    dn_high, res_high, hidden, dpre, dres, dlogits = from_high
    dn_high = exchange(dn_high)
    res_sent = jnp.concatenate(
        [value.reshape(n_experts, most // 2, width) for value in (res_low, res_high)], axis=1
    ).reshape(slots, width)
    grad_expert_in, grad_expert_out, routed, bias_rows = weights_back(
        x_low, x_high, hidden, dpre, dres, dlogits
    )
    grad_router_bias = bias_rows[0]
    ring = Ring(n_grp, n_loc)
    rank = me[0]
    where = ring.where(rank)
    dn_high, res_sent, grad_expert_in, grad_expert_out, routed, grad_router_bias, where = tie(
        dn_high, res_sent, grad_expert_in, grad_expert_out, routed, grad_router_bias, where
    )
    res_rows = exchange(res_sent)
    dmid, sent_a, kept_a, moe_gain_rows, grads, dscores, sent_b, kept_b = back(
        me & 1, dn_low, dn_high, col, middle, cotangent, moe_gain, w_output, attended_t, routed, query,
        keys, values, weights, normed_t, n_heads // 3,
    )

    def step(kept, got, shifts):
        sent = add(ring.cut(kept, rank, shifts)[0], ring.cut(got, rank, shifts)[0])
        sent, kept, got = tie(sent, kept, got)
        return sent, add(ring.cut(kept, rank, shifts)[1], ring.cut(got, rank, shifts)[1])

    order_a, order_b = ring.order_a, ring.order_b
    got_a = ring.swap(sent_a, ring.core)
    sent_a, kept_a = step(kept_a, got_a, order_a[0])
    got_b = ring.swap(sent_b, ring.core)
    got_b, sent_a = tie(got_b, sent_a)
    got_a = ring.swap(sent_a, order_a[0])
    sent_b, kept_b = step(kept_b, got_b, order_b[0])
    sent_b, grads, res_rows = tie(sent_b, grads, res_rows)
    got_b = ring.swap(sent_b, order_b[0])
    grad_tokens, attn_gain_rows = tokens_back(grads, weights_t, tokens, attn_gain, dmid)
    got_a, grad_tokens, attn_gain_rows = tie(got_a, grad_tokens, attn_gain_rows)
    count = len(order_a)
    for at in range(1, count - 1):
        sent_a, kept_a = step(kept_a, got_a, order_a[at])
        got_a = ring.swap(sent_a, order_a[at])
        got_a, got_b = tie(got_a, got_b)
        sent_b, kept_b = step(kept_b, got_b, order_b[at])
        got_b = ring.swap(sent_b, order_b[at])
    value_a, value_b = add(kept_a, got_a), add(kept_b, got_b)
    value_a, dscores = tie(value_a, dscores)
    got_a, got_b = ring.swap(value_a, order_a[-1]), ring.swap(value_b, order_b[-1])
    grad_table = table_back(dscores, bucket_ids, n_buckets)
    got_a, got_b, grad_table = tie(got_a, got_b, grad_table)
    value_a, value_b = add(value_a, got_a), add(value_b, got_b)
    small_parts = (attn_gain_rows[0], grad_table, moe_gain_rows[0], grad_router_bias)
    small = pack_small(small_parts)
    *plane, near, far = order_a
    early, middle_bits, late = [near], [plane[0], far], plane[1:] + [ring.core]

    def swaps(value, todo):
        for shifts in todo:
            value = value + ring.swap(value, shifts)
        return value

    for at in range(count - 2, 0, -1):
        first = at == count - 2
        if first:
            value_a, value_b, res_rows, small = tie(value_a, value_b, res_rows, small)
        got_a, got_b = ring.swap(value_a, order_a[at]), ring.swap(value_b, order_b[at])
        small = swaps(small, early if first else middle_bits if at == 1 else ())
        if first:
            layer_out = leave(res_rows, col, middle)
            got_a, got_b, small, layer_out = tie(got_a, got_b, small, layer_out)
        else:
            got_a, got_b, small = tie(got_a, got_b, small)
        value_a = ring.join(value_a, got_a, rank, order_a[at])
        value_b = ring.join(value_b, got_b, rank, order_b[at])
    near_a, near_b = ring.swap(value_a, order_a[0]), ring.swap(value_b, order_b[0])
    core_a, core_b = ring.swap(value_a, ring.core), ring.swap(value_b, ring.core)
    outs = unpack(where, value_a, core_a, value_b, core_b, False, (), width, n_experts)
    small, *outs = tie(small, *outs)
    small = swaps(small, late)
    near_a, near_b, small, *outs = tie(near_a, near_b, small, *outs)
    far_a, far_b = ring.swap(near_a, ring.core), ring.swap(near_b, ring.core)
    smalls = unpack_small(small, small_parts)
    outs = unpack(where, near_a, far_a, near_b, far_b, True, outs, width, n_experts)
    grad_query, grad_key, grad_value, grad_output, grad_router = outs
    grad_attn_gain, grad_table, grad_moe_gain, grad_router_bias = smalls
    return (
        layer_out,
        grad_tokens,
        grad_query,
        grad_key,
        grad_value,
        grad_output,
        grad_attn_gain,
        grad_table.T,
        grad_moe_gain,
        grad_router.T,
        grad_router_bias,
        grad_expert_in[None],
        grad_expert_out[None],
    )


def solution(mesh):
    rows, flat = P(AXES, None), P(AXES, None, None)
    return jax.shard_map(
        functools.partial(body, mesh.shape["grp"], mesh.shape["loc"]),
        mesh=mesh,
        in_specs=(
            rows, rows, P(), P(), P(), P(), P(), P(), P(), P(), P(), flat, flat, rows, P(),
        ),
        out_specs=(
            rows, rows, P(), P(), P(), P(), P(), P(), P(), P(), P(), flat, flat,
        ),
        check_vma=False,
    )
```

```python
import functools

import jax
import jax.numpy as jnp
from jax import lax
from jax.experimental import pallas as pl
from jax.experimental.pallas import tpu as pltpu
from jax.sharding import PartitionSpec as P

AXES = ("grp", "loc")
LOW = jnp.bfloat16
F32 = jnp.float32
NN = (((1,), (0,)), ((), ()))
NT = (((1,), (1,)), ((), ()))
TN = (((0,), (0,)), ((), ()))
VMEM_BYTES = 56 * 1024 * 1024
EMPTY = 2.0**20


def dot(left, right, dims=NN):
    return lax.dot_general(left, right, dims, preferred_element_type=F32)


def split(values):
    high = values.astype(LOW)
    rest = values - high.astype(F32)
    middle = rest.astype(LOW)
    return high, middle, (rest - middle.astype(F32)).astype(LOW)


def params():
    return pltpu.CompilerParams(vmem_limit_bytes=VMEM_BYTES)


def cost(flops, nbytes, trans=0):
    return pl.CostEstimate(flops=int(flops), bytes_accessed=int(nbytes), transcendentals=int(trans))


def shape(dims, dtype):
    return jax.ShapeDtypeStruct(dims, dtype)


def norm_scale(values):
    return lax.rsqrt(jnp.mean(values * values, axis=-1, keepdims=True) + 1e-06)


def dispatch_kernel(ids_ref, dy_ref, out_ref, row_ref, col_ref, *, most):
    n = ids_ref.shape[1]
    slots = out_ref.shape[0]
    sub = lax.broadcasted_iota(jnp.int32, (n, n), 0)
    lane = lax.broadcasted_iota(jnp.int32, (n, n), 1)
    ids_row = ids_ref[...]
    ids_col = jnp.sum(jnp.where(sub == lane, ids_row, 0), axis=1, keepdims=True)
    same = ids_col == ids_row
    rank_row = jnp.sum(jnp.where(same & (sub < lane), 1, 0), axis=0, keepdims=True)
    rank_col = jnp.sum(jnp.where(same & (lane < sub), 1, 0), axis=1, keepdims=True)
    half = most // 2

    def halves(ids, rank):
        low = jnp.where(rank < half, ids * half + rank, -1)
        return low, jnp.where(rank < half, -1, ids * half + rank - half)

    low, high = halves(ids_row, rank_row)
    upper = lax.broadcasted_iota(jnp.int32, row_ref.shape, 0) < 4
    row_ref[...] = jnp.where(upper, low, high)
    low, high = halves(ids_col, rank_col)
    spot = lax.broadcasted_iota(jnp.int32, col_ref.shape, 1)
    full = ids_col * most + rank_col
    col_ref[...] = jnp.where(spot < 32, low, jnp.where(spot < 64, high, full))
    place = lax.broadcasted_iota(jnp.int32, (slots, n), 0) == ids_row * most + rank_row
    hot = place.astype(F32)
    filled = jnp.sum(hot, axis=1, keepdims=True)
    rows = dot(hot.astype(LOW), dy_ref[...])
    out_ref[...] = jnp.where(filled > 0.0, rows, EMPTY).astype(LOW)


def dispatch(ids, dy, slots, most):
    n, width = dy.shape
    return pl.pallas_call(
        functools.partial(dispatch_kernel, most=most),
        out_shape=(
            shape((slots, width), LOW),
            shape((8, n), jnp.int32),
            shape((n, 128), jnp.int32),
        ),
        compiler_params=params(),
        cost_estimate=cost(2 * slots * n * width, 4 * slots * width),
        name="dispatch",
    )(ids.reshape(1, n), dy)


def attend_kernel(
    tok_ref,
    gain_ref,
    tab_ref,
    bucket_ref,
    wq_ref,
    wk_ref,
    wv_ref,
    wo_ref,
    moe_gain_ref,
    row_ref,
    q_ref,
    k_ref,
    v_ref,
    w_ref,
    att_t_ref,
    normed_t_ref,
    mid_ref,
    low_ref,
    high_ref,
    wt_ref,
    att_s,
    normed_s,
    *,
    scaling,
):
    step = pl.program_id(0)
    pairs = pl.num_programs(0)
    n = tok_ref.shape[0]

    @pl.when(step == 0)
    def _():
        inputs = tok_ref[...].astype(F32)
        normed_one = (inputs * norm_scale(inputs) * gain_ref[...]).astype(LOW)
        normed_s[...] = normed_one
        normed_t_ref[...] = normed_one.T

    normed = normed_s[...]
    query = dot(normed, wq_ref[...]).astype(LOW)
    keys = dot(normed, wk_ref[...]).astype(LOW)
    values = dot(normed, wv_ref[...]).astype(LOW)
    q_ref[...] = query
    k_ref[...] = keys
    v_ref[...] = values
    span = query.shape[1]
    for i, ref in enumerate((wq_ref, wk_ref, wv_ref)):
        wt_ref[i * span : (i + 1) * span, :] = ref[...].T
    low_half = lax.broadcasted_iota(jnp.int32, query.shape, 1) < query.shape[1] // 2
    zero = jnp.zeros_like(query)
    total = jnp.zeros((n, query.shape[1]), F32)
    for h in range(2):
        mine = low_half if h == 0 else ~low_half
        scores = dot(jnp.where(mine, query, zero), keys, NT) * scaling
        table = jnp.broadcast_to(tab_ref[step, pl.ds(h, 1), :], (n, 128))
        bias = [
            jnp.take_along_axis(
                table, bucket_ref[:, c * 128 : (c + 1) * 128], axis=1, mode="promise_in_bounds"
            )
            for c in range(n // 128)
        ]
        scores = scores + jnp.concatenate(bias, axis=1)
        top = jnp.max(scores, axis=1, keepdims=True)
        grown = jnp.exp(scores - top)
        weights = (grown * (1.0 / jnp.sum(grown, axis=1, keepdims=True))).astype(LOW)
        w_ref[h] = weights
        total = total + dot(weights, jnp.where(mine, values, zero))
    att_s[step] = total.astype(LOW)

    @pl.when(step == pairs - 1)
    def _():
        attended = jnp.concatenate([att_s[i] for i in range(att_s.shape[0])], axis=1)
        att_t_ref[...] = attended.T
        middle = tok_ref[...].astype(F32) + dot(attended, wo_ref[...])
        mid_ref[...] = middle
        normed_two = (middle * norm_scale(middle) * moe_gain_ref[...]).astype(LOW)
        for ref, row in ((low_ref, 0), (high_ref, 4)):
            slot = lax.broadcasted_iota(jnp.int32, (ref.shape[0], n), 0)
            place = slot == row_ref[row : row + 1, :]
            ref[...] = dot(place.astype(F32).astype(LOW), normed_two).astype(LOW)


def attend(tokens, gain, table, buckets, wq, wk, wv, wo, moe_gain, row, slots, n_heads):
    n, width = tokens.shape
    pairs = n_heads // 2
    span = width // pairs
    whole = lambda *dims: pl.BlockSpec(dims, lambda p: (0,) * len(dims))
    cols = lambda rows: pl.BlockSpec((rows, span), lambda p: (0, p))
    return pl.pallas_call(
        functools.partial(attend_kernel, scaling=(width // n_heads) ** -0.5),
        grid=(pairs,),
        in_specs=[
            whole(n, width),
            whole(1, width),
            whole(*table.shape),
            whole(n, n),
            cols(width),
            cols(width),
            cols(width),
            whole(width, width),
            whole(1, width),
            whole(8, n),
        ],
        out_specs=[
            cols(n),
            cols(n),
            cols(n),
            pl.BlockSpec((2, n, n), lambda p: (p, 0, 0)),
            whole(width, n),
            whole(width, n),
            whole(n, width),
            whole(slots // 2, width),
            whole(slots // 2, width),
            pl.BlockSpec((3 * span, width), lambda p: (p, 0)),
        ],
        out_shape=[
            shape((n, width), LOW),
            shape((n, width), LOW),
            shape((n, width), LOW),
            shape((n_heads, n, n), LOW),
            shape((width, n), LOW),
            shape((width, n), LOW),
            shape((n, width), F32),
            shape((slots // 2, width), LOW),
            shape((slots // 2, width), LOW),
            shape((3 * width, width), LOW),
        ],
        scratch_shapes=[pltpu.VMEM((pairs, n, span), LOW), pltpu.VMEM((n, width), LOW)],
        compiler_params=params(),
        cost_estimate=cost(
            8 * n * width * width + 4 * n_heads * n * n * span + 2 * slots * n * width,
            2 * n_heads * n * n + 24 * n * width,
            n_heads * n * n,
        ),
        name="attend",
    )(
        tokens,
        gain.reshape(1, width),
        table,
        buckets,
        wq,
        wk,
        wv,
        wo,
        moe_gain.reshape(1, width),
        row,
    )


def arrive_kernel(dy_ref, low_ref, high_ref, low_kept, high_kept, *, most, keep):
    slots = dy_ref.shape[0]
    half = most // 2
    edge = dy_ref[:, 0:128]
    valid = jnp.where(edge.astype(F32) < EMPTY * 0.5, 1.0, 0.0).astype(LOW)
    sub = lax.broadcasted_iota(jnp.int32, (slots, slots), 0)
    lane = lax.broadcasted_iota(jnp.int32, (slots, slots), 1)
    before = jnp.where(lane < sub, 1.0, 0.0).astype(LOW)
    first = jnp.where(lax.broadcasted_iota(jnp.int32, (8, 128), 1) == 0, 1.0, 0.0).astype(LOW)
    valid_row = dot(first, valid, NT)
    slot_row = dot(valid_row.astype(LOW), before, NT)
    kept = ((valid_row > 0.5) & (slot_row < keep - 0.5))[0:1, :]
    sub = lax.broadcasted_iota(jnp.int32, (slots // 2, slots), 0)
    lane = lax.broadcasted_iota(jnp.int32, (slots // 2, slots), 1)
    here = sub // half * most + sub % half
    for at, ref, kept_ref in ((0, low_ref, low_kept), (half, high_ref, high_kept)):
        place = jnp.where((lane == here + at) & kept, 1.0, 0.0)
        kept_ref[...] = jnp.broadcast_to(jnp.sum(place, axis=1, keepdims=True), kept_ref.shape)
        ref[...] = dot(place.astype(LOW), dy_ref[...]).astype(LOW)


def arrive(dy_rows, most, keep):
    slots, width = dy_rows.shape
    return pl.pallas_call(
        functools.partial(arrive_kernel, most=most, keep=keep),
        out_shape=(
            shape((slots // 2, width), LOW),
            shape((slots // 2, width), LOW),
            shape((slots // 2, 128), F32),
            shape((slots // 2, 128), F32),
        ),
        compiler_params=params(),
        cost_estimate=cost(2 * slots * slots * width, 4 * slots * width),
        name="arrive",
    )(dy_rows)


def expert_kernel(
    me_ref, x_ref, dyc_ref, kept_ref, router_ref, rbias_ref, win_ref, wout_ref, *refs, n_in
):
    dn_ref, res_ref, hid_ref, dpre_ref, dres_ref, dlog_ref, sum_s, drow_s, prob_s = refs[n_in:]
    step = pl.program_id(0)

    def gate_of(probs):
        mine = lax.broadcasted_iota(jnp.int32, probs.shape, 1) == me_ref[0]
        return mine, jnp.sum(jnp.where(mine, probs, 0.0), axis=1, keepdims=True)

    @pl.when(step == 0)
    def _():
        rows = x_ref[...]
        high, middle, low = split(router_ref[...])
        logits = dot(rows, high) + (dot(rows, middle) + dot(rows, low)) + rbias_ref[...]
        grown = jnp.exp(logits - jnp.max(logits, axis=1, keepdims=True))
        probs = grown / jnp.sum(grown, axis=1, keepdims=True)
        prob_s[...] = probs
        dres_ref[...] = (gate_of(probs)[1] * dyc_ref[...].astype(F32)).astype(LOW)
        sum_s[...] = jnp.zeros_like(sum_s)
        drow_s[...] = jnp.zeros_like(drow_s)

    rows = x_ref[...]
    win = win_ref[...]
    wout = wout_ref[...]
    pre = dot(rows, win)
    rate = 0.7978845608028654
    square = pre * pre
    tanh = jnp.tanh(rate * pre * (1.0 + 0.044715 * square))
    half = 0.5 * (1.0 + tanh)
    hidden = (pre * half).astype(LOW)
    slope = half + (0.5 * rate) * pre * (1.0 - tanh * tanh) * (1.0 + 3 * 0.044715 * square)
    dhid = dot(dres_ref[...], wout, NT)
    dpre = (dhid * slope).astype(LOW)
    hid_ref[...] = hidden
    dpre_ref[...] = dpre
    sum_s[...] += dot(hidden, wout)
    drow_s[...] += dot(dpre, win, NT)

    @pl.when(step == pl.num_programs(0) - 1)
    def _():
        result = sum_s[...].astype(LOW).astype(F32)
        dgate = jnp.sum(dyc_ref[...].astype(F32) * result, axis=1, keepdims=True)
        probs = prob_s[...]
        mine, gate = gate_of(probs)
        dlogits = probs * (jnp.where(mine, dgate, 0.0) - gate * dgate)
        dlog_ref[...] = dlogits
        high, middle, _ = split(router_ref[...])
        dhigh, dmiddle, _ = split(dlogits)
        side = dot(dhigh, high, NT) + (dot(dhigh, middle, NT) + dot(dmiddle, high, NT))
        dn_ref[...] = (drow_s[...] + side).astype(LOW)
        res_ref[...] = (kept_ref[:, 0:1] * gate * result).astype(LOW)


def expert(me, rows, dyc, kept, router, rbias, expert_in, expert_out, earlier=()):
    n, width = rows.shape
    n_exp = router.shape[1]
    ff = expert_in.shape[2]
    block = 768 if ff % 768 == 0 else ff
    at = 1 if earlier else 0
    whole = lambda *dims: pl.BlockSpec(dims, lambda f: (0,) * len(dims))
    return pl.pallas_call(
        functools.partial(expert_kernel, n_in=len(earlier)),
        grid=(ff // block,),
        in_specs=[
            pl.BlockSpec(memory_space=pltpu.SMEM),
            whole(n, width),
            whole(n, width),
            whole(n, 128),
            whole(width, n_exp),
            whole(1, n_exp),
            pl.BlockSpec((None, width, block), lambda f: (0, 0, f)),
            pl.BlockSpec((None, block, width), lambda f: (0, f, 0)),
        ]
        + [pl.BlockSpec(memory_space=pl.ANY)] * len(earlier),
        out_specs=[
            whole(n, width),
            whole(n, width),
            pl.BlockSpec((n, block), lambda f: (at, f)),
            pl.BlockSpec((n, block), lambda f: (at, f)),
            pl.BlockSpec((n, width), lambda f: (at, 0)),
            pl.BlockSpec((n, n_exp), lambda f: (at, 0)),
        ],
        out_shape=[
            shape((n, width), LOW),
            shape((n, width), LOW),
            shape((2 * n, ff), LOW),
            shape((2 * n, ff), LOW),
            shape((2 * n, width), LOW),
            shape((2 * n, n_exp), F32),
        ],
        scratch_shapes=[
            pltpu.VMEM((n, width), F32),
            pltpu.VMEM((n, width), F32),
            pltpu.VMEM((n, n_exp), F32),
        ],
        input_output_aliases={8 + i: 2 + i for i in range(len(earlier))},
        compiler_params=params(),
        cost_estimate=cost(8 * n * width * ff, 16 * width * ff, n * ff),
        name="expert",
    )(me, rows, dyc, kept, router, rbias.reshape(1, n_exp), expert_in, expert_out, *earlier)


def weights_kernel(
    low_ref, high_ref, hid_ref, dpre_ref, dres_ref, dlog_ref, in_ref, out_ref, routed_ref, bias_ref,
    x_s,
):
    @pl.when(pl.program_id(0) == 0)
    def _():
        n = low_ref.shape[0]
        x_s[:, :n] = low_ref[...].T
        x_s[:, n:] = high_ref[...].T
        dlogits = dlog_ref[...]
        rows = x_s[...]
        high, middle, low = split(dlogits)
        routed = dot(rows, high) + (dot(rows, middle) + dot(rows, low))
        routed_ref[...] = jnp.zeros_like(routed_ref)
        routed_ref[:, : routed.shape[1]] = routed
        bias_ref[...] = jnp.broadcast_to(jnp.sum(dlogits, axis=0, keepdims=True), bias_ref.shape)

    in_ref[...] = dot(x_s[...], dpre_ref[...])
    out_ref[...] = dot(hid_ref[...].T, dres_ref[...])


def weights_back(x_low, x_high, hidden, dpre, dres, dlogits):
    n, width = x_low.shape
    ff = hidden.shape[1]
    n_exp = dlogits.shape[1]
    tail = -(-n_exp // 128) * 128
    block = 512 if ff % 512 == 0 else ff
    whole = lambda *dims: pl.BlockSpec(dims, lambda f: (0,) * len(dims))
    cols = lambda rows: pl.BlockSpec((rows, block), lambda f: (0, f))
    return pl.pallas_call(
        weights_kernel,
        grid=(ff // block,),
        in_specs=[
            whole(n, width),
            whole(n, width),
            cols(2 * n),
            cols(2 * n),
            whole(2 * n, width),
            whole(2 * n, n_exp),
        ],
        out_specs=[
            cols(width),
            pl.BlockSpec((block, width), lambda f: (f, 0)),
            whole(width, tail),
            whole(8, n_exp),
        ],
        out_shape=[
            shape((width, ff), F32),
            shape((ff, width), F32),
            shape((width, tail), F32),
            shape((8, n_exp), F32),
        ],
        scratch_shapes=[pltpu.VMEM((width, 2 * n), LOW)],
        compiler_params=params(),
        cost_estimate=cost(8 * n * width * ff, 8 * width * ff),
        name="weights_back",
    )(x_low, x_high, hidden, dpre, dres, dlogits)


def back_kernel(
    core_ref,
    low_hbm,
    high_hbm,
    col_hbm,
    mid_hbm,
    dy_hbm,
    wo_hbm,
    attended_hbm,
    routed_hbm,
    normed_hbm,
    gain_ref,
    q_ref,
    k_ref,
    v_ref,
    w_ref,
    dmid_hbm,
    sent_hbm,
    kept_hbm,
    gain_out,
    grads_ref,
    ds_ref,
    sent_b,
    kept_b,
    datt_s,
    low_ref,
    high_ref,
    col_ref,
    mid_ref,
    dy_ref,
    wo_ref,
    attended_ref,
    routed_ref,
    normed_ref,
    dmid_ref,
    sent_a,
    kept_a,
    sems,
    *,
    scaling,
):
    step = pl.program_id(0)
    n, span = q_ref.shape
    width = mid_ref.shape[1]
    part = width // 2
    half = span // 2
    tail = routed_ref.shape[1]
    lead = sent_a.shape[1] - tail - width
    lead_pairs = lead // (3 * span)
    sides = [
        pl.ds(pl.multiple_of(core * part, 128), part) for core in (1 - core_ref[0], core_ref[0])
    ]
    ins = [
        (low_hbm, low_ref),
        (high_hbm, high_ref),
        (col_hbm, col_ref),
        (mid_hbm, mid_ref),
        (dy_hbm, dy_ref),
        (wo_hbm, wo_ref),
        (attended_hbm, attended_ref),
        (routed_hbm, routed_ref),
        (normed_hbm, normed_ref),
    ]
    outs = [(dmid_ref, dmid_hbm), (sent_a, sent_hbm), (kept_a, kept_hbm)]
    copies = [
        pltpu.make_async_copy(source, target, sems.at[at])
        for at, (source, target) in enumerate(ins + outs)
    ]
    from_low, from_high, from_col, from_mid, from_dy, from_wo, from_att, from_routed = copies[:8]
    from_normed, to_dmid, to_sent, to_kept = copies[8:]

    @pl.when(step == 0)
    def _():
        for copy in copies[:9]:
            copy.start()
        dnormed = jnp.zeros((n, width), F32)
        from_col.wait()
        for copy, ref, at in ((from_low, low_ref, 0), (from_high, high_ref, 32)):
            place = lax.broadcasted_iota(jnp.int32, (n, ref.shape[0]), 1) == col_ref[:, at : at + 1]
            copy.wait()
            dnormed = dnormed + dot(place.astype(F32).astype(LOW), ref[...])
        from_mid.wait()
        from_dy.wait()
        middle = mid_ref[...]
        inv = norm_scale(middle)
        scaled = dnormed * gain_ref[...]
        inner = jnp.mean(scaled * middle, axis=1, keepdims=True)
        dmid = dy_ref[...].astype(F32) + inv * scaled - middle * (inv * inv * inv) * inner
        dmid_ref[...] = dmid
        to_dmid.start()
        branch = dmid.astype(LOW)
        from_wo.wait()
        datt = dot(branch, wo_ref[...], NT).astype(LOW)
        for p in range(datt_s.shape[0]):
            datt_s[p] = datt[:, p * span : (p + 1) * span]
        gain_out[...] = jnp.broadcast_to(
            jnp.sum(dnormed * middle * inv, axis=0, keepdims=True), gain_out.shape
        )
        from_att.wait()
        from_routed.wait()
        for ref, rows in zip((sent_a, kept_a), sides):
            ref[:, :width] = dot(attended_ref[rows, :], branch).astype(LOW)
            ref[:, width + lead :] = routed_ref[rows, :].astype(LOW)
        from_normed.wait()

    @pl.when(step > 0)
    def _():
        pair = step - 1
        query, keys, values, grad = q_ref[...], k_ref[...], v_ref[...], datt_s[pair]
        low_half = lax.broadcasted_iota(jnp.int32, query.shape, 1) < half
        low_rows = lax.broadcasted_iota(jnp.int32, (span, n), 0) < half

        def stack(value):
            zero = jnp.zeros_like(value)
            return jnp.concatenate(
                [jnp.where(low_half, value, zero), jnp.where(low_half, zero, value)], axis=0
            )

        def spread(value):
            value = value.astype(F32).T.astype(LOW)
            zero = jnp.zeros_like(value)
            return jnp.concatenate(
                [jnp.where(low_rows, value, zero), jnp.where(low_rows, zero, value)], axis=1
            )

        weights_low = jnp.concatenate([w_ref[0], w_ref[1]], axis=0)
        weights = weights_low.astype(F32)
        both = weights * dot(stack(grad), values, NT)
        dscores = (both - weights * jnp.sum(both, axis=1, keepdims=True)).astype(LOW)
        ds_ref[0] = dscores[:n]
        ds_ref[1] = dscores[n:]
        dquery = dot(jnp.concatenate([dscores[:n], dscores[n:]], axis=1), stack(keys))
        dvalues = dot(spread(grad), weights_low)
        dkeys = dot(spread(query), dscores)
        grads = jnp.concatenate([dquery * scaling, dkeys.T * scaling, dvalues.T], axis=1)
        grads = grads.astype(LOW)
        grads_ref[...] = grads
        products = [dot(normed_ref[rows, :], grads).astype(LOW) for rows in sides]

        @pl.when(pair < lead_pairs)
        def _():
            at = pl.multiple_of(width + pair * (3 * span), 128)
            for ref, product in zip((sent_a, kept_a), products):
                ref[:, pl.ds(at, 3 * span)] = product

        @pl.when(pair >= lead_pairs)
        def _():
            for ref, product in zip((sent_b, kept_b), products):
                ref[...] = product

    @pl.when(step == lead_pairs)
    def _():
        to_sent.start()
        to_kept.start()

    @pl.when(step == pl.num_programs(0) - 1)
    def _():
        to_dmid.wait()
        to_sent.wait()
        to_kept.wait()


def back(
    core, low, high, col, middle, dy, moe_gain, wo, attended_t, routed, query, keys, values, weights,
    normed_t, lead_pairs,
):
    n_heads, n, _ = weights.shape
    width = low.shape[1]
    pairs = n_heads // 2
    span = width // pairs
    part = width // 2
    columns_a = width + 3 * span * lead_pairs + routed.shape[1]
    columns_b = 3 * span * (pairs - lead_pairs)
    pair = lambda p: jnp.maximum(p - 1, 0)
    late = lambda p: jnp.maximum(p - 1 - lead_pairs, 0)
    cols = lambda size: pl.BlockSpec((n, size), lambda p: (0, pair(p)))
    square = pl.BlockSpec((2, n, n), lambda p: (pair(p), 0, 0))
    piece = pl.BlockSpec((part, 3 * span), lambda p: (0, late(p)))
    anywhere = pl.BlockSpec(memory_space=pl.ANY)
    loaded = (low, high, col, middle, dy, wo, attended_t, routed, normed_t)
    return pl.pallas_call(
        functools.partial(back_kernel, scaling=(width // n_heads) ** -0.5),
        grid=(1 + pairs,),
        in_specs=[pl.BlockSpec(memory_space=pltpu.SMEM)]
        + [anywhere] * len(loaded)
        + [pl.BlockSpec((1, width), lambda p: (0, 0)), cols(span), cols(span), cols(span), square],
        out_specs=[anywhere] * 3
        + [pl.BlockSpec((8, width), lambda p: (0, 0)), cols(3 * span), square, piece, piece],
        out_shape=[
            shape((n, width), F32),
            shape((part, columns_a), LOW),
            shape((part, columns_a), LOW),
            shape((8, width), F32),
            shape((n, 3 * width), LOW),
            shape((n_heads, n, n), LOW),
            shape((part, columns_b), LOW),
            shape((part, columns_b), LOW),
        ],
        scratch_shapes=[pltpu.VMEM((pairs, n, span), LOW)]
        + [pltpu.VMEM(value.shape, value.dtype) for value in loaded]
        + [
            pltpu.VMEM((n, width), F32),
            pltpu.VMEM((part, columns_a), LOW),
            pltpu.VMEM((part, columns_a), LOW),
            pltpu.SemaphoreType.DMA((len(loaded) + 3,)),
        ],
        compiler_params=params(),
        cost_estimate=cost(1000, 1000),
        name="back",
    )(core, *loaded, moe_gain.reshape(1, width), query, keys, values, weights)


def table_kernel(ds_ref, bucket_ref, out_ref, sum_s, *, n_buckets):
    step = pl.program_id(0)
    n_heads, rows, n = ds_ref.shape
    band = 16

    @pl.when(step == 0)
    def _():
        sum_s[...] = jnp.zeros_like(sum_s)

    total = sum_s[...]
    for r in range(rows // band):
        span = slice(r * band, (r + 1) * band)
        grads = ds_ref[:, span, :].reshape(n_heads * band, n)
        buckets = bucket_ref[span, :]
        hot = jnp.concatenate(
            [jnp.where(buckets == b, 1.0, 0.0).astype(LOW) for b in range(n_buckets)], axis=0
        )
        total = total + dot(grads, hot, NT)
    sum_s[...] = total

    @pl.when(step == pl.num_programs(0) - 1)
    def _():
        left = lax.broadcasted_iota(jnp.int32, total.shape, 0) % band
        right = lax.broadcasted_iota(jnp.int32, total.shape, 1) % band
        own = jnp.where(left == right, total, 0.0)
        own = jnp.sum(own.reshape(n_heads, band, n_buckets * band), axis=1)
        bucket = lax.broadcasted_iota(jnp.int32, (n_buckets * band, n_buckets), 1)
        column = lax.broadcasted_iota(jnp.int32, (n_buckets * band, n_buckets), 0)
        fold = jnp.where(column // band == bucket, 1.0, 0.0).astype(LOW)
        high, middle, low = split(own)
        out_ref[...] = dot(high, fold) + dot(middle, fold) + dot(low, fold)


def table_back(dscores, buckets, n_buckets):
    n_heads, n, _ = dscores.shape
    rows, band = 64, 16
    dims = (n_heads * band, n_buckets * band)
    return pl.pallas_call(
        functools.partial(table_kernel, n_buckets=n_buckets),
        grid=(n // rows,),
        in_specs=[
            pl.BlockSpec((n_heads, rows, n), lambda r: (0, r, 0)),
            pl.BlockSpec((rows, n), lambda r: (r, 0)),
        ],
        out_specs=pl.BlockSpec((n_heads, n_buckets), lambda r: (0, 0)),
        out_shape=shape((n_heads, n_buckets), F32),
        scratch_shapes=[pltpu.VMEM(dims, F32)],
        compiler_params=params(),
        cost_estimate=cost(2 * dims[0] * dims[1] * n * n // band, 2 * n_heads * n * n),
        name="table_back",
    )(dscores, buckets)


def add(left, right):
    return (left.astype(F32) + right.astype(F32)).astype(LOW)


def tie(*values):
    return lax.optimization_barrier(values)


class Ring:
    def __init__(self, n_grp, n_loc):
        size = n_grp * n_loc
        bits = size.bit_length() - 1
        low = n_loc.bit_length() - 1
        self.size = size
        ys, xs = list(range(1, low)), list(range(low, bits - 2))
        first, second = (ys + xs, xs + ys) if len(ys) == len(xs) else (ys + xs, ys + xs)
        self.plane = list(zip(first, second))
        self.near, self.far = (bits - 2, bits - 2), (bits - 1, bits - 1)
        self.core = (0, 0)

    def swap(self, value, shifts):
        pairs = [(i, i ^ (1 << shifts[i & 1])) for i in range(self.size)]
        return lax.ppermute(value, AXES, pairs)

    def side(self, me, shifts):
        shift = jnp.where(me & 1 == 0, shifts[0], shifts[1])
        return (me >> shift) & 1

    def cut(self, value, me, shifts):
        halves = value.reshape(2, value.shape[0] // 2, value.shape[1])
        side = self.side(me, shifts)
        return [lax.dynamic_index_in_dim(halves, at, 0, keepdims=False) for at in (1 - side, side)]

    def join(self, value, got, me, shifts):
        side = self.side(me, shifts)
        low = jnp.where(side == 0, value, got)
        high = jnp.where(side == 0, got, value)
        return jnp.concatenate([low, high], axis=0)

    def where(self, me):
        sides = [self.side(me, self.plane[0]), self.side(me ^ 1, self.plane[0])]
        return jnp.stack([me & 1] + sides)


def unpack_kernel(where_ref, own_a, core_a, own_b, core_b, *refs, late):
    mine = pl.program_id(0) == where_ref[0]
    rows_a = jnp.where(mine, own_a[...], core_a[...]).astype(F32)
    rows_b = jnp.where(mine, own_b[...], core_b[...]).astype(F32)
    outs = refs[-5:]
    width = outs[3].shape[1]
    outs[3][...] = rows_a[:, :width]
    span = 128
    half = rows_b.shape[1] // 3
    routed = rows_a[:, width + 3 * half :].T[: outs[4].shape[0], :]
    size = routed.shape[1]
    side = jnp.where(mine, where_ref[1], where_ref[2])
    quarter = 2 * pl.program_id(0) + (1 - side if late else side)

    @pl.when(pl.program_id(0) == 0)
    def _():
        outs[4][...] = refs[0][...] if late else jnp.zeros_like(outs[4])

    for at in range(4):

        @pl.when(quarter == at)
        def _():
            outs[4][:, at * size : (at + 1) * size] = routed

    for i in range(3):
        for p in range(half // span):
            at = (3 * p + i) * span
            here = slice(p * span, (p + 1) * span)
            outs[i][:, here] = rows_a[:, width + at : width + at + span]
            there = slice(half + p * span, half + (p + 1) * span)
            outs[i][:, there] = rows_b[:, at : at + span]


def unpack(where, own_a, core_a, own_b, core_b, late, earlier, width, n_experts):
    rows = own_a.shape[0]
    earlier = tuple(earlier)

    def place(c, where_ref):
        side = jnp.where(c == where_ref[0], where_ref[1], where_ref[2])
        return 2 * c + (1 - side if late else side), 0

    whole = lambda *dims: pl.BlockSpec(dims, lambda c, where_ref: (0, 0))
    inputs = (own_a, core_a, own_b, core_b) + earlier[4:]
    return pl.pallas_call(
        functools.partial(unpack_kernel, late=late),
        grid_spec=pltpu.PrefetchScalarGridSpec(
            num_scalar_prefetch=1,
            grid=(2,),
            in_specs=[whole(*value.shape) for value in inputs]
            + [pl.BlockSpec(memory_space=pl.ANY)] * len(earlier[:4]),
            out_specs=[pl.BlockSpec((rows, width), place)] * 4 + [whole(n_experts, width)],
        ),
        out_shape=[shape((width, width), F32)] * 4 + [shape((n_experts, width), F32)],
        input_output_aliases={6 + i: i for i in range(len(earlier[:4]))},
        compiler_params=pltpu.CompilerParams(vmem_limit_bytes=24 * 1024 * 1024),
        cost_estimate=cost(rows * width, 24 * rows * width),
        name="unpack",
    )(where, *inputs, *earlier[:4])


def tokens_kernel(grads_ref, wt_ref, tok_ref, gain_ref, dmid_ref, out_ref, gain_out, sum_s):
    step = pl.program_id(0)
    part = dot(grads_ref[...], wt_ref[...])

    @pl.when(step == 0)
    def _():
        sum_s[...] = part

    @pl.when(step > 0)
    def _():
        sum_s[...] += part

    @pl.when(step == pl.num_programs(0) - 1)
    def _():
        dnormed = sum_s[...]
        inputs = tok_ref[...].astype(F32)
        inv = norm_scale(inputs)
        scaled = dnormed * gain_ref[...]
        inner = jnp.mean(scaled * inputs, axis=1, keepdims=True)
        out_ref[...] = (
            dmid_ref[...] + inv * scaled - inputs * (inv * inv * inv) * inner
        ).astype(LOW)
        gain_out[...] = jnp.broadcast_to(
            jnp.sum(dnormed * inputs * inv, axis=0, keepdims=True), gain_out.shape
        )


def tokens_back(grads, weights_t, tokens, gain, dmid):
    n, width = tokens.shape
    steps = 3
    block = grads.shape[1] // steps
    whole = lambda *dims: pl.BlockSpec(dims, lambda p: (0,) * len(dims))
    return pl.pallas_call(
        tokens_kernel,
        grid=(steps,),
        in_specs=[
            pl.BlockSpec((n, block), lambda p: (0, p)),
            pl.BlockSpec((block, width), lambda p: (p, 0)),
            whole(n, width),
            whole(1, width),
            whole(n, width),
        ],
        out_specs=[whole(n, width), whole(8, width)],
        out_shape=[shape((n, width), LOW), shape((8, width), F32)],
        scratch_shapes=[pltpu.VMEM((n, width), F32)],
        compiler_params=params(),
        cost_estimate=cost(6 * n * width * width, 6 * width * width + 14 * n * width),
        name="tokens_back",
    )(grads, weights_t, tokens, gain.reshape(1, width), dmid)


def leave_kernel(res_ref, col_ref, mid_ref, out_ref):
    n = mid_ref.shape[0]
    slots = res_ref.shape[0]
    place = lax.broadcasted_iota(jnp.int32, (n, slots), 1) == col_ref[:, 64:65]
    out_ref[...] = (mid_ref[...] + dot(place.astype(F32).astype(LOW), res_ref[...])).astype(LOW)


def leave(res_rows, col, middle):
    n, width = middle.shape
    return pl.pallas_call(
        leave_kernel,
        out_shape=shape((n, width), LOW),
        compiler_params=params(),
        cost_estimate=cost(2 * n * width * res_rows.shape[0], 10 * n * width),
        name="leave",
    )(res_rows, col, middle)


def exchange(rows):
    return lax.all_to_all(rows, AXES, split_axis=0, concat_axis=0, tiled=True)


def sum_small(parts, n_dev):
    flat = jnp.concatenate([part.reshape(-1) for part in parts])
    size = flat.shape[0]
    lines = -(-size // 1024) * 8
    block = jnp.pad(flat, (0, lines * 128 - size)).reshape(1, lines, 128)
    sent = jnp.broadcast_to(block, (n_dev, lines, 128))
    total = jnp.sum(exchange(sent), axis=0).reshape(-1)
    found, start = [], 0
    for part in parts:
        found.append(total[start : start + part.size].reshape(part.shape))
        start += part.size
    return found


def body(
    n_grp,
    n_loc,
    tokens,
    cotangent,
    w_query,
    w_key,
    w_value,
    w_output,
    attn_gain,
    bias_table,
    moe_gain,
    router_weight,
    router_bias,
    expert_in,
    expert_out,
    expert_ids,
    bucket_ids,
):
    n_rows, width = tokens.shape
    n_buckets, n_heads = bias_table.shape
    n_experts = router_weight.shape[1]
    most = max(2, 2 * n_rows // n_experts)
    slots = n_experts * most
    keep = 5 * n_rows // 4
    me = (lax.axis_index("grp") * lax.axis_size("loc") + lax.axis_index("loc")).reshape(1)

    dy_out, row, col = dispatch(expert_ids, cotangent, slots, most)
    dy_out, attn_gain, moe_gain, bias_table = tie(dy_out, attn_gain, moe_gain, bias_table)
    dy_rows = exchange(dy_out)

    table = jnp.pad(bias_table.T, ((0, 0), (0, 128 - n_buckets))).reshape(n_heads // 2, 2, 128)
    query, keys, values, weights, attended_t, normed_t, middle, x_low, x_high, weights_t = attend(
        tokens, attn_gain, table, bucket_ids, w_query, w_key, w_value, w_output, moe_gain, row,
        slots, n_heads,
    )
    dy_rows, x_low = tie(dy_rows, x_low)
    x_low = exchange(x_low)
    arrived = arrive(dy_rows, most, keep)
    x_low, x_high, *arrived = tie(x_low, x_high, *arrived)
    dy_low, dy_high, kept_low, kept_high = arrived
    x_high = exchange(x_high)
    model = (router_weight, router_bias, expert_in, expert_out)
    dn_low, res_low, *earlier = expert(me, x_low, dy_low, kept_low, *model)
    dn_low, x_high = tie(dn_low, x_high)
    dn_low = exchange(dn_low)
    from_high = expert(me, x_high, dy_high, kept_high, *model, earlier)
    dn_low, *from_high = tie(dn_low, *from_high)
    dn_high, res_high, hidden, dpre, dres, dlogits = from_high
    dn_high = exchange(dn_high)
    res_sent = jnp.concatenate(
        [value.reshape(n_experts, most // 2, width) for value in (res_low, res_high)], axis=1
    ).reshape(slots, width)
    grad_expert_in, grad_expert_out, routed, bias_rows = weights_back(
        x_low, x_high, hidden, dpre, dres, dlogits
    )
    grad_router_bias = bias_rows[0]
    ring = Ring(n_grp, n_loc)
    rank = me[0]
    where = ring.where(rank)
    dn_high, res_sent, grad_expert_in, grad_expert_out, routed, grad_router_bias, where = tie(
        dn_high, res_sent, grad_expert_in, grad_expert_out, routed, grad_router_bias, where
    )
    res_rows = exchange(res_sent)
    dmid, sent_a, kept_a, moe_gain_rows, grads, dscores, sent_b, kept_b = back(
        me & 1, dn_low, dn_high, col, middle, cotangent, moe_gain, w_output, attended_t, routed, query,
        keys, values, weights, normed_t, n_heads // 4,
    )

    def step(kept, got, shifts):
        sent = add(ring.cut(kept, rank, shifts)[0], ring.cut(got, rank, shifts)[0])
        sent, kept, got = tie(sent, kept, got)
        return sent, add(ring.cut(kept, rank, shifts)[1], ring.cut(got, rank, shifts)[1])

    got_a = ring.swap(sent_a, ring.core)
    sent_a, kept_a = step(kept_a, got_a, ring.plane[0])
    got_b = ring.swap(sent_b, ring.core)
    got_b, sent_a = tie(got_b, sent_a)
    got_a = ring.swap(sent_a, ring.plane[0])
    sent_b, kept_b = step(kept_b, got_b, ring.plane[0])
    sent_b, grads, dscores = tie(sent_b, grads, dscores)
    got_b = ring.swap(sent_b, ring.plane[0])
    grad_tokens, attn_gain_rows = tokens_back(grads, weights_t, tokens, attn_gain, dmid)
    grad_table = table_back(dscores, bucket_ids, n_buckets)
    got_a, got_b, grad_tokens, attn_gain_rows, grad_table, res_rows = tie(
        got_a, got_b, grad_tokens, attn_gain_rows, grad_table, res_rows
    )
    for shifts in ring.plane[1:] + [ring.near]:
        sent_a, kept_a = step(kept_a, got_a, shifts)
        sent_b, kept_b = step(kept_b, got_b, shifts)
        got_a, got_b = ring.swap(sent_a, shifts), ring.swap(sent_b, shifts)
    value_a, value_b = add(kept_a, got_a), add(kept_b, got_b)
    value_a, value_b, grad_table, res_rows = tie(value_a, value_b, grad_table, res_rows)
    got_a, got_b = ring.swap(value_a, ring.far), ring.swap(value_b, ring.far)
    smalls = sum_small(
        (attn_gain_rows[0], grad_table, moe_gain_rows[0], grad_router_bias), n_grp * n_loc
    )
    layer_out = leave(res_rows, col, middle)
    got_a, got_b, layer_out = tie(got_a, got_b, layer_out)
    value_a, value_b = add(value_a, got_a), add(value_b, got_b)
    for shifts in reversed(ring.plane[1:] + [ring.near]):
        got_a, got_b = ring.swap(value_a, shifts), ring.swap(value_b, shifts)
        value_a = ring.join(value_a, got_a, rank, shifts)
        value_b = ring.join(value_b, got_b, rank, shifts)
    value_a, value_b, *smalls = tie(value_a, value_b, *smalls)
    near_a, near_b = ring.swap(value_a, ring.plane[0]), ring.swap(value_b, ring.plane[0])
    core_a, core_b = ring.swap(value_a, ring.core), ring.swap(value_b, ring.core)
    outs = unpack(where, value_a, core_a, value_b, core_b, False, (), width, n_experts)
    near_a, near_b, *outs = tie(near_a, near_b, *outs)
    far_a, far_b = ring.swap(near_a, ring.core), ring.swap(near_b, ring.core)
    outs = unpack(where, near_a, far_a, near_b, far_b, True, outs, width, n_experts)
    grad_query, grad_key, grad_value, grad_output, grad_router = outs
    grad_attn_gain, grad_table, grad_moe_gain, grad_router_bias = smalls
    return (
        layer_out,
        grad_tokens,
        grad_query,
        grad_key,
        grad_value,
        grad_output,
        grad_attn_gain,
        grad_table.T,
        grad_moe_gain,
        grad_router.T,
        grad_router_bias,
        grad_expert_in[None],
        grad_expert_out[None],
    )


def solution(mesh):
    rows, flat = P(AXES, None), P(AXES, None, None)
    return jax.shard_map(
        functools.partial(body, mesh.shape["grp"], mesh.shape["loc"]),
        mesh=mesh,
        in_specs=(
            rows, rows, P(), P(), P(), P(), P(), P(), P(), P(), P(), flat, flat, rows, P(),
        ),
        out_specs=(
            rows, rows, P(), P(), P(), P(), P(), P(), P(), P(), P(), flat, flat,
        ),
        check_vma=False,
    )
```

```python
import functools

import jax
import jax.numpy as jnp
from jax import lax
from jax.experimental import pallas as pl
from jax.experimental.pallas import tpu as pltpu
from jax.sharding import PartitionSpec as P

AXES = ("grp", "loc")
LOW = jnp.bfloat16
F32 = jnp.float32
NN = (((1,), (0,)), ((), ()))
NT = (((1,), (1,)), ((), ()))
TN = (((0,), (0,)), ((), ()))
VMEM_BYTES = 56 * 1024 * 1024
EMPTY = 2.0**20


def dot(left, right, dims=NN):
    return lax.dot_general(left, right, dims, preferred_element_type=F32)


def split(values):
    high = values.astype(LOW)
    rest = values - high.astype(F32)
    middle = rest.astype(LOW)
    return high, middle, (rest - middle.astype(F32)).astype(LOW)


def params():
    return pltpu.CompilerParams(vmem_limit_bytes=VMEM_BYTES)


def cost(flops, nbytes, trans=0):
    return pl.CostEstimate(flops=int(flops), bytes_accessed=int(nbytes), transcendentals=int(trans))


def shape(dims, dtype):
    return jax.ShapeDtypeStruct(dims, dtype)


def norm_scale(values):
    return lax.rsqrt(jnp.mean(values * values, axis=-1, keepdims=True) + 1e-06)


def dispatch_kernel(ids_ref, dy_ref, out_ref, row_ref, col_ref, *, most):
    n = ids_ref.shape[1]
    slots = out_ref.shape[0]
    sub = lax.broadcasted_iota(jnp.int32, (n, n), 0)
    lane = lax.broadcasted_iota(jnp.int32, (n, n), 1)
    ids_row = ids_ref[...]
    ids_col = jnp.sum(jnp.where(sub == lane, ids_row, 0), axis=1, keepdims=True)
    same = ids_col == ids_row
    rank_row = jnp.sum(jnp.where(same & (sub < lane), 1, 0), axis=0, keepdims=True)
    rank_col = jnp.sum(jnp.where(same & (lane < sub), 1, 0), axis=1, keepdims=True)
    half = most // 2

    def halves(ids, rank):
        low = jnp.where(rank < half, ids * half + rank, -1)
        return low, jnp.where(rank < half, -1, ids * half + rank - half)

    low, high = halves(ids_row, rank_row)
    upper = lax.broadcasted_iota(jnp.int32, row_ref.shape, 0) < 4
    row_ref[...] = jnp.where(upper, low, high)
    low, high = halves(ids_col, rank_col)
    spot = lax.broadcasted_iota(jnp.int32, col_ref.shape, 1)
    full = ids_col * most + rank_col
    col_ref[...] = jnp.where(spot < 32, low, jnp.where(spot < 64, high, full))
    place = lax.broadcasted_iota(jnp.int32, (slots, n), 0) == ids_row * most + rank_row
    hot = place.astype(F32)
    filled = jnp.sum(hot, axis=1, keepdims=True)
    rows = dot(hot.astype(LOW), dy_ref[...])
    out_ref[...] = jnp.where(filled > 0.0, rows, EMPTY).astype(LOW)


def dispatch(ids, dy, slots, most):
    n, width = dy.shape
    return pl.pallas_call(
        functools.partial(dispatch_kernel, most=most),
        out_shape=(
            shape((slots, width), LOW),
            shape((8, n), jnp.int32),
            shape((n, 128), jnp.int32),
        ),
        compiler_params=params(),
        cost_estimate=cost(2 * slots * n * width, 4 * slots * width),
        name="dispatch",
    )(ids.reshape(1, n), dy)


def attend_kernel(
    tok_ref,
    gain_ref,
    tab_ref,
    bucket_ref,
    wq_ref,
    wk_ref,
    wv_ref,
    wo_ref,
    moe_gain_ref,
    row_ref,
    q_ref,
    k_ref,
    v_ref,
    w_ref,
    att_t_ref,
    normed_t_ref,
    mid_ref,
    low_ref,
    high_ref,
    wt_ref,
    att_s,
    normed_s,
    *,
    scaling,
):
    step = pl.program_id(0)
    pairs = pl.num_programs(0)
    n = tok_ref.shape[0]

    @pl.when(step == 0)
    def _():
        inputs = tok_ref[...].astype(F32)
        normed_one = (inputs * norm_scale(inputs) * gain_ref[...]).astype(LOW)
        normed_s[...] = normed_one
        normed_t_ref[...] = normed_one.T

    normed = normed_s[...]
    query = dot(normed, wq_ref[...]).astype(LOW)
    keys = dot(normed, wk_ref[...]).astype(LOW)
    values = dot(normed, wv_ref[...]).astype(LOW)
    q_ref[...] = query
    k_ref[...] = keys
    v_ref[...] = values
    span = query.shape[1]
    for i, ref in enumerate((wq_ref, wk_ref, wv_ref)):
        wt_ref[i * span : (i + 1) * span, :] = ref[...].T
    low_half = lax.broadcasted_iota(jnp.int32, query.shape, 1) < query.shape[1] // 2
    zero = jnp.zeros_like(query)
    total = jnp.zeros((n, query.shape[1]), F32)
    for h in range(2):
        mine = low_half if h == 0 else ~low_half
        scores = dot(jnp.where(mine, query, zero), keys, NT) * scaling
        table = jnp.broadcast_to(tab_ref[step, pl.ds(h, 1), :], (n, 128))
        bias = [
            jnp.take_along_axis(
                table, bucket_ref[:, c * 128 : (c + 1) * 128], axis=1, mode="promise_in_bounds"
            )
            for c in range(n // 128)
        ]
        scores = scores + jnp.concatenate(bias, axis=1)
        top = jnp.max(scores, axis=1, keepdims=True)
        grown = jnp.exp(scores - top)
        weights = (grown * (1.0 / jnp.sum(grown, axis=1, keepdims=True))).astype(LOW)
        w_ref[h] = weights
        total = total + dot(weights, jnp.where(mine, values, zero))
    att_s[step] = total.astype(LOW)

    @pl.when(step == pairs - 1)
    def _():
        attended = jnp.concatenate([att_s[i] for i in range(att_s.shape[0])], axis=1)
        att_t_ref[...] = attended.T
        middle = tok_ref[...].astype(F32) + dot(attended, wo_ref[...])
        mid_ref[...] = middle
        normed_two = (middle * norm_scale(middle) * moe_gain_ref[...]).astype(LOW)
        for ref, row in ((low_ref, 0), (high_ref, 4)):
            slot = lax.broadcasted_iota(jnp.int32, (ref.shape[0], n), 0)
            place = slot == row_ref[row : row + 1, :]
            ref[...] = dot(place.astype(F32).astype(LOW), normed_two).astype(LOW)


def attend(tokens, gain, table, buckets, wq, wk, wv, wo, moe_gain, row, slots, n_heads):
    n, width = tokens.shape
    pairs = n_heads // 2
    span = width // pairs
    whole = lambda *dims: pl.BlockSpec(dims, lambda p: (0,) * len(dims))
    cols = lambda rows: pl.BlockSpec((rows, span), lambda p: (0, p))
    return pl.pallas_call(
        functools.partial(attend_kernel, scaling=(width // n_heads) ** -0.5),
        grid=(pairs,),
        in_specs=[
            whole(n, width),
            whole(1, width),
            whole(*table.shape),
            whole(n, n),
            cols(width),
            cols(width),
            cols(width),
            whole(width, width),
            whole(1, width),
            whole(8, n),
        ],
        out_specs=[
            cols(n),
            cols(n),
            cols(n),
            pl.BlockSpec((2, n, n), lambda p: (p, 0, 0)),
            whole(width, n),
            whole(width, n),
            whole(n, width),
            whole(slots // 2, width),
            whole(slots // 2, width),
            pl.BlockSpec((3 * span, width), lambda p: (p, 0)),
        ],
        out_shape=[
            shape((n, width), LOW),
            shape((n, width), LOW),
            shape((n, width), LOW),
            shape((n_heads, n, n), LOW),
            shape((width, n), LOW),
            shape((width, n), LOW),
            shape((n, width), F32),
            shape((slots // 2, width), LOW),
            shape((slots // 2, width), LOW),
            shape((3 * width, width), LOW),
        ],
        scratch_shapes=[pltpu.VMEM((pairs, n, span), LOW), pltpu.VMEM((n, width), LOW)],
        compiler_params=params(),
        cost_estimate=cost(
            8 * n * width * width + 4 * n_heads * n * n * span + 2 * slots * n * width,
            2 * n_heads * n * n + 24 * n * width,
            n_heads * n * n,
        ),
        name="attend",
    )(
        tokens,
        gain.reshape(1, width),
        table,
        buckets,
        wq,
        wk,
        wv,
        wo,
        moe_gain.reshape(1, width),
        row,
    )


def arrive_kernel(dy_ref, low_ref, high_ref, low_kept, high_kept, *, most, keep):
    slots = dy_ref.shape[0]
    half = most // 2
    edge = dy_ref[:, 0:128]
    valid = jnp.where(edge.astype(F32) < EMPTY * 0.5, 1.0, 0.0).astype(LOW)
    sub = lax.broadcasted_iota(jnp.int32, (slots, slots), 0)
    lane = lax.broadcasted_iota(jnp.int32, (slots, slots), 1)
    before = jnp.where(lane < sub, 1.0, 0.0).astype(LOW)
    first = jnp.where(lax.broadcasted_iota(jnp.int32, (8, 128), 1) == 0, 1.0, 0.0).astype(LOW)
    valid_row = dot(first, valid, NT)
    slot_row = dot(valid_row.astype(LOW), before, NT)
    kept = ((valid_row > 0.5) & (slot_row < keep - 0.5))[0:1, :]
    sub = lax.broadcasted_iota(jnp.int32, (slots // 2, slots), 0)
    lane = lax.broadcasted_iota(jnp.int32, (slots // 2, slots), 1)
    here = sub // half * most + sub % half
    for at, ref, kept_ref in ((0, low_ref, low_kept), (half, high_ref, high_kept)):
        place = jnp.where((lane == here + at) & kept, 1.0, 0.0)
        kept_ref[...] = jnp.broadcast_to(jnp.sum(place, axis=1, keepdims=True), kept_ref.shape)
        ref[...] = dot(place.astype(LOW), dy_ref[...]).astype(LOW)


def arrive(dy_rows, most, keep):
    slots, width = dy_rows.shape
    return pl.pallas_call(
        functools.partial(arrive_kernel, most=most, keep=keep),
        out_shape=(
            shape((slots // 2, width), LOW),
            shape((slots // 2, width), LOW),
            shape((slots // 2, 128), F32),
            shape((slots // 2, 128), F32),
        ),
        compiler_params=params(),
        cost_estimate=cost(2 * slots * slots * width, 4 * slots * width),
        name="arrive",
    )(dy_rows)


def expert_kernel(
    me_ref, x_ref, dyc_ref, kept_ref, router_ref, rbias_ref, win_ref, wout_ref, *refs, n_in
):
    dn_ref, res_ref, hid_ref, dpre_ref, dres_ref, dlog_ref, sum_s, drow_s, prob_s = refs[n_in:]
    step = pl.program_id(0)

    def gate_of(probs):
        mine = lax.broadcasted_iota(jnp.int32, probs.shape, 1) == me_ref[0]
        return mine, jnp.sum(jnp.where(mine, probs, 0.0), axis=1, keepdims=True)

    @pl.when(step == 0)
    def _():
        rows = x_ref[...]
        high, middle, low = split(router_ref[...])
        logits = dot(rows, high) + (dot(rows, middle) + dot(rows, low)) + rbias_ref[...]
        grown = jnp.exp(logits - jnp.max(logits, axis=1, keepdims=True))
        probs = grown / jnp.sum(grown, axis=1, keepdims=True)
        prob_s[...] = probs
        dres_ref[...] = (gate_of(probs)[1] * dyc_ref[...].astype(F32)).astype(LOW)
        sum_s[...] = jnp.zeros_like(sum_s)
        drow_s[...] = jnp.zeros_like(drow_s)

    rows = x_ref[...]
    win = win_ref[...]
    wout = wout_ref[...]
    pre = dot(rows, win)
    rate = 0.7978845608028654
    square = pre * pre
    tanh = jnp.tanh(rate * pre * (1.0 + 0.044715 * square))
    half = 0.5 * (1.0 + tanh)
    hidden = (pre * half).astype(LOW)
    slope = half + (0.5 * rate) * pre * (1.0 - tanh * tanh) * (1.0 + 3 * 0.044715 * square)
    dhid = dot(dres_ref[...], wout, NT)
    dpre = (dhid * slope).astype(LOW)
    hid_ref[...] = hidden
    dpre_ref[...] = dpre
    sum_s[...] += dot(hidden, wout)
    drow_s[...] += dot(dpre, win, NT)

    @pl.when(step == pl.num_programs(0) - 1)
    def _():
        result = sum_s[...].astype(LOW).astype(F32)
        dgate = jnp.sum(dyc_ref[...].astype(F32) * result, axis=1, keepdims=True)
        probs = prob_s[...]
        mine, gate = gate_of(probs)
        dlogits = probs * (jnp.where(mine, dgate, 0.0) - gate * dgate)
        dlog_ref[...] = dlogits
        high, middle, _ = split(router_ref[...])
        dhigh, dmiddle, _ = split(dlogits)
        side = dot(dhigh, high, NT) + (dot(dhigh, middle, NT) + dot(dmiddle, high, NT))
        dn_ref[...] = (drow_s[...] + side).astype(LOW)
        res_ref[...] = (kept_ref[:, 0:1] * gate * result).astype(LOW)


def expert(me, rows, dyc, kept, router, rbias, expert_in, expert_out, earlier=()):
    n, width = rows.shape
    n_exp = router.shape[1]
    ff = expert_in.shape[2]
    block = 768 if ff % 768 == 0 else ff
    at = 1 if earlier else 0
    whole = lambda *dims: pl.BlockSpec(dims, lambda f: (0,) * len(dims))
    return pl.pallas_call(
        functools.partial(expert_kernel, n_in=len(earlier)),
        grid=(ff // block,),
        in_specs=[
            pl.BlockSpec(memory_space=pltpu.SMEM),
            whole(n, width),
            whole(n, width),
            whole(n, 128),
            whole(width, n_exp),
            whole(1, n_exp),
            pl.BlockSpec((None, width, block), lambda f: (0, 0, f)),
            pl.BlockSpec((None, block, width), lambda f: (0, f, 0)),
        ]
        + [pl.BlockSpec(memory_space=pl.ANY)] * len(earlier),
        out_specs=[
            whole(n, width),
            whole(n, width),
            pl.BlockSpec((n, block), lambda f: (at, f)),
            pl.BlockSpec((n, block), lambda f: (at, f)),
            pl.BlockSpec((n, width), lambda f: (at, 0)),
            pl.BlockSpec((n, n_exp), lambda f: (at, 0)),
        ],
        out_shape=[
            shape((n, width), LOW),
            shape((n, width), LOW),
            shape((2 * n, ff), LOW),
            shape((2 * n, ff), LOW),
            shape((2 * n, width), LOW),
            shape((2 * n, n_exp), F32),
        ],
        scratch_shapes=[
            pltpu.VMEM((n, width), F32),
            pltpu.VMEM((n, width), F32),
            pltpu.VMEM((n, n_exp), F32),
        ],
        input_output_aliases={8 + i: 2 + i for i in range(len(earlier))},
        compiler_params=params(),
        cost_estimate=cost(8 * n * width * ff, 16 * width * ff, n * ff),
        name="expert",
    )(me, rows, dyc, kept, router, rbias.reshape(1, n_exp), expert_in, expert_out, *earlier)


def weights_kernel(
    low_ref, high_ref, hid_ref, dpre_ref, dres_ref, dlog_ref, in_ref, out_ref, routed_ref, bias_ref,
    x_s,
):
    @pl.when(pl.program_id(0) == 0)
    def _():
        n = low_ref.shape[0]
        x_s[:, :n] = low_ref[...].T
        x_s[:, n:] = high_ref[...].T
        dlogits = dlog_ref[...]
        rows = x_s[...]
        high, middle, low = split(dlogits)
        routed = dot(rows, high) + (dot(rows, middle) + dot(rows, low))
        routed_ref[...] = jnp.zeros_like(routed_ref)
        routed_ref[:, : routed.shape[1]] = routed
        bias_ref[...] = jnp.broadcast_to(jnp.sum(dlogits, axis=0, keepdims=True), bias_ref.shape)

    in_ref[...] = dot(x_s[...], dpre_ref[...])
    out_ref[...] = dot(hid_ref[...].T, dres_ref[...])


def weights_back(x_low, x_high, hidden, dpre, dres, dlogits):
    n, width = x_low.shape
    ff = hidden.shape[1]
    n_exp = dlogits.shape[1]
    tail = -(-n_exp // 128) * 128
    block = 512 if ff % 512 == 0 else ff
    whole = lambda *dims: pl.BlockSpec(dims, lambda f: (0,) * len(dims))
    cols = lambda rows: pl.BlockSpec((rows, block), lambda f: (0, f))
    return pl.pallas_call(
        weights_kernel,
        grid=(ff // block,),
        in_specs=[
            whole(n, width),
            whole(n, width),
            cols(2 * n),
            cols(2 * n),
            whole(2 * n, width),
            whole(2 * n, n_exp),
        ],
        out_specs=[
            cols(width),
            pl.BlockSpec((block, width), lambda f: (f, 0)),
            whole(width, tail),
            whole(8, n_exp),
        ],
        out_shape=[
            shape((width, ff), F32),
            shape((ff, width), F32),
            shape((width, tail), F32),
            shape((8, n_exp), F32),
        ],
        scratch_shapes=[pltpu.VMEM((width, 2 * n), LOW)],
        compiler_params=params(),
        cost_estimate=cost(8 * n * width * ff, 8 * width * ff),
        name="weights_back",
    )(x_low, x_high, hidden, dpre, dres, dlogits)


def back_kernel(
    core_ref,
    low_hbm,
    high_hbm,
    col_hbm,
    mid_hbm,
    dy_hbm,
    wo_hbm,
    attended_hbm,
    routed_hbm,
    normed_hbm,
    gain_ref,
    q_ref,
    k_ref,
    v_ref,
    w_ref,
    dmid_hbm,
    sent_hbm,
    kept_hbm,
    gain_out,
    grads_ref,
    ds_ref,
    sent_b,
    kept_b,
    datt_s,
    low_ref,
    high_ref,
    col_ref,
    mid_ref,
    dy_ref,
    wo_ref,
    attended_ref,
    routed_ref,
    normed_ref,
    dmid_ref,
    sent_a,
    kept_a,
    sems,
    *,
    scaling,
):
    step = pl.program_id(0)
    n, span = q_ref.shape
    width = mid_ref.shape[1]
    part = width // 2
    half = span // 2
    tail = routed_ref.shape[1]
    lead = sent_a.shape[1] - tail - width
    lead_pairs = lead // (3 * span)
    sides = [
        pl.ds(pl.multiple_of(core * part, 128), part) for core in (1 - core_ref[0], core_ref[0])
    ]
    ins = [
        (low_hbm, low_ref),
        (high_hbm, high_ref),
        (col_hbm, col_ref),
        (mid_hbm, mid_ref),
        (dy_hbm, dy_ref),
        (wo_hbm, wo_ref),
        (attended_hbm, attended_ref),
        (routed_hbm, routed_ref),
        (normed_hbm, normed_ref),
    ]
    outs = [(dmid_ref, dmid_hbm), (sent_a, sent_hbm), (kept_a, kept_hbm)]
    copies = [
        pltpu.make_async_copy(source, target, sems.at[at])
        for at, (source, target) in enumerate(ins + outs)
    ]
    from_low, from_high, from_col, from_mid, from_dy, from_wo, from_att, from_routed = copies[:8]
    from_normed, to_dmid, to_sent, to_kept = copies[8:]

    @pl.when(step == 0)
    def _():
        for copy in copies[:9]:
            copy.start()
        dnormed = jnp.zeros((n, width), F32)
        from_col.wait()
        for copy, ref, at in ((from_low, low_ref, 0), (from_high, high_ref, 32)):
            place = lax.broadcasted_iota(jnp.int32, (n, ref.shape[0]), 1) == col_ref[:, at : at + 1]
            copy.wait()
            dnormed = dnormed + dot(place.astype(F32).astype(LOW), ref[...])
        from_mid.wait()
        from_dy.wait()
        middle = mid_ref[...]
        inv = norm_scale(middle)
        scaled = dnormed * gain_ref[...]
        inner = jnp.mean(scaled * middle, axis=1, keepdims=True)
        dmid = dy_ref[...].astype(F32) + inv * scaled - middle * (inv * inv * inv) * inner
        dmid_ref[...] = dmid
        to_dmid.start()
        branch = dmid.astype(LOW)
        from_wo.wait()
        datt = dot(branch, wo_ref[...], NT).astype(LOW)
        for p in range(datt_s.shape[0]):
            datt_s[p] = datt[:, p * span : (p + 1) * span]
        gain_out[...] = jnp.broadcast_to(
            jnp.sum(dnormed * middle * inv, axis=0, keepdims=True), gain_out.shape
        )
        from_att.wait()
        from_routed.wait()
        for ref, rows in zip((sent_a, kept_a), sides):
            ref[:, :width] = dot(attended_ref[rows, :], branch).astype(LOW)
            ref[:, width + lead :] = routed_ref[rows, :].astype(LOW)
        from_normed.wait()

    @pl.when(step > 0)
    def _():
        pair = step - 1
        query, keys, values, grad = q_ref[...], k_ref[...], v_ref[...], datt_s[pair]
        low_half = lax.broadcasted_iota(jnp.int32, query.shape, 1) < half
        low_rows = lax.broadcasted_iota(jnp.int32, (span, n), 0) < half

        def stack(value):
            zero = jnp.zeros_like(value)
            return jnp.concatenate(
                [jnp.where(low_half, value, zero), jnp.where(low_half, zero, value)], axis=0
            )

        def spread(value):
            value = value.astype(F32).T.astype(LOW)
            zero = jnp.zeros_like(value)
            return jnp.concatenate(
                [jnp.where(low_rows, value, zero), jnp.where(low_rows, zero, value)], axis=1
            )

        weights_low = jnp.concatenate([w_ref[0], w_ref[1]], axis=0)
        weights = weights_low.astype(F32)
        both = weights * dot(stack(grad), values, NT)
        dscores = (both - weights * jnp.sum(both, axis=1, keepdims=True)).astype(LOW)
        ds_ref[0] = dscores[:n]
        ds_ref[1] = dscores[n:]
        dquery = dot(jnp.concatenate([dscores[:n], dscores[n:]], axis=1), stack(keys))
        dvalues = dot(spread(grad), weights_low)
        dkeys = dot(spread(query), dscores)
        grads = jnp.concatenate([dquery * scaling, dkeys.T * scaling, dvalues.T], axis=1)
        grads = grads.astype(LOW)
        grads_ref[...] = grads
        products = [dot(normed_ref[rows, :], grads).astype(LOW) for rows in sides]

        @pl.when(pair < lead_pairs)
        def _():
            at = pl.multiple_of(width + pair * (3 * span), 128)
            for ref, product in zip((sent_a, kept_a), products):
                ref[:, pl.ds(at, 3 * span)] = product

        @pl.when(pair >= lead_pairs)
        def _():
            for ref, product in zip((sent_b, kept_b), products):
                ref[...] = product

    @pl.when(step == lead_pairs)
    def _():
        to_sent.start()
        to_kept.start()

    @pl.when(step == pl.num_programs(0) - 1)
    def _():
        to_dmid.wait()
        to_sent.wait()
        to_kept.wait()


def back(
    core, low, high, col, middle, dy, moe_gain, wo, attended_t, routed, query, keys, values, weights,
    normed_t, lead_pairs,
):
    n_heads, n, _ = weights.shape
    width = low.shape[1]
    pairs = n_heads // 2
    span = width // pairs
    part = width // 2
    columns_a = width + 3 * span * lead_pairs + routed.shape[1]
    columns_b = 3 * span * (pairs - lead_pairs)
    pair = lambda p: jnp.maximum(p - 1, 0)
    late = lambda p: jnp.maximum(p - 1 - lead_pairs, 0)
    cols = lambda size: pl.BlockSpec((n, size), lambda p: (0, pair(p)))
    square = pl.BlockSpec((2, n, n), lambda p: (pair(p), 0, 0))
    piece = pl.BlockSpec((part, 3 * span), lambda p: (0, late(p)))
    anywhere = pl.BlockSpec(memory_space=pl.ANY)
    loaded = (low, high, col, middle, dy, wo, attended_t, routed, normed_t)
    return pl.pallas_call(
        functools.partial(back_kernel, scaling=(width // n_heads) ** -0.5),
        grid=(1 + pairs,),
        in_specs=[pl.BlockSpec(memory_space=pltpu.SMEM)]
        + [anywhere] * len(loaded)
        + [pl.BlockSpec((1, width), lambda p: (0, 0)), cols(span), cols(span), cols(span), square],
        out_specs=[anywhere] * 3
        + [pl.BlockSpec((8, width), lambda p: (0, 0)), cols(3 * span), square, piece, piece],
        out_shape=[
            shape((n, width), F32),
            shape((part, columns_a), LOW),
            shape((part, columns_a), LOW),
            shape((8, width), F32),
            shape((n, 3 * width), LOW),
            shape((n_heads, n, n), LOW),
            shape((part, columns_b), LOW),
            shape((part, columns_b), LOW),
        ],
        scratch_shapes=[pltpu.VMEM((pairs, n, span), LOW)]
        + [pltpu.VMEM(value.shape, value.dtype) for value in loaded]
        + [
            pltpu.VMEM((n, width), F32),
            pltpu.VMEM((part, columns_a), LOW),
            pltpu.VMEM((part, columns_a), LOW),
            pltpu.SemaphoreType.DMA((len(loaded) + 3,)),
        ],
        compiler_params=params(),
        cost_estimate=cost(1000, 1000),
        name="back",
    )(core, *loaded, moe_gain.reshape(1, width), query, keys, values, weights)


def table_kernel(ds_ref, bucket_ref, out_ref, sum_s, *, n_buckets):
    step = pl.program_id(0)
    n_heads, rows, n = ds_ref.shape
    band = 16

    @pl.when(step == 0)
    def _():
        sum_s[...] = jnp.zeros_like(sum_s)

    total = sum_s[...]
    for r in range(rows // band):
        span = slice(r * band, (r + 1) * band)
        grads = ds_ref[:, span, :].reshape(n_heads * band, n)
        buckets = bucket_ref[span, :]
        hot = jnp.concatenate(
            [jnp.where(buckets == b, 1.0, 0.0).astype(LOW) for b in range(n_buckets)], axis=0
        )
        total = total + dot(grads, hot, NT)
    sum_s[...] = total

    @pl.when(step == pl.num_programs(0) - 1)
    def _():
        left = lax.broadcasted_iota(jnp.int32, total.shape, 0) % band
        right = lax.broadcasted_iota(jnp.int32, total.shape, 1) % band
        own = jnp.where(left == right, total, 0.0)
        own = jnp.sum(own.reshape(n_heads, band, n_buckets * band), axis=1)
        bucket = lax.broadcasted_iota(jnp.int32, (n_buckets * band, n_buckets), 1)
        column = lax.broadcasted_iota(jnp.int32, (n_buckets * band, n_buckets), 0)
        fold = jnp.where(column // band == bucket, 1.0, 0.0).astype(LOW)
        high, middle, low = split(own)
        out_ref[...] = dot(high, fold) + dot(middle, fold) + dot(low, fold)


def table_back(dscores, buckets, n_buckets):
    n_heads, n, _ = dscores.shape
    rows, band = 64, 16
    dims = (n_heads * band, n_buckets * band)
    return pl.pallas_call(
        functools.partial(table_kernel, n_buckets=n_buckets),
        grid=(n // rows,),
        in_specs=[
            pl.BlockSpec((n_heads, rows, n), lambda r: (0, r, 0)),
            pl.BlockSpec((rows, n), lambda r: (r, 0)),
        ],
        out_specs=pl.BlockSpec((n_heads, n_buckets), lambda r: (0, 0)),
        out_shape=shape((n_heads, n_buckets), F32),
        scratch_shapes=[pltpu.VMEM(dims, F32)],
        compiler_params=params(),
        cost_estimate=cost(2 * dims[0] * dims[1] * n * n // band, 2 * n_heads * n * n),
        name="table_back",
    )(dscores, buckets)


def add(left, right):
    return (left.astype(F32) + right.astype(F32)).astype(LOW)


def tie(*values):
    return lax.optimization_barrier(values)


class Ring:
    def __init__(self, n_grp, n_loc):
        size = n_grp * n_loc
        bits = size.bit_length() - 1
        low = n_loc.bit_length() - 1
        self.size = size
        ys, xs = list(range(1, low)), list(range(low, bits - 2))
        first, second = (ys + xs, xs + ys) if len(ys) == len(xs) else (ys + xs, ys + xs)
        self.plane = list(zip(first, second))
        self.near, self.far = (bits - 2, bits - 2), (bits - 1, bits - 1)
        self.core = (0, 0)

    def swap(self, value, shifts):
        pairs = [(i, i ^ (1 << shifts[i & 1])) for i in range(self.size)]
        return lax.ppermute(value, AXES, pairs)

    def side(self, me, shifts):
        shift = jnp.where(me & 1 == 0, shifts[0], shifts[1])
        return (me >> shift) & 1

    def cut(self, value, me, shifts):
        halves = value.reshape(2, value.shape[0] // 2, value.shape[1])
        side = self.side(me, shifts)
        return [lax.dynamic_index_in_dim(halves, at, 0, keepdims=False) for at in (1 - side, side)]

    def join(self, value, got, me, shifts):
        side = self.side(me, shifts)
        low = jnp.where(side == 0, value, got)
        high = jnp.where(side == 0, got, value)
        return jnp.concatenate([low, high], axis=0)

    def where(self, me):
        sides = [self.side(me, self.plane[0]), self.side(me ^ 1, self.plane[0])]
        return jnp.stack([me & 1] + sides)


def unpack_kernel(where_ref, own_a, core_a, own_b, core_b, *refs, late):
    mine = pl.program_id(0) == where_ref[0]
    rows_a = jnp.where(mine, own_a[...], core_a[...]).astype(F32)
    rows_b = jnp.where(mine, own_b[...], core_b[...]).astype(F32)
    outs = refs[-5:]
    width = outs[3].shape[1]
    outs[3][...] = rows_a[:, :width]
    span = 128
    half = rows_b.shape[1] // 3
    routed = rows_a[:, width + 3 * half :].T[: outs[4].shape[0], :]
    size = routed.shape[1]
    side = jnp.where(mine, where_ref[1], where_ref[2])
    quarter = 2 * pl.program_id(0) + (1 - side if late else side)

    @pl.when(pl.program_id(0) == 0)
    def _():
        outs[4][...] = refs[0][...] if late else jnp.zeros_like(outs[4])

    for at in range(4):

        @pl.when(quarter == at)
        def _():
            outs[4][:, at * size : (at + 1) * size] = routed

    for i in range(3):
        for p in range(half // span):
            at = (3 * p + i) * span
            here = slice(p * span, (p + 1) * span)
            outs[i][:, here] = rows_a[:, width + at : width + at + span]
            there = slice(half + p * span, half + (p + 1) * span)
            outs[i][:, there] = rows_b[:, at : at + span]


def unpack(where, own_a, core_a, own_b, core_b, late, earlier, width, n_experts):
    rows = own_a.shape[0]
    earlier = tuple(earlier)

    def place(c, where_ref):
        side = jnp.where(c == where_ref[0], where_ref[1], where_ref[2])
        return 2 * c + (1 - side if late else side), 0

    whole = lambda *dims: pl.BlockSpec(dims, lambda c, where_ref: (0, 0))
    inputs = (own_a, core_a, own_b, core_b) + earlier[4:]
    return pl.pallas_call(
        functools.partial(unpack_kernel, late=late),
        grid_spec=pltpu.PrefetchScalarGridSpec(
            num_scalar_prefetch=1,
            grid=(2,),
            in_specs=[whole(*value.shape) for value in inputs]
            + [pl.BlockSpec(memory_space=pl.ANY)] * len(earlier[:4]),
            out_specs=[pl.BlockSpec((rows, width), place)] * 4 + [whole(n_experts, width)],
        ),
        out_shape=[shape((width, width), F32)] * 4 + [shape((n_experts, width), F32)],
        input_output_aliases={6 + i: i for i in range(len(earlier[:4]))},
        compiler_params=pltpu.CompilerParams(vmem_limit_bytes=24 * 1024 * 1024),
        cost_estimate=cost(rows * width, 24 * rows * width),
        name="unpack",
    )(where, *inputs, *earlier[:4])


def tokens_kernel(grads_ref, wt_ref, tok_ref, gain_ref, dmid_ref, out_ref, gain_out, sum_s):
    step = pl.program_id(0)
    part = dot(grads_ref[...], wt_ref[...])

    @pl.when(step == 0)
    def _():
        sum_s[...] = part

    @pl.when(step > 0)
    def _():
        sum_s[...] += part

    @pl.when(step == pl.num_programs(0) - 1)
    def _():
        dnormed = sum_s[...]
        inputs = tok_ref[...].astype(F32)
        inv = norm_scale(inputs)
        scaled = dnormed * gain_ref[...]
        inner = jnp.mean(scaled * inputs, axis=1, keepdims=True)
        out_ref[...] = (
            dmid_ref[...] + inv * scaled - inputs * (inv * inv * inv) * inner
        ).astype(LOW)
        gain_out[...] = jnp.broadcast_to(
            jnp.sum(dnormed * inputs * inv, axis=0, keepdims=True), gain_out.shape
        )


def tokens_back(grads, weights_t, tokens, gain, dmid):
    n, width = tokens.shape
    steps = 3
    block = grads.shape[1] // steps
    whole = lambda *dims: pl.BlockSpec(dims, lambda p: (0,) * len(dims))
    return pl.pallas_call(
        tokens_kernel,
        grid=(steps,),
        in_specs=[
            pl.BlockSpec((n, block), lambda p: (0, p)),
            pl.BlockSpec((block, width), lambda p: (p, 0)),
            whole(n, width),
            whole(1, width),
            whole(n, width),
        ],
        out_specs=[whole(n, width), whole(8, width)],
        out_shape=[shape((n, width), LOW), shape((8, width), F32)],
        scratch_shapes=[pltpu.VMEM((n, width), F32)],
        compiler_params=params(),
        cost_estimate=cost(6 * n * width * width, 6 * width * width + 14 * n * width),
        name="tokens_back",
    )(grads, weights_t, tokens, gain.reshape(1, width), dmid)


def leave_kernel(res_ref, col_ref, mid_ref, out_ref):
    n = mid_ref.shape[0]
    slots = res_ref.shape[0]
    place = lax.broadcasted_iota(jnp.int32, (n, slots), 1) == col_ref[:, 64:65]
    out_ref[...] = (mid_ref[...] + dot(place.astype(F32).astype(LOW), res_ref[...])).astype(LOW)


def leave(res_rows, col, middle):
    n, width = middle.shape
    return pl.pallas_call(
        leave_kernel,
        out_shape=shape((n, width), LOW),
        compiler_params=params(),
        cost_estimate=cost(2 * n * width * res_rows.shape[0], 10 * n * width),
        name="leave",
    )(res_rows, col, middle)


def exchange(rows):
    return lax.all_to_all(rows, AXES, split_axis=0, concat_axis=0, tiled=True)


def pack_small(parts):
    flat = jnp.concatenate([part.reshape(-1) for part in parts])
    lines = -(-flat.shape[0] // 1024) * 8
    return jnp.pad(flat, (0, lines * 128 - flat.shape[0])).reshape(lines, 128)


def unpack_small(packed, parts):
    flat, found, start = packed.reshape(-1), [], 0
    for part in parts:
        found.append(flat[start : start + part.size].reshape(part.shape))
        start += part.size
    return found


def body(
    n_grp,
    n_loc,
    tokens,
    cotangent,
    w_query,
    w_key,
    w_value,
    w_output,
    attn_gain,
    bias_table,
    moe_gain,
    router_weight,
    router_bias,
    expert_in,
    expert_out,
    expert_ids,
    bucket_ids,
):
    n_rows, width = tokens.shape
    n_buckets, n_heads = bias_table.shape
    n_experts = router_weight.shape[1]
    most = max(2, 2 * n_rows // n_experts)
    slots = n_experts * most
    keep = 5 * n_rows // 4
    me = (lax.axis_index("grp") * lax.axis_size("loc") + lax.axis_index("loc")).reshape(1)

    dy_out, row, col = dispatch(expert_ids, cotangent, slots, most)
    dy_out, attn_gain, moe_gain, bias_table = tie(dy_out, attn_gain, moe_gain, bias_table)
    dy_rows = exchange(dy_out)

    table = jnp.pad(bias_table.T, ((0, 0), (0, 128 - n_buckets))).reshape(n_heads // 2, 2, 128)
    query, keys, values, weights, attended_t, normed_t, middle, x_low, x_high, weights_t = attend(
        tokens, attn_gain, table, bucket_ids, w_query, w_key, w_value, w_output, moe_gain, row,
        slots, n_heads,
    )
    dy_rows, x_low = tie(dy_rows, x_low)
    x_low = exchange(x_low)
    arrived = arrive(dy_rows, most, keep)
    x_low, x_high, *arrived = tie(x_low, x_high, *arrived)
    dy_low, dy_high, kept_low, kept_high = arrived
    x_high = exchange(x_high)
    model = (router_weight, router_bias, expert_in, expert_out)
    dn_low, res_low, *earlier = expert(me, x_low, dy_low, kept_low, *model)
    dn_low, x_high = tie(dn_low, x_high)
    dn_low = exchange(dn_low)
    from_high = expert(me, x_high, dy_high, kept_high, *model, earlier)
    dn_low, *from_high = tie(dn_low, *from_high)
    dn_high, res_high, hidden, dpre, dres, dlogits = from_high
    dn_high = exchange(dn_high)
    res_sent = jnp.concatenate(
        [value.reshape(n_experts, most // 2, width) for value in (res_low, res_high)], axis=1
    ).reshape(slots, width)
    grad_expert_in, grad_expert_out, routed, bias_rows = weights_back(
        x_low, x_high, hidden, dpre, dres, dlogits
    )
    grad_router_bias = bias_rows[0]
    ring = Ring(n_grp, n_loc)
    rank = me[0]
    where = ring.where(rank)
    dn_high, res_sent, grad_expert_in, grad_expert_out, routed, grad_router_bias, where = tie(
        dn_high, res_sent, grad_expert_in, grad_expert_out, routed, grad_router_bias, where
    )
    res_rows = exchange(res_sent)
    dmid, sent_a, kept_a, moe_gain_rows, grads, dscores, sent_b, kept_b = back(
        me & 1, dn_low, dn_high, col, middle, cotangent, moe_gain, w_output, attended_t, routed, query,
        keys, values, weights, normed_t, n_heads // 4,
    )

    def step(kept, got, shifts):
        sent = add(ring.cut(kept, rank, shifts)[0], ring.cut(got, rank, shifts)[0])
        sent, kept, got = tie(sent, kept, got)
        return sent, add(ring.cut(kept, rank, shifts)[1], ring.cut(got, rank, shifts)[1])

    got_a = ring.swap(sent_a, ring.core)
    sent_a, kept_a = step(kept_a, got_a, ring.plane[0])
    got_b = ring.swap(sent_b, ring.core)
    got_b, sent_a = tie(got_b, sent_a)
    got_a = ring.swap(sent_a, ring.plane[0])
    sent_b, kept_b = step(kept_b, got_b, ring.plane[0])
    sent_b, dscores = tie(sent_b, dscores)
    got_b = ring.swap(sent_b, ring.plane[0])
    grad_table = table_back(dscores, bucket_ids, n_buckets)
    grad_table, res_rows = tie(grad_table, res_rows)
    layer_out = leave(res_rows, col, middle)
    got_a, got_b, grad_table, layer_out = tie(got_a, got_b, grad_table, layer_out)
    for shifts in ring.plane[1:] + [ring.near]:
        sent_a, kept_a = step(kept_a, got_a, shifts)
        sent_b, kept_b = step(kept_b, got_b, shifts)
        got_a, got_b = ring.swap(sent_a, shifts), ring.swap(sent_b, shifts)
    value_a, value_b = add(kept_a, got_a), add(kept_b, got_b)
    value_a, value_b, grads = tie(value_a, value_b, grads)
    got_a, got_b = ring.swap(value_a, ring.far), ring.swap(value_b, ring.far)
    grad_tokens, attn_gain_rows = tokens_back(grads, weights_t, tokens, attn_gain, dmid)
    got_a, got_b, grad_tokens, attn_gain_rows = tie(got_a, got_b, grad_tokens, attn_gain_rows)
    small_parts = (attn_gain_rows[0], grad_table, moe_gain_rows[0], grad_router_bias)
    small = pack_small(small_parts)

    def swaps(value, todo):
        for shifts in todo:
            value = value + ring.swap(value, shifts)
        return value

    value_a, value_b = add(value_a, got_a), add(value_b, got_b)
    turn = list(reversed(ring.plane[1:] + [ring.near]))
    for place, shifts in enumerate(turn):
        got_a, got_b = ring.swap(value_a, shifts), ring.swap(value_b, shifts)
        if place == 0:
            small = swaps(small, ring.plane)
        if place == len(turn) - 1:
            small = swaps(small, [ring.near, ring.far])
        got_a, small = tie(got_a, small)
        value_a = ring.join(value_a, got_a, rank, shifts)
        value_b = ring.join(value_b, got_b, rank, shifts)
    small = swaps(small, [ring.core])
    smalls = unpack_small(small, small_parts)
    near_a, near_b = ring.swap(value_a, ring.plane[0]), ring.swap(value_b, ring.plane[0])
    core_a, core_b = ring.swap(value_a, ring.core), ring.swap(value_b, ring.core)
    outs = unpack(where, value_a, core_a, value_b, core_b, False, (), width, n_experts)
    near_a, near_b, *outs = tie(near_a, near_b, *outs)
    far_a, far_b = ring.swap(near_a, ring.core), ring.swap(near_b, ring.core)
    outs = unpack(where, near_a, far_a, near_b, far_b, True, outs, width, n_experts)
    grad_query, grad_key, grad_value, grad_output, grad_router = outs
    grad_attn_gain, grad_table, grad_moe_gain, grad_router_bias = smalls
    return (
        layer_out,
        grad_tokens,
        grad_query,
        grad_key,
        grad_value,
        grad_output,
        grad_attn_gain,
        grad_table.T,
        grad_moe_gain,
        grad_router.T,
        grad_router_bias,
        grad_expert_in[None],
        grad_expert_out[None],
    )


def solution(mesh):
    rows, flat = P(AXES, None), P(AXES, None, None)
    return jax.shard_map(
        functools.partial(body, mesh.shape["grp"], mesh.shape["loc"]),
        mesh=mesh,
        in_specs=(
            rows, rows, P(), P(), P(), P(), P(), P(), P(), P(), P(), flat, flat, rows, P(),
        ),
        out_specs=(
            rows, rows, P(), P(), P(), P(), P(), P(), P(), P(), P(), flat, flat,
        ),
        check_vma=False,
    )
```
